32 devices in a mesh: seq: 8 (over z, x), head: 4 (over y, core).
Axes of the slice: x: 2, y: 2, z: 4, core: 2. Of those that a mesh axis runs over, the one named last changes fastest.
Arguments:
- queries: bfloat16 [8192, 4096], P('seq', 'head'), may hold values from -6 to 6
- key_vectors: bfloat16 [8192, 4096], P('seq', 'head'), may hold values from -6 to 6
- value_vectors: bfloat16 [8192, 4096], P('seq', 'head'), may hold values from -6 to 6
- gate_input: bfloat16 [8192, 4096], P('seq', 'head'), may hold values from -6 to 6
- log_decay: float32 [8192, 32], P('seq', 'head'), may hold values from -1.5 to 0, as said below
- out_weight: bfloat16 [4096, 4096], P('head'), may hold values from -0.09375 to 0.09375
Outputs:
- projected: bfloat16 [8192, 4096], P(('seq', 'head'))
The draws below stay inside these ranges and needn't reach their ends.
Inputs may be any that keep to these rules, and one draw needn't show every extreme that they name: `log_decay`: every entry is negative.
All inputs are finite; a program needn't handle non-finite values.
Results may differ from the reference program's by a relative error of at most 0.0054.
Values sent between devices are 32-bit elements; how exact they have to be, the bound alone decides.
No kernel may reach another device: no remote copies, remote signals or barrier semaphores. Data moves between devices by JAX's collectives and lax.ppermute only.
A program may use at most 128 MiB of HBM per device.

```python
import math
import jax
import jax.numpy as jnp
from jax import lax

D = 4096
HEAD_COUNT = 32
HEAD_DIM = 128
BLOCK_LEN = 256
TOK_DEV = 1024
SEQUENCE_LENGTH = 8192


def draw_log_decay(key, part):
    every_key = jax.random.split(key, 6)
    fast_share = 0.5
    fast = jax.random.uniform(every_key[0], (HEAD_COUNT,)) < fast_share
    fast_rate = jax.random.uniform(every_key[1], (HEAD_COUNT,), jnp.float32, 1.0 / 50.0, 1.0 / 30.0)
    slow_rate = 0.5 / SEQUENCE_LENGTH
    base = jnp.where(fast, fast_rate, slow_rate)
    block_scale = jnp.exp(jax.random.uniform(every_key[2], (SEQUENCE_LENGTH // TOK_DEV, 1, HEAD_COUNT), jnp.float32, math.log(0.6), math.log(1.4)))
    block_scale = jnp.broadcast_to(block_scale, (SEQUENCE_LENGTH // TOK_DEV, TOK_DEV, HEAD_COUNT)).reshape(SEQUENCE_LENGTH, HEAD_COUNT)
    rough = jax.random.uniform(every_key[3], (SEQUENCE_LENGTH, HEAD_COUNT), jnp.float32, 0.5, 1.5)
    decay_speed = base[None, :] * block_scale * rough
    spike_locations = jax.random.randint(every_key[4], (2, HEAD_COUNT), 0, SEQUENCE_LENGTH)
    spike_penalty = jax.random.uniform(every_key[5], (2, HEAD_COUNT), jnp.float32, 0.2, 0.5)
    token_places = jnp.arange(SEQUENCE_LENGTH, dtype=jnp.int32)[:, None]
    spike_flag = jnp.zeros((SEQUENCE_LENGTH, HEAD_COUNT), jnp.float32)
    for selector_index in range(2):
        spike_flag = spike_flag + jnp.where(token_places == spike_locations[selector_index][None, :], jnp.log(1.0 - spike_penalty[selector_index])[None, :], 0.0)
    return (spike_flag - decay_speed).astype(jnp.float32)


def levels(rng, dims, pieces, smallest, high):
    gain, own = 1.0, jax.random.fold_in(rng, 6)
    for position, shards_of in pieces:
        heights = jnp.exp(jax.random.uniform(jax.random.fold_in(own, position), (shards_of,), jnp.float32, smallest / len(pieces), high / len(pieces)))
        gain = gain * jnp.repeat(heights, dims[position] // shards_of).reshape([-1 if axis == position else 1 for axis in range(len(dims))])
    return gain


def scatter_about(rng, extent, width, most, cuts=(), kind=jnp.bfloat16):
    factor_of = levels(rng, extent, cuts, -0.22, 0.18) if cuts else 1.0
    array = jax.random.normal(rng, extent, jnp.float32) * width * factor_of
    return jnp.minimum(jnp.maximum(array, -most), most).astype(kind)


def setup_inputs(seed: int = 0) -> dict:
    key_of = jax.random.split(jax.random.key(seed), 7)
    return {
        "queries": scatter_about(key_of[0], (SEQUENCE_LENGTH, HEAD_COUNT * HEAD_DIM), 1.0, 6.0, ((0, 8), (1, 4))),
        "key_vectors": scatter_about(key_of[1], (SEQUENCE_LENGTH, HEAD_COUNT * HEAD_DIM), 1.0, 6.0, ((0, 8), (1, 4))),
        "value_vectors": scatter_about(key_of[2], (SEQUENCE_LENGTH, HEAD_COUNT * HEAD_DIM), 1.0, 6.0, ((0, 8), (1, 4))),
        "gate_input": scatter_about(key_of[3], (SEQUENCE_LENGTH, HEAD_COUNT * HEAD_DIM), 1.0, 6.0, ((0, 8), (1, 4))),
        "log_decay": draw_log_decay(jax.random.fold_in(key_of[6], 71), 0),
        "out_weight": scatter_about(key_of[5], (HEAD_COUNT * HEAD_DIM, D), (HEAD_COUNT * HEAD_DIM) ** -0.5, 0.09375, ((0, 4),)),
    }


def reference(queries, key_vectors, value_vectors, gate_input, log_decay, out_weight):
    block_count = SEQUENCE_LENGTH // BLOCK_LEN
    split_shape = (block_count, BLOCK_LEN, HEAD_COUNT, HEAD_DIM)
    token_places = lax.iota(jnp.int32, BLOCK_LEN)
    causal = token_places[:, None] >= token_places[None, :]
    highest = lax.Precision.HIGHEST

    def advance(kv_state, blocks):
        query_block, key_block, value_block, rate_block = blocks
        running = jnp.cumsum(rate_block, axis=0)
        block_total = running[-1]
        query_float = query_block.astype(jnp.float32)
        key_float = key_block.astype(jnp.float32)
        value_float = value_block.astype(jnp.float32)
        scores = jnp.einsum('ihd,jhd->hij', query_float, key_float, precision=highest)
        by_head = running.T
        spread = by_head[:, :, None] - by_head[:, None, :]
        decay = jnp.exp(jnp.where(causal, spread, -1e+30))
        weights = lax.optimization_barrier((scores * decay).astype(jnp.bfloat16)).astype(jnp.float32)
        inside = jnp.einsum('hij,jhd->ihd', weights, value_float, precision=highest)
        query_scaled = query_float * jnp.exp(running)[:, :, None]
        carried = jnp.einsum('ihd,hde->ihe', query_scaled, kv_state, precision=highest)
        key_scaled = key_float * jnp.exp(block_total[None, :] - running)[:, :, None]
        kv_next = jnp.exp(block_total)[:, None, None] * kv_state + jnp.einsum('jhd,jhe->hde', key_scaled, value_float, precision=highest)
        return (kv_next, inside + carried)
    initial = jnp.zeros((HEAD_COUNT, HEAD_DIM, HEAD_DIM), jnp.float32)
    _, attended = lax.scan(advance, initial, (queries.reshape(split_shape), key_vectors.reshape(split_shape), value_vectors.reshape(split_shape), log_decay.reshape(block_count, BLOCK_LEN, HEAD_COUNT)))
    attended = attended.reshape(SEQUENCE_LENGTH, HEAD_COUNT, HEAD_DIM)
    inverse_rms = lax.rsqrt(lax.optimization_barrier(jnp.mean(attended * attended, axis=-1, keepdims=True)) + 1e-06)
    normed = (attended * inverse_rms).reshape(SEQUENCE_LENGTH, HEAD_COUNT * HEAD_DIM)
    hidden = (normed * jax.nn.silu(gate_input.astype(jnp.float32))).astype(jnp.bfloat16)
    hidden_float = lax.optimization_barrier(hidden).astype(jnp.float32)
    projected = jnp.dot(hidden_float, out_weight.astype(jnp.float32), precision=highest)
    return projected.astype(jnp.bfloat16)
```

```python
import functools

import jax
import jax.numpy as jnp
from jax import lax
from jax.experimental import pallas as pl
from jax.experimental.pallas import tpu as pltpu
from jax.sharding import PartitionSpec as P

HEAD_DIM = 128
VMEM_LIMIT = 32 * 1024 * 1024
ROW_GROUPS = 4
CHAIN_PARTS = 2
F32 = jnp.float32
BF16 = jnp.bfloat16


def head_columns(head):
    return slice(head * HEAD_DIM, (head + 1) * HEAD_DIM)


def split_pair(value):
    high = value.astype(BF16)
    low = (value - high.astype(F32)).astype(BF16)
    return jnp.concatenate([high, low], axis=1)


def fold_pair(value):
    return value[:, :HEAD_DIM] + value[:, HEAD_DIM:]


def lower_triangle(size):
    rows = lax.broadcasted_iota(jnp.int32, (size, size), 0)
    columns = lax.broadcasted_iota(jnp.int32, (size, size), 1)
    return rows >= columns


def running_sum(log_rates):
    ones = lower_triangle(log_rates.shape[0]).astype(F32)
    return jnp.dot(ones, log_rates, precision=lax.Precision.HIGHEST, preferred_element_type=F32)


def running_sum_rows(log_rates):
    ones = lower_triangle(log_rates.shape[0]).astype(F32)
    return lax.dot_general(
        log_rates, ones, (((0,), (1,)), ((), ())),
        precision=lax.Precision.HIGHEST, preferred_element_type=F32,
    )


def params():
    return pltpu.CompilerParams(vmem_limit_bytes=VMEM_LIMIT)


def states_kernel(odd_ref, rate_ref, key_ref, value_ref, keep_ref, send_ref, start_ref, lead_ref,
                  state, lead):
    block, blocks = pl.program_id(0), pl.num_programs(0)
    heads = rate_ref.shape[1]
    half = heads // 2

    @pl.when(block == 0)
    def _():
        state[...] = jnp.zeros_like(state)
        lead[...] = jnp.zeros_like(lead)

    running = running_sum(rate_ref[...])
    total = running[-1:, :]
    fade = jnp.exp(total - running)
    block_decay = jnp.exp(total)
    lead_ref[...] = jnp.exp(running + lead[...])
    lead[...] = lead[...] + total
    for head in range(heads):
        at = head_columns(head)
        scaled = value_ref[:, at].astype(F32) * fade[:, head:head + 1]
        gained = fold_pair(lax.dot_general(
            key_ref[:, at], split_pair(scaled), (((0,), (0,)), ((), ())), preferred_element_type=F32
        ))
        before = state[head]
        start_ref[0, head] = before
        state[head] = block_decay[:, head:head + 1] * before + gained

    @pl.when(block == blocks - 1)
    def _():
        through = jnp.exp(lead[...])
        for head in range(heads):
            side, place = head // half, head % half
            decay = jnp.broadcast_to(through[:, head:head + 1], (8, HEAD_DIM))

            @pl.when(odd_ref[0] == side)
            def _():
                keep_ref[place, :HEAD_DIM] = state[head]
                keep_ref[place, HEAD_DIM:] = decay

            @pl.when(odd_ref[0] != side)
            def _():
                send_ref[place, :HEAD_DIM] = state[head]
                send_ref[place, HEAD_DIM:] = decay


def local_states(odd, log_decay, key_vectors, value_vectors, block_len):
    tokens, features = key_vectors.shape
    heads = features // HEAD_DIM
    blocks = tokens // block_len
    message = jax.ShapeDtypeStruct((heads // 2, HEAD_DIM + 8, HEAD_DIM), F32)
    whole = pl.BlockSpec(message.shape, lambda b, odd: (0, 0, 0))
    rows = pl.BlockSpec((block_len, features), lambda b, odd: (b, 0))
    rates = pl.BlockSpec((block_len, heads), lambda b, odd: (b, 0))
    return pl.pallas_call(
        states_kernel,
        grid_spec=pltpu.PrefetchScalarGridSpec(
            num_scalar_prefetch=1,
            grid=(blocks,),
            in_specs=[rates, rows, rows],
            out_specs=[
                whole, whole,
                pl.BlockSpec((1, heads, HEAD_DIM, HEAD_DIM), lambda b, odd: (b, 0, 0, 0)),
                rates,
            ],
            scratch_shapes=[
                pltpu.VMEM((heads, HEAD_DIM, HEAD_DIM), F32), pltpu.VMEM((1, heads), F32)
            ],
        ),
        out_shape=[
            message, message,
            jax.ShapeDtypeStruct((blocks, heads, HEAD_DIM, HEAD_DIM), F32),
            jax.ShapeDtypeStruct((tokens, heads), F32),
        ],
        compiler_params=params(),
        cost_estimate=pl.CostEstimate(
            flops=4 * tokens * features * HEAD_DIM, bytes_accessed=8 * tokens * features,
            transcendentals=0),
    )(odd, log_decay, key_vectors, value_vectors)


def inside_kernel(first_ref, rate_ref, query_ref, key_ref, value_ref, start_ref, part_ref):
    heads = rate_ref.shape[1]
    size = rate_ref.shape[0]
    running = running_sum(rate_ref[...])
    running_rows = running_sum_rows(rate_ref[...])
    fade = jnp.exp(running)
    causal = lower_triangle(size)
    for head in range(heads):
        at = head_columns(head)
        queries = query_ref[:, at]
        scores = lax.dot_general(
            queries, key_ref[:, at], (((1,), (1,)), ((), ())), preferred_element_type=F32
        )
        spread = running[:, head:head + 1] - running_rows[head:head + 1, :]
        decay = jnp.exp(jnp.where(causal, spread, -1e30))
        weights = (scores * decay).astype(BF16)
        inside = jnp.dot(weights, value_ref[:, at], preferred_element_type=F32)
        carried = fold_pair(
            jnp.dot(queries, split_pair(start_ref[0, head]), preferred_element_type=F32)
        )
        part_ref[:, at] = inside + carried * fade[:, head:head + 1]


def inside_part(first, log_decay, queries, key_vectors, value_vectors, starts, block_len, count):
    tokens, features = queries.shape
    heads = features // HEAD_DIM
    rows = pl.BlockSpec((block_len, features), lambda b, first: (first[0] + b, 0))
    return pl.pallas_call(
        inside_kernel,
        grid_spec=pltpu.PrefetchScalarGridSpec(
            num_scalar_prefetch=1,
            grid=(count,),
            in_specs=[
                pl.BlockSpec((block_len, heads), lambda b, first: (first[0] + b, 0)),
                rows, rows, rows,
                pl.BlockSpec((1, heads, HEAD_DIM, HEAD_DIM), lambda b, first: (first[0] + b, 0, 0, 0)),
            ],
            out_specs=pl.BlockSpec((block_len, features), lambda b, first: (b, 0)),
        ),
        out_shape=jax.ShapeDtypeStruct((count * block_len, features), F32),
        compiler_params=params(),
        cost_estimate=pl.CostEstimate(
            flops=count * block_len * features * (4 * block_len + 4 * HEAD_DIM),
            bytes_accessed=count * block_len * features * 10,
            transcendentals=count * block_len * block_len * heads),
    )(first, log_decay, queries, key_vectors, value_vectors, starts)


def project_kernel(place_ref, *refs):
    sides = (refs[0:4], refs[4:8])
    keep_ref, got_ref, weight_ref = refs[8:11]
    outs, hidden = refs[11:13], refs[13]
    heads = keep_ref.shape[0] * 2
    half = heads // 2
    rows = outs[0].shape[0]

    @pl.when(pl.program_id(0) == 0)
    def _():
        is_odd = place_ref[2] == 1
        for head in range(heads):
            at = head_columns(head)
            side, place = head // half, head % half
            kept, got = keep_ref[place], got_ref[place]
            incoming = jnp.where(is_odd, kept, got) if side else jnp.where(is_odd, got, kept)
            pair = split_pair(incoming)
            for which, (query_ref, part_ref, gate_ref, lead_ref) in enumerate(sides):
                carried = fold_pair(jnp.dot(query_ref[:, at], pair, preferred_element_type=F32))
                attended = part_ref[:, at] + carried * lead_ref[:, head:head + 1]
                mean = jnp.mean(attended * attended, axis=1, keepdims=True)
                gate = gate_ref[:, at].astype(F32)
                normed = attended * lax.rsqrt(mean + 1e-6)
                hidden[which * rows:(which + 1) * rows, at] = (
                    normed * (gate / (1.0 + jnp.exp(-gate)))
                ).astype(BF16)

    result = jnp.dot(hidden[...], weight_ref[...], preferred_element_type=F32)
    outs[0][...] = result[:rows]
    outs[1][...] = result[rows:]


def project_rows(place, rows, row_group, block_len, queries, part, gate_input, lead, kept, got,
                 out_weight):
    tokens, features = queries.shape
    heads = features // HEAD_DIM
    width = out_weight.shape[1]
    tile = min(512, width)
    per_block = block_len // rows

    def side(which):
        def global_row(j, place):
            return (place[which] * per_block + row_group, 0)

        def group_row(j, place):
            core = place[3]
            local = core if which == 1 else 1 - core
            return (local * per_block + row_group, 0)

        return [
            pl.BlockSpec((rows, features), global_row),
            pl.BlockSpec((rows, features), group_row),
            pl.BlockSpec((rows, features), global_row),
            pl.BlockSpec((rows, heads), global_row),
        ]

    states = pl.BlockSpec((heads // 2, HEAD_DIM, HEAD_DIM), lambda j, place: (0, 0, 0))
    out = pl.BlockSpec((rows, tile), lambda j, place: (0, j))
    shape = jax.ShapeDtypeStruct((rows, width), F32)
    return pl.pallas_call(
        project_kernel,
        grid_spec=pltpu.PrefetchScalarGridSpec(
            num_scalar_prefetch=1,
            grid=(width // tile,),
            in_specs=side(0) + side(1) + [
                states, states, pl.BlockSpec((features, tile), lambda j, place: (0, j))
            ],
            out_specs=[out, out],
            scratch_shapes=[pltpu.VMEM((2 * rows, features), BF16)],
        ),
        out_shape=[shape, shape],
        compiler_params=params(),
        cost_estimate=pl.CostEstimate(
            flops=4 * rows * features * width, bytes_accessed=2 * features * width + 8 * rows * width,
            transcendentals=2 * rows * features),
    )(place, queries, part, gate_input, lead, queries, part, gate_input, lead, kept, got, out_weight)


def finish_kernel(*refs):
    out_ref = refs[-1]
    total = refs[0][...]
    for ref in refs[1:]:
        if ref is not out_ref and ref.dtype == F32:
            total = total + ref[...]
    out_ref[...] = total.astype(out_ref.dtype)


def finish_rows(group, arrived, own, sibling, result):
    rows, width = arrived[0].shape
    block_len = own.shape[0]
    here = pl.BlockSpec((rows, width), lambda i: (group, 0))
    plain = pl.BlockSpec((rows, width), lambda i: (0, 0))
    operands = [own, sibling, *arrived]
    specs = [here, here] + [plain] * len(arrived)
    aliases = {}
    if result is not None:
        aliases = {len(operands): 0}
        operands.append(result)
        specs.append(pl.BlockSpec(memory_space=pl.ANY))
    return pl.pallas_call(
        finish_kernel if result is None else lambda *refs: finish_kernel(*refs[:-2], refs[-1]),
        grid=(1,),
        in_specs=specs,
        out_specs=here,
        out_shape=jax.ShapeDtypeStruct((block_len, width), BF16),
        input_output_aliases=aliases,
        compiler_params=params(),
        cost_estimate=pl.CostEstimate(
            flops=rows * width, bytes_accessed=14 * rows * width, transcendentals=0),
    )(*operands)


def incoming_states(odd, kept, sent):
    count = lax.axis_size("seq")
    swap = [(i, i ^ 1) for i in range(count)]
    is_odd = odd == 1
    size = kept.shape[0] // CHAIN_PARTS
    pieces = [slice(i * size, (i + 1) * size) for i in range(CHAIN_PARTS)]
    got = [lax.ppermute(sent[at], "seq", swap) for at in pieces]
    first, first_decay, pair, pair_decay = [], [], [], []
    for at, other in zip(pieces, got):
        mine = kept[at]
        early = jnp.where(is_odd, other, mine)
        late = jnp.where(is_odd, mine, other)
        early_decay, late_decay = early[:, HEAD_DIM:HEAD_DIM + 1], late[:, HEAD_DIM:HEAD_DIM + 1]
        first.append(early[:, :HEAD_DIM])
        first_decay.append(early_decay)
        pair.append(late_decay * early[:, :HEAD_DIM] + late[:, :HEAD_DIM])
        pair_decay.append(late_decay * early_decay)
    entering = [None] * CHAIN_PARTS
    for hop in range(count // 2 - 1):
        along = [(2 * hop, 2 * hop + 2), (2 * hop + 1, 2 * hop + 3)]
        for i in range(CHAIN_PARTS):
            value = pair[i] if entering[i] is None else pair_decay[i] * entering[i] + pair[i]
            landed = lax.ppermute(value, "seq", along)
            entering[i] = landed if entering[i] is None else entering[i] + landed
    keep, back = [], []
    for i in range(CHAIN_PARTS):
        before = entering[i]
        after = first_decay[i] * before + first[i]
        keep.append(jnp.where(is_odd, after, before))
        back.append(lax.ppermute(jnp.where(is_odd, before, after), "seq", swap))
    return jnp.concatenate(keep), jnp.concatenate(back)


def per_device(queries, key_vectors, value_vectors, gate_input, log_decay, out_weight):
    tokens, features = queries.shape
    count = lax.axis_size("head")
    chips = count // 2
    block_len = tokens // count
    rows = block_len // ROW_GROUPS
    index = lax.axis_index("head")
    chip, core = index // 2, index % 2
    odd = lax.axis_index("seq") % 2
    odd_1 = odd.reshape(1).astype(jnp.int32)

    kept, sent, starts, lead = local_states(odd_1, log_decay, key_vectors, value_vectors, block_len)

    def part_of(target):
        return inside_part(
            (2 * target).reshape(1).astype(jnp.int32), log_decay, queries, key_vectors,
            value_vectors, starts, block_len, 2)

    def project(target, part, group, size):
        place = jnp.stack([2 * target + 1 - core, 2 * target + core, odd, core]).astype(jnp.int32)
        return project_rows(place, size, group, block_len, queries, part, gate_input, lead, keep, got,
                            out_weight)

    cores = [(i, i ^ 1) for i in range(count)]
    targets = [(chip + step) % chips for step in range(1, chips)]
    parts = [part_of(target) for target in targets]
    keep, got = incoming_states(odd, kept, sent)
    arrived = [[] for _ in range(ROW_GROUPS)]
    for step, (target, part) in enumerate(zip(targets, parts), 1):
        across = [(i, ((i // 2 + step) % chips) * 2 + i % 2) for i in range(count)]
        for group in range(ROW_GROUPS):
            theirs, mine = project(target, part, group, rows)
            total = mine + lax.ppermute(theirs, "head", cores)
            arrived[group].append(lax.ppermute(total, "head", across))
    theirs, mine = project(chip, part_of(chip), 0, block_len)
    sibling = lax.ppermute(theirs, "head", cores)
    result = None
    for group in range(ROW_GROUPS):
        result = finish_rows(group, arrived[group], mine, sibling, result)
    return result


def solution(mesh):
    placed = (
        P("seq", "head"),
        P("seq", "head"),
        P("seq", "head"),
        P("seq", "head"),
        P("seq", "head"),
        P("head", None),
    )
    return jax.shard_map(
        per_device, mesh=mesh, in_specs=placed, out_specs=P(("seq", "head"), None), check_vma=False
    )
```

```python
import functools

import jax
import jax.numpy as jnp
from jax import lax
from jax.experimental import pallas as pl
from jax.experimental.pallas import tpu as pltpu
from jax.sharding import PartitionSpec as P

HEAD_DIM = 128
VMEM_LIMIT = 32 * 1024 * 1024
ROW_GROUPS = 4
CHAIN_PARTS = 2
CORE_PIECES = 4
OWN_PIECES = 2
DEPTH = 2
SHORT = pl.CostEstimate(flops=1, bytes_accessed=1, transcendentals=0)
F32 = jnp.float32
BF16 = jnp.bfloat16


def head_columns(head):
    return slice(head * HEAD_DIM, (head + 1) * HEAD_DIM)


def split_pair(value):
    high = value.astype(BF16)
    low = (value - high.astype(F32)).astype(BF16)
    return jnp.concatenate([high, low], axis=1)


def fold_pair(value):
    return value[:, :HEAD_DIM] + value[:, HEAD_DIM:]


def lower_triangle(size):
    rows = lax.broadcasted_iota(jnp.int32, (size, size), 0)
    columns = lax.broadcasted_iota(jnp.int32, (size, size), 1)
    return rows >= columns


def running_sum(log_rates):
    ones = lower_triangle(log_rates.shape[0]).astype(F32)
    return jnp.dot(ones, log_rates, precision=lax.Precision.HIGHEST, preferred_element_type=F32)


def running_sum_rows(log_rates):
    ones = lower_triangle(log_rates.shape[0]).astype(F32)
    return lax.dot_general(
        log_rates, ones, (((0,), (1,)), ((), ())),
        precision=lax.Precision.HIGHEST, preferred_element_type=F32,
    )


def params():
    return pltpu.CompilerParams(vmem_limit_bytes=VMEM_LIMIT)


def states_kernel(odd_ref, rate_ref, key_ref, value_ref, keep_ref, send_ref, start_ref, lead_ref,
                  state, lead):
    block, blocks = pl.program_id(0), pl.num_programs(0)
    heads = rate_ref.shape[1]
    half = heads // 2

    @pl.when(block == 0)
    def _():
        state[...] = jnp.zeros_like(state)
        lead[...] = jnp.zeros_like(lead)

    running = running_sum(rate_ref[...])
    total = running[-1:, :]
    fade = jnp.exp(total - running)
    block_decay = jnp.exp(total)
    lead_ref[...] = jnp.exp(running + lead[...])
    lead[...] = lead[...] + total
    for head in range(heads):
        at = head_columns(head)
        scaled = value_ref[:, at].astype(F32) * fade[:, head:head + 1]
        gained = fold_pair(lax.dot_general(
            key_ref[:, at], split_pair(scaled), (((0,), (0,)), ((), ())), preferred_element_type=F32
        ))
        before = state[head]
        start_ref[0, head] = before
        state[head] = block_decay[:, head:head + 1] * before + gained

    @pl.when(block == blocks - 1)
    def _():
        through = jnp.exp(lead[...])
        for head in range(heads):
            side, place = head // half, head % half
            decay = jnp.broadcast_to(through[:, head:head + 1], (8, HEAD_DIM))

            @pl.when(odd_ref[0] == side)
            def _():
                keep_ref[place, :HEAD_DIM] = state[head]
                keep_ref[place, HEAD_DIM:] = decay

            @pl.when(odd_ref[0] != side)
            def _():
                send_ref[place, :HEAD_DIM] = state[head]
                send_ref[place, HEAD_DIM:] = decay


def local_states(odd, log_decay, key_vectors, value_vectors, block_len):
    tokens, features = key_vectors.shape
    heads = features // HEAD_DIM
    blocks = tokens // block_len
    message = jax.ShapeDtypeStruct((heads // 2, HEAD_DIM + 8, HEAD_DIM), F32)
    whole = pl.BlockSpec(message.shape, lambda b, odd: (0, 0, 0))
    rows = pl.BlockSpec((block_len, features), lambda b, odd: (b, 0))
    rates = pl.BlockSpec((block_len, heads), lambda b, odd: (b, 0))
    return pl.pallas_call(
        states_kernel,
        grid_spec=pltpu.PrefetchScalarGridSpec(
            num_scalar_prefetch=1,
            grid=(blocks,),
            in_specs=[rates, rows, rows],
            out_specs=[
                whole, whole,
                pl.BlockSpec((1, heads, HEAD_DIM, HEAD_DIM), lambda b, odd: (b, 0, 0, 0)),
                rates,
            ],
            scratch_shapes=[
                pltpu.VMEM((heads, HEAD_DIM, HEAD_DIM), F32), pltpu.VMEM((1, heads), F32)
            ],
        ),
        out_shape=[
            message, message,
            jax.ShapeDtypeStruct((blocks, heads, HEAD_DIM, HEAD_DIM), F32),
            jax.ShapeDtypeStruct((tokens, heads), F32),
        ],
        compiler_params=params(),
        cost_estimate=SHORT,
    )(odd, log_decay, key_vectors, value_vectors)


def inside_kernel(first_ref, rate_ref, query_ref, key_ref, value_ref, start_ref, after_ref, part_ref):
    del after_ref
    heads = rate_ref.shape[1]
    size = rate_ref.shape[0]
    running = running_sum(rate_ref[...])
    running_rows = running_sum_rows(rate_ref[...])
    fade = jnp.exp(running)
    causal = lower_triangle(size)
    for head in range(heads):
        at = head_columns(head)
        queries = query_ref[:, at]
        scores = lax.dot_general(
            queries, key_ref[:, at], (((1,), (1,)), ((), ())), preferred_element_type=F32
        )
        spread = running[:, head:head + 1] - running_rows[head:head + 1, :]
        decay = jnp.exp(jnp.where(causal, spread, -1e30))
        weights = (scores * decay).astype(BF16)
        inside = jnp.dot(weights, value_ref[:, at], preferred_element_type=F32)
        carried = fold_pair(
            jnp.dot(queries, split_pair(start_ref[0, head]), preferred_element_type=F32)
        )
        part_ref[:, at] = inside + carried * fade[:, head:head + 1]


def inside_part(first, log_decay, queries, key_vectors, value_vectors, starts, block_len, count, after):
    tokens, features = queries.shape
    heads = features // HEAD_DIM
    rows = pl.BlockSpec((block_len, features), lambda b, first: (first[0] + b, 0))
    return pl.pallas_call(
        inside_kernel,
        grid_spec=pltpu.PrefetchScalarGridSpec(
            num_scalar_prefetch=1,
            grid=(count,),
            in_specs=[
                pl.BlockSpec((block_len, heads), lambda b, first: (first[0] + b, 0)),
                rows, rows, rows,
                pl.BlockSpec((1, heads, HEAD_DIM, HEAD_DIM), lambda b, first: (first[0] + b, 0, 0, 0)),
                pl.BlockSpec(memory_space=pl.ANY),
            ],
            out_specs=pl.BlockSpec((block_len, features), lambda b, first: (b, 0)),
        ),
        out_shape=jax.ShapeDtypeStruct((count * block_len, features), F32),
        compiler_params=params(),
        cost_estimate=SHORT,
    )(first, log_decay, queries, key_vectors, value_vectors, starts, after)


def project_kernel(place_ref, *refs):
    sides = (refs[0:4], refs[4:8])
    keep_ref, got_ref, weight_ref = refs[8:11]
    outs, hidden = refs[12:-1], refs[-1]
    heads = keep_ref.shape[0] * 2
    half = heads // 2
    rows = outs[-1].shape[0]
    piece = outs[0].shape[0]

    @pl.when(pl.program_id(0) == 0)
    def _():
        is_odd = place_ref[2] == 1
        for head in range(heads):
            at = head_columns(head)
            side, place = head // half, head % half
            kept, got = keep_ref[place], got_ref[place]
            incoming = jnp.where(is_odd, kept, got) if side else jnp.where(is_odd, got, kept)
            pair = split_pair(incoming)
            for which, (query_ref, part_ref, gate_ref, lead_ref) in enumerate(sides):
                carried = fold_pair(jnp.dot(query_ref[:, at], pair, preferred_element_type=F32))
                attended = part_ref[:, at] + carried * lead_ref[:, head:head + 1]
                mean = jnp.mean(attended * attended, axis=1, keepdims=True)
                gate = gate_ref[:, at].astype(F32)
                normed = attended * lax.rsqrt(mean + 1e-6)
                hidden[which * rows:(which + 1) * rows, at] = (
                    normed * (gate / (1.0 + jnp.exp(-gate)))
                ).astype(BF16)

    result = jnp.dot(hidden[...], weight_ref[...], preferred_element_type=F32)
    for i, out_ref in enumerate(outs[:-1]):
        out_ref[...] = result[i * piece:(i + 1) * piece]
    outs[-1][...] = result[rows:]


def project_rows(place, rows, row_group, block_len, queries, part, gate_input, lead, kept, got,
                 out_weight, after, pieces):
    tokens, features = queries.shape
    heads = features // HEAD_DIM
    width = out_weight.shape[1]
    tile = min(512, width)
    per_block = block_len // rows

    def side(which):
        def global_row(j, place):
            return (place[which] * per_block + row_group, 0)

        def group_row(j, place):
            core = place[3]
            local = core if which == 1 else 1 - core
            return (local * per_block + row_group, 0)

        return [
            pl.BlockSpec((rows, features), global_row),
            pl.BlockSpec((rows, features), group_row),
            pl.BlockSpec((rows, features), global_row),
            pl.BlockSpec((rows, heads), global_row),
        ]

    states = pl.BlockSpec((heads // 2, HEAD_DIM, HEAD_DIM), lambda j, place: (0, 0, 0))
    sizes = [rows // pieces] * pieces + [rows]
    return pl.pallas_call(
        project_kernel,
        grid_spec=pltpu.PrefetchScalarGridSpec(
            num_scalar_prefetch=1,
            grid=(width // tile,),
            in_specs=side(0) + side(1) + [
                states, states, pl.BlockSpec((features, tile), lambda j, place: (0, j)),
                pl.BlockSpec(memory_space=pl.ANY),
            ],
            out_specs=[pl.BlockSpec((size, tile), lambda j, place: (0, j)) for size in sizes],
            scratch_shapes=[pltpu.VMEM((2 * rows, features), BF16)],
        ),
        out_shape=[jax.ShapeDtypeStruct((size, width), F32) for size in sizes],
        compiler_params=params(),
        cost_estimate=SHORT,
    )(place, queries, part, gate_input, lead, queries, part, gate_input, lead, kept, got, out_weight,
      after)


def add_kernel(own_ref, *refs):
    pieces, out_ref = refs[:-2], refs[-1]
    at = 0
    for ref in pieces:
        size = ref.shape[0]
        out_ref[at:at + size] = own_ref[at:at + size] + ref[...]
        at += size


def add_pieces(own, pieces, after):
    whole = pl.BlockSpec(own.shape, lambda: (0, 0))
    return pl.pallas_call(
        add_kernel,
        in_specs=[whole] + [pl.BlockSpec(piece.shape, lambda: (0, 0)) for piece in pieces]
        + [pl.BlockSpec(memory_space=pl.ANY)],
        out_specs=whole,
        out_shape=jax.ShapeDtypeStruct(own.shape, F32),
        compiler_params=params(),
        cost_estimate=SHORT,
    )(own, *pieces, after)


def finish_kernel(arrivals, own_ref, *refs):
    out_ref = refs[-1]
    arrived, pieces = refs[:arrivals], refs[arrivals:-2]
    at = 0
    for ref in pieces:
        size = ref.shape[0]
        total = own_ref[at:at + size] + ref[...]
        for other in arrived:
            total = total + other[at:at + size]
        out_ref[at:at + size] = total.astype(out_ref.dtype)
        at += size


def finish_rows(group, arrived, own, pieces, result, block_len):
    rows, width = own.shape
    whole = pl.BlockSpec((rows, width), lambda i: (0, 0))
    alias = {}
    if result is None:
        result = own
    else:
        alias = {1 + len(arrived) + len(pieces): 0}
    return pl.pallas_call(
        functools.partial(finish_kernel, len(arrived)),
        grid=(1,),
        in_specs=[whole] * (1 + len(arrived))
        + [pl.BlockSpec(piece.shape, lambda i: (0, 0)) for piece in pieces]
        + [pl.BlockSpec(memory_space=pl.ANY)],
        out_specs=pl.BlockSpec((rows, width), lambda i: (group, 0)),
        out_shape=jax.ShapeDtypeStruct((block_len, width), BF16),
        input_output_aliases=alias,
        compiler_params=params(),
        cost_estimate=SHORT,
    )(own, *arrived, *pieces, result)


def incoming_states(odd, kept, sent):
    count = lax.axis_size("seq")
    swap = [(i, i ^ 1) for i in range(count)]
    is_odd = odd == 1
    size = kept.shape[0] // CHAIN_PARTS
    pieces = [slice(i * size, (i + 1) * size) for i in range(CHAIN_PARTS)]
    got = [lax.ppermute(sent[at], "seq", swap) for at in pieces]
    first, first_decay, pair, pair_decay = [], [], [], []
    for at, other in zip(pieces, got):
        mine = kept[at]
        early = jnp.where(is_odd, other, mine)
        late = jnp.where(is_odd, mine, other)
        early_decay, late_decay = early[:, HEAD_DIM:HEAD_DIM + 1], late[:, HEAD_DIM:HEAD_DIM + 1]
        first.append(early[:, :HEAD_DIM])
        first_decay.append(early_decay)
        pair.append(late_decay * early[:, :HEAD_DIM] + late[:, :HEAD_DIM])
        pair_decay.append(late_decay * early_decay)
    entering = [None] * CHAIN_PARTS
    for hop in range(count // 2 - 1):
        along = [(2 * hop, 2 * hop + 2), (2 * hop + 1, 2 * hop + 3)]
        for i in range(CHAIN_PARTS):
            value = pair[i] if entering[i] is None else pair_decay[i] * entering[i] + pair[i]
            landed = lax.ppermute(value, "seq", along)
            entering[i] = landed if entering[i] is None else entering[i] + landed
    keep, back = [], []
    for i in range(CHAIN_PARTS):
        before = entering[i]
        after = first_decay[i] * before + first[i]
        keep.append(jnp.where(is_odd, after, before))
        back.append(lax.ppermute(jnp.where(is_odd, before, after), "seq", swap))
    return jnp.concatenate(keep), jnp.concatenate(back)


def per_device(queries, key_vectors, value_vectors, gate_input, log_decay, out_weight):
    tokens, features = queries.shape
    count = lax.axis_size("head")
    chips = count // 2
    block_len = tokens // count
    rows = block_len // ROW_GROUPS
    index = lax.axis_index("head")
    chip, core = index // 2, index % 2
    odd = lax.axis_index("seq") % 2
    odd_1 = odd.reshape(1).astype(jnp.int32)

    kept, sent, starts, lead = local_states(odd_1, log_decay, key_vectors, value_vectors, block_len)

    def part_of(target, after):
        return inside_part(
            (2 * target).reshape(1).astype(jnp.int32), log_decay, queries, key_vectors,
            value_vectors, starts, block_len, 2, after)

    def project(target, part, group, after, pieces):
        place = jnp.stack([2 * target + 1 - core, 2 * target + core, odd, core]).astype(jnp.int32)
        *theirs, mine = project_rows(
            place, rows, group, block_len, queries, part, gate_input, lead, keep, got, out_weight,
            after, pieces)
        return mine, [lax.ppermute(piece, "head", cores) for piece in theirs]

    cores = [(i, i ^ 1) for i in range(count)]
    targets = [(chip + step) % chips for step in range(1, chips)]
    parts = [part_of(target, sent) for target in targets]
    keep, got = incoming_states(odd, kept, sent)
    landed, last, own, result = [sent, sent], sent, [], None
    arrived = [[] for _ in range(ROW_GROUPS)]
    for group in range(ROW_GROUPS):
        for step, (target, part) in enumerate(zip(targets, parts), 1):
            across = [(i, ((i // 2 + step) % chips) * 2 + i % 2) for i in range(count)]
            mine, pieces = project(target, part, group, last, CORE_PIECES)
            last = add_pieces(mine, pieces, landed[-DEPTH])
            landed.append(lax.ppermute(last, "head", across))
            arrived[group].append(landed[-1])
    own_part = part_of(chip, last)
    for group in range(ROW_GROUPS):
        if group == ROW_GROUPS - 1:
            last = landed[-2]
        own.append(project(chip, own_part, group, last, OWN_PIECES))
        last = own[-1][0]
    for group in range(ROW_GROUPS):
        result = finish_rows(group, arrived[group], *own[group], result, block_len)
    return result


def solution(mesh):
    placed = (
        P("seq", "head"),
        P("seq", "head"),
        P("seq", "head"),
        P("seq", "head"),
        P("seq", "head"),
        P("head", None),
    )
    return jax.shard_map(
        per_device, mesh=mesh, in_specs=placed, out_specs=P(("seq", "head"), None), check_vma=False
    )
```

```python
import functools

import jax
import jax.numpy as jnp
from jax import lax
from jax.experimental import pallas as pl
from jax.experimental.pallas import tpu as pltpu
from jax.sharding import PartitionSpec as P

HEAD_DIM = 128
MIB = 1024 * 1024
ROW_GROUPS = 4
OWN_GROUPS = 2
CHAIN_PARTS = 2
CORE_PIECES = 4
OWN_PIECES = 2
DEPTH = 2
TILE = 1024
STREAM_MIB = 32
KERNEL_MIB = 32
SHORT = pl.CostEstimate(flops=1, bytes_accessed=1, transcendentals=0)
F32 = jnp.float32
BF16 = jnp.bfloat16


def head_columns(head):
    return slice(head * HEAD_DIM, (head + 1) * HEAD_DIM)


def split_pair(value):
    high = value.astype(BF16)
    low = (value - high.astype(F32)).astype(BF16)
    return jnp.concatenate([high, low], axis=1)


def fold_pair(value):
    return value[:, :HEAD_DIM] + value[:, HEAD_DIM:]


def lower_triangle(size):
    rows = lax.broadcasted_iota(jnp.int32, (size, size), 0)
    columns = lax.broadcasted_iota(jnp.int32, (size, size), 1)
    return rows >= columns


def split_three(value):
    high = value.astype(BF16).astype(F32)
    rest = value - high
    middle = rest.astype(BF16).astype(F32)
    return jnp.concatenate([high, middle, rest - middle], axis=0).astype(BF16)


def fold_three(value):
    count = value.shape[1] // 3
    return value[:, :count] + value[:, count:2 * count] + value[:, 2 * count:]


def running_sum(rates):
    ones = lower_triangle(rates.shape[1]).astype(F32).astype(BF16)
    return fold_three(lax.dot_general(
        ones, split_three(rates), (((1,), (1,)), ((), ())), preferred_element_type=F32
    ))


def running_sum_rows(rates):
    ones = lower_triangle(rates.shape[1]).astype(F32).astype(BF16)
    count = rates.shape[0]
    value = lax.dot_general(
        split_three(rates), ones, (((1,), (1,)), ((), ())), preferred_element_type=F32
    )
    return value[:count] + value[count:2 * count] + value[2 * count:]


def in_hbm(*arrays):
    return [pltpu.with_memory_space_constraint(array, pltpu.HBM) for array in arrays]


def params(mib=KERNEL_MIB):
    return pltpu.CompilerParams(vmem_limit_bytes=mib * MIB)


def states_kernel(side_ref, rate_ref, key_hbm, value_hbm, *refs):
    message_refs = refs[:CHAIN_PARTS]
    start_hbm, keys, values, starts, key_sem, value_sem, start_sem = refs[CHAIN_PARTS:]
    blocks, half = starts.shape[:2]
    width = keys.shape[1]
    size = keys.shape[0] // blocks
    per_part = half // CHAIN_PARTS
    columns = pl.ds(pl.multiple_of(side_ref[0] * width, width), width)
    rows = [slice(block * size, (block + 1) * size) for block in range(blocks)]
    loads = [
        (pltpu.make_async_copy(key_hbm.at[at, columns], keys.at[at], key_sem.at[block]),
         pltpu.make_async_copy(value_hbm.at[at, columns], values.at[at], value_sem.at[block]))
        for block, at in enumerate(rows)
    ]
    stores = [
        pltpu.make_async_copy(starts.at[block], start_hbm.at[block], start_sem.at[block])
        for block in range(blocks)
    ]
    for load in [load for pair in loads[:2] for load in pair]:
        load.start()
    starts[0] = jnp.zeros_like(starts[0])
    stores[0].start()
    rates = jnp.where(side_ref[0] == 1, rate_ref[half:, :], rate_ref[:half, :])
    lead = jnp.zeros((1, half), F32)
    for block, at in enumerate(rows):
        running = running_sum(rates[:, at])
        total = running[-1:, :]
        fade = jnp.exp(total - running)
        block_decay = jnp.exp(total)
        lead = lead + total
        for load in loads[block]:
            load.wait()
        for load in loads[block + 2] if block + 2 < blocks else ():
            load.start()
        for head in range(half):
            of_head = head_columns(head)
            scaled = values[at, of_head].astype(F32) * fade[:, head:head + 1]
            gained = fold_pair(lax.dot_general(
                keys[at, of_head], split_pair(scaled), (((0,), (0,)), ((), ())),
                preferred_element_type=F32
            ))
            state = block_decay[:, head:head + 1] * starts[block, head] + gained
            if block + 1 < blocks:
                starts[block + 1, head] = state
            else:
                message_refs[head // per_part][head % per_part, :HEAD_DIM] = state
        if block + 1 < blocks:
            stores[block + 1].start()
    through = jnp.exp(lead)
    for head in range(half):
        message_refs[head // per_part][head % per_part, HEAD_DIM:] = jnp.broadcast_to(
            through[:, head:head + 1], (8, HEAD_DIM))
    for store in stores:
        store.wait()


def local_states(side, rates, key_vectors, value_vectors, block_len):
    tokens, features = key_vectors.shape
    half = features // HEAD_DIM // 2
    blocks = tokens // block_len
    message = jax.ShapeDtypeStruct((half // CHAIN_PARTS, HEAD_DIM + 8, HEAD_DIM), F32)
    starts = pltpu.HBM((blocks, half, HEAD_DIM, HEAD_DIM), F32)
    vmem, far = pl.BlockSpec(memory_space=pltpu.VMEM), pl.BlockSpec(memory_space=pl.ANY)
    *messages, starts = pl.pallas_call(
        states_kernel,
        in_specs=[pl.BlockSpec(memory_space=pltpu.SMEM), vmem, far, far],
        out_specs=[vmem] * CHAIN_PARTS + [far],
        out_shape=[message] * CHAIN_PARTS + [starts],
        scratch_shapes=[
            pltpu.VMEM((tokens, features // 2), BF16),
            pltpu.VMEM((tokens, features // 2), BF16),
            pltpu.VMEM((blocks, half, HEAD_DIM, HEAD_DIM), F32),
        ] + [pltpu.SemaphoreType.DMA((blocks,))] * 3,
        compiler_params=params(STREAM_MIB),
        cost_estimate=SHORT,
    )(side, *in_hbm(rates, key_vectors, value_vectors))
    return messages, starts


def inside_kernel(place_ref, rate_ref, query_hbm, key_hbm, value_hbm, keep_hbm, send_hbm, after_ref,
                  *refs):
    del after_ref
    queries, keys, values, keeps, sends, parts, load_sem, store_sem = refs[-8:]
    outs = refs[:-8]
    heads, tokens = rate_ref.shape
    count, half = keeps.shape[:2]
    size = queries.shape[0] // count
    is_odd = place_ref[count] == 1
    rows = [slice(block * size, (block + 1) * size) for block in range(count)]
    loads = [[] for _ in rows]
    for block, at in enumerate(rows):
        place = place_ref[block]
        far = pl.ds(pl.multiple_of(place * size, size), size)
        pairs = [(query_hbm.at[far], queries.at[at]), (key_hbm.at[far], keys.at[at]),
                 (value_hbm.at[far], values.at[at]), (keep_hbm.at[place], keeps.at[block]),
                 (send_hbm.at[place], sends.at[block])]
        for i, (source, target) in enumerate(pairs):
            loads[block].append(pltpu.make_async_copy(source, target, load_sem.at[block, i]))
    for load in loads[0]:
        load.start()
    stores = [
        pltpu.make_async_copy(parts.at[at], outs[2 * block], store_sem.at[block])
        for block, at in enumerate(rows)
    ]
    causal = lower_triangle(size)
    for block, at in enumerate(rows):
        begin = place_ref[block] * size
        rates = rate_ref[:, pl.ds(pl.multiple_of(begin, size), size)]
        ahead = (lax.broadcasted_iota(jnp.int32, (8, tokens), 1) < begin).astype(F32)
        lead = fold_three(lax.dot_general(
            ahead.astype(BF16), split_three(rate_ref[...]), (((1,), (1,)), ((), ())),
            preferred_element_type=F32,
        ))
        running = running_sum(rates)
        running_rows = running_sum_rows(rates)
        fade = jnp.exp(running)
        outs[2 * block + 1][...] = jnp.exp(running + lead[:1])
        for load in loads[block]:
            load.wait()
        for load in loads[block + 1] if block + 1 < count else ():
            load.start()
        for head in range(heads):
            of_head = head_columns(head)
            side, slot = head // half, head % half
            kept, sent = keeps[block, slot], sends[block, slot]
            start = jnp.where(is_odd, kept, sent) if side else jnp.where(is_odd, sent, kept)
            query = queries[at, of_head]
            scores = lax.dot_general(
                query, keys[at, of_head], (((1,), (1,)), ((), ())), preferred_element_type=F32
            )
            spread = running[:, head:head + 1] - running_rows[head:head + 1, :]
            decay = jnp.exp(jnp.where(causal, spread, -1e30))
            weights = (scores * decay).astype(BF16)
            inside = jnp.dot(weights, values[at, of_head], preferred_element_type=F32)
            carried = fold_pair(jnp.dot(query, split_pair(start), preferred_element_type=F32))
            parts[at, of_head] = inside + carried * fade[:, head:head + 1]
        stores[block].start()
    for store in stores:
        store.wait()


def inside_part(place, rates, queries, key_vectors, value_vectors, starts, block_len, after):
    count = place.shape[0] - 1
    features = queries.shape[1]
    heads = features // HEAD_DIM
    vmem, far = pl.BlockSpec(memory_space=pltpu.VMEM), pl.BlockSpec(memory_space=pl.ANY)
    rows = pltpu.VMEM((count * block_len, features), BF16)
    state = pltpu.VMEM((count, heads // 2, HEAD_DIM, HEAD_DIM), F32)
    return pl.pallas_call(
        inside_kernel,
        in_specs=[pl.BlockSpec(memory_space=pltpu.SMEM), vmem] + [far] * 6,
        out_specs=[far, vmem] * count,
        out_shape=[
            pltpu.HBM((block_len, features), F32), pltpu.HBM((block_len, heads), F32),
        ] * count,
        scratch_shapes=[rows, rows, rows, state, state,
                        pltpu.VMEM((count * block_len, features), F32),
                        pltpu.SemaphoreType.DMA((count, 5)), pltpu.SemaphoreType.DMA((count,))],
        compiler_params=params(STREAM_MIB),
        cost_estimate=SHORT,
    )(place, *in_hbm(rates, queries, key_vectors, value_vectors, *starts, after))


def project_kernel(first_row, block_len, pieces, place_ref, query_hbm, gate_hbm, weight_hbm, part_0,
                   lead_0, part_1, lead_1, after_ref, *refs):
    del after_ref
    states, refs = refs[:2 * CHAIN_PARTS], refs[2 * CHAIN_PARTS:]
    outs, refs = refs[:pieces + 1], refs[pieces + 1:]
    queries, parts, gates, leads, incoming, weight, hidden, result = refs[:8]
    row_sem, state_sem, weight_sem, out_sem = refs[8:]
    rows, width = outs[-1].shape
    features = queries.shape[1]
    heads = features // HEAD_DIM
    half = heads // 2
    per_part = half // CHAIN_PARTS
    tile = width // weight_sem.shape[0]
    is_odd = place_ref[2] == 1

    loads = []
    for which, (part_hbm, lead_hbm) in enumerate(((part_0, lead_0), (part_1, lead_1))):
        whole = pl.ds(pl.multiple_of(place_ref[which] * block_len + first_row, rows), rows)
        group = slice(first_row, first_row + rows)
        at = slice(which * rows, (which + 1) * rows)
        pairs = [(query_hbm.at[whole], queries.at[at]), (part_hbm.at[group], parts.at[at]),
                 (gate_hbm.at[whole], gates.at[at]), (lead_hbm.at[group], leads.at[at])]
        loads += [pltpu.make_async_copy(source, target, row_sem.at[which, i])
                  for i, (source, target) in enumerate(pairs)]
    loads += [pltpu.make_async_copy(ref, incoming.at[i], state_sem.at[i])
              for i, ref in enumerate(states)]
    columns = [slice(at, at + tile) for at in range(0, width, tile)]
    weights = [
        pltpu.make_async_copy(weight_hbm.at[:, at], weight.at[:, at], weight_sem.at[i])
        for i, at in enumerate(columns)
    ]
    for load in loads + weights[:1]:
        load.start()
    for load in loads:
        load.wait()
    for load in weights[1:]:
        load.start()
    for head in range(heads):
        at = head_columns(head)
        side, place = head // half, head % half
        part, slot = place // per_part, place % per_part
        kept, got = incoming[part, slot], incoming[CHAIN_PARTS + part, slot]
        state = jnp.where(is_odd, kept, got) if side else jnp.where(is_odd, got, kept)
        carried = fold_pair(jnp.dot(queries[:, at], split_pair(state), preferred_element_type=F32))
        attended = parts[:, at] + carried * leads[:, head:head + 1]
        mean = jnp.mean(attended * attended, axis=1, keepdims=True)
        gate = gates[:, at].astype(F32)
        normed = attended * lax.rsqrt(mean + 1e-6)
        hidden[:, at] = (normed * (gate / (1.0 + jnp.exp(-gate)))).astype(BF16)
    stores = []
    for i, at in enumerate(columns):
        weights[i].wait()
        result[:, at] = jnp.dot(hidden[...], weight[:, at], preferred_element_type=F32)
        begin = 0
        for j, out in enumerate(outs):
            size = out.shape[0]
            store = pltpu.make_async_copy(
                result.at[begin:begin + size, at], out.at[:, at], out_sem.at[j, i])
            store.start()
            stores.append(store)
            begin += size
    for store in stores:
        store.wait()


def project_rows(place, rows, first_row, block_len, queries, parts, gate_input, kept, got,
                 out_weight, after, pieces):
    features = queries.shape[1]
    width = out_weight.shape[1]
    tiles = max(1, width // TILE)
    sizes = [rows // pieces] * pieces + [rows]
    far = pl.BlockSpec(memory_space=pl.ANY)
    dma = pltpu.SemaphoreType.DMA
    return pl.pallas_call(
        functools.partial(project_kernel, first_row, block_len, pieces),
        in_specs=[pl.BlockSpec(memory_space=pltpu.SMEM)] + [far] * (8 + 2 * CHAIN_PARTS),
        out_specs=[far] * len(sizes),
        out_shape=[jax.ShapeDtypeStruct((size, width), F32) for size in sizes],
        scratch_shapes=[
            pltpu.VMEM((2 * rows, features), BF16),
            pltpu.VMEM((2 * rows, features), F32),
            pltpu.VMEM((2 * rows, features), BF16),
            pltpu.VMEM((2 * rows, features // HEAD_DIM), F32),
            pltpu.VMEM((2 * CHAIN_PARTS, *kept[0].shape), F32),
            pltpu.VMEM(out_weight.shape, BF16),
            pltpu.VMEM((2 * rows, features), BF16),
            pltpu.VMEM((2 * rows, width), F32),
            dma((2, 4)), dma((2 * CHAIN_PARTS,)), dma((tiles,)), dma((len(sizes), tiles)),
        ],
        compiler_params=params(),
        cost_estimate=SHORT,
    )(place, *in_hbm(queries, gate_input, out_weight, *parts[0], *parts[1], after), *kept, *got)


def add_kernel(own_ref, *refs):
    pieces, out_ref = refs[:-2], refs[-1]
    at = 0
    for ref in pieces:
        size = ref.shape[0]
        out_ref[at:at + size] = own_ref[at:at + size] + ref[...]
        at += size


def add_pieces(own, pieces, after):
    whole = pl.BlockSpec(own.shape, lambda: (0, 0))
    return pl.pallas_call(
        add_kernel,
        in_specs=[whole] + [pl.BlockSpec(piece.shape, lambda: (0, 0)) for piece in pieces]
        + [pl.BlockSpec(memory_space=pl.ANY)],
        out_specs=whole,
        out_shape=jax.ShapeDtypeStruct(own.shape, F32),
        compiler_params=params(),
        cost_estimate=SHORT,
    )(own, *pieces, *in_hbm(after))


def finish_kernel(arrivals, own_ref, *refs):
    out_ref = refs[-1]
    arrived, pieces = refs[:arrivals], refs[arrivals:-2]
    at = 0
    for ref in pieces:
        size = ref.shape[0]
        total = own_ref[at:at + size] + ref[...]
        for other in arrived:
            total = total + other[at:at + size]
        out_ref[at:at + size] = total.astype(out_ref.dtype)
        at += size


def finish_rows(group, arrived, own, own_group, pieces, result, block_len):
    rows, width = arrived[0].shape
    whole = pl.BlockSpec((rows, width), lambda i: (0, 0))
    alias = {}
    if result is None:
        result = own
    else:
        alias = {1 + len(arrived) + len(pieces): 0}
    return pl.pallas_call(
        functools.partial(finish_kernel, len(arrived)),
        grid=(1,),
        in_specs=[pl.BlockSpec((rows, width), lambda i: (own_group, 0))] + [whole] * len(arrived)
        + [pl.BlockSpec(piece.shape, lambda i: (0, 0)) for piece in pieces]
        + [pl.BlockSpec(memory_space=pl.ANY)],
        out_specs=pl.BlockSpec((rows, width), lambda i: (group, 0)),
        out_shape=jax.ShapeDtypeStruct((block_len, width), BF16),
        input_output_aliases=alias,
        compiler_params=params(),
        cost_estimate=SHORT,
    )(own, *arrived, *pieces, result)


def hop_kernel(hops, odd_ref, *refs):
    landed, (kept_ref, got_ref, after_ref, value_ref) = refs[:hops], refs[hops:]
    del after_ref
    is_odd = odd_ref[0] == 1
    for slot in range(value_ref.shape[0]):
        kept, got = kept_ref[slot], got_ref[slot]
        early, late = jnp.where(is_odd, got, kept), jnp.where(is_odd, kept, got)
        late_decay = late[HEAD_DIM:HEAD_DIM + 1]
        value = early[:HEAD_DIM]
        if landed:
            before = landed[0][slot]
            for ref in landed[1:]:
                before = before + ref[slot]
            value = early[HEAD_DIM:HEAD_DIM + 1] * before + value
        value_ref[slot] = late_decay * value + late[:HEAD_DIM]


def hop_states(odd, landed, kept, got, after):
    vmem = pl.BlockSpec(memory_space=pltpu.VMEM)
    return pl.pallas_call(
        functools.partial(hop_kernel, len(landed)),
        in_specs=[pl.BlockSpec(memory_space=pltpu.SMEM)] + [vmem] * (len(landed) + 2)
        + [pl.BlockSpec(memory_space=pl.ANY)],
        out_specs=vmem,
        out_shape=jax.ShapeDtypeStruct((kept.shape[0], HEAD_DIM, HEAD_DIM), F32),
        compiler_params=params(),
        cost_estimate=SHORT,
    )(odd, *landed, kept, got, *in_hbm(after))


def entering_kernel(hops, odd_ref, *refs):
    landed, (kept_ref, got_ref, after_ref, keep_ref, back_ref) = refs[:hops], refs[hops:]
    del after_ref
    is_odd = odd_ref[0] == 1
    for slot in range(keep_ref.shape[0]):
        before = landed[0][slot]
        for ref in landed[1:]:
            before = before + ref[slot]
        first = jnp.where(is_odd, got_ref[slot], kept_ref[slot])
        after = first[HEAD_DIM:HEAD_DIM + 1] * before + first[:HEAD_DIM]
        keep_ref[slot] = jnp.where(is_odd, after, before)
        back_ref[slot] = jnp.where(is_odd, before, after)


def entering_states(odd, landed, kept, got, after):
    shape = jax.ShapeDtypeStruct(landed[0].shape, F32)
    vmem = pl.BlockSpec(memory_space=pltpu.VMEM)
    return pl.pallas_call(
        functools.partial(entering_kernel, len(landed)),
        in_specs=[pl.BlockSpec(memory_space=pltpu.SMEM)] + [vmem] * (len(landed) + 2)
        + [pl.BlockSpec(memory_space=pl.ANY)],
        out_specs=[vmem, vmem],
        out_shape=[shape, shape],
        compiler_params=params(),
        cost_estimate=SHORT,
    )(odd, *landed, kept, got, *in_hbm(after))


def incoming_states(odd, kept, got, after, meanwhile):
    count = lax.axis_size("seq")
    swap = [(i, i ^ 1) for i in range(count)]
    parts = range(CHAIN_PARTS)
    landed = [[] for _ in parts]
    for hop in range(count // 2 - 1):
        along = [(2 * hop, 2 * hop + 2), (2 * hop + 1, 2 * hop + 3)]
        for i in parts:
            value = hop_states(odd, landed[i], kept[i], got[i], after)
            landed[i].append(lax.ppermute(value, "seq", along))
        if hop == count // 2 - 3:
            for work in meanwhile:
                after = work(value)
    keep, back = [], []
    for i in parts:
        mine, other = entering_states(odd, landed[i], kept[i], got[i], after)
        keep.append(mine)
        back.append(lax.ppermute(other, "seq", swap))
    return keep, back


def per_device(queries, key_vectors, value_vectors, gate_input, log_decay, out_weight):
    tokens = queries.shape[0]
    count = lax.axis_size("head")
    chips = count // 2
    block_len = tokens // count
    sizes = [block_len // ROW_GROUPS] * ROW_GROUPS
    firsts = [sum(sizes[:i]) for i in range(len(sizes))]
    index = lax.axis_index("head")
    chip, core = index // 2, index % 2
    place_in_seq = lax.axis_index("seq")
    odd = (place_in_seq % 2).reshape(1).astype(jnp.int32)
    rates = log_decay.T
    swap = [(i, i ^ 1) for i in range(lax.axis_size("seq"))]

    sent, sent_starts = local_states(1 - odd, rates, key_vectors, value_vectors, block_len)
    met = [lax.ppermute(piece, "seq", swap) for piece in sent]
    kept, kept_starts = local_states(odd, rates, key_vectors, value_vectors, block_len)

    def parts_of(target, after):
        place = jnp.stack([2 * target + 1 - core, 2 * target + core, odd[0]]).astype(jnp.int32)
        outs = inside_part(place, rates, queries, key_vectors, value_vectors,
                           (kept_starts, sent_starts), block_len, after)
        return outs[:2], outs[2:]

    def project(target, parts, group, after, pieces):
        place = jnp.stack([2 * target + 1 - core, 2 * target + core, odd[0]]).astype(jnp.int32)
        *theirs, mine = project_rows(
            place, sizes[group], firsts[group], block_len, queries, parts, gate_input, keep, got,
            out_weight, after, pieces)
        return mine, [lax.ppermute(piece, "head", cores) for piece in theirs]

    cores = [(i, i ^ 1) for i in range(count)]
    targets = [(chip + step) % chips for step in range(1, chips)]
    parts = []

    def inside_of(target, after):
        parts.append(parts_of(target, after))
        return parts[-1][1][1]

    keep, got = incoming_states(
        odd, kept, met, kept_starts, [functools.partial(inside_of, target) for target in targets])
    last = keep[0]
    landed, own, result = [last, last], [], None
    arrived = [[] for _ in sizes]
    for group in range(len(sizes)):
        for step, target in enumerate(targets):
            across = [(i, ((i // 2 + step + 1) % chips) * 2 + i % 2) for i in range(count)]
            mine, pieces = project(target, parts[step], group, last, CORE_PIECES)
            last = add_pieces(mine, pieces, landed[-DEPTH])
            landed.append(lax.ppermute(last, "head", across))
            arrived[group].append(landed[-1])
    own_parts = parts_of(chip, last)
    ratio = ROW_GROUPS // OWN_GROUPS
    sizes = [block_len // OWN_GROUPS] * OWN_GROUPS
    firsts = [sum(sizes[:i]) for i in range(len(sizes))]
    for group in range(len(sizes)):
        if group == len(sizes) - 1:
            last = landed[-2]
        own.append(project(chip, own_parts, group, last, OWN_PIECES * ratio))
        last = own[-1][0]
    for group in range(len(arrived)):
        mine, pieces = own[group // ratio]
        place = group % ratio
        result = finish_rows(group, arrived[group], mine, place,
                             pieces[place * OWN_PIECES:(place + 1) * OWN_PIECES], result, block_len)
    return result


def solution(mesh):
    placed = (
        P("seq", "head"),
        P("seq", "head"),
        P("seq", "head"),
        P("seq", "head"),
        P("seq", "head"),
        P("head", None),
    )
    return jax.shard_map(
        per_device, mesh=mesh, in_specs=placed, out_specs=P(("seq", "head"), None), check_vma=False
    )
```

```python
import functools

import jax
import jax.numpy as jnp
from jax import lax
from jax.experimental import pallas as pl
from jax.experimental.pallas import tpu as pltpu
from jax.sharding import PartitionSpec as P

HEAD_DIM = 128
MIB = 1024 * 1024
ROW_SHARES = (4, 4, 4, 4)
OWN_GROUPS = 2
CHAIN_PARTS = 2
CORE_PIECES = 4
DEPTH = 2
TILE = 1024
STREAM_MIB = 32
KERNEL_MIB = 32
SHORT = pl.CostEstimate(flops=1, bytes_accessed=1, transcendentals=0)
F32 = jnp.float32
BF16 = jnp.bfloat16


def head_columns(head):
    return slice(head * HEAD_DIM, (head + 1) * HEAD_DIM)


def split_pair(value):
    high = value.astype(BF16)
    low = (value - high.astype(F32)).astype(BF16)
    return jnp.concatenate([high, low], axis=1)


def fold_pair(value):
    return value[:, :HEAD_DIM] + value[:, HEAD_DIM:]


def lower_triangle(size):
    rows = lax.broadcasted_iota(jnp.int32, (size, size), 0)
    columns = lax.broadcasted_iota(jnp.int32, (size, size), 1)
    return rows >= columns


def split_three(value):
    high = value.astype(BF16).astype(F32)
    rest = value - high
    middle = rest.astype(BF16).astype(F32)
    return jnp.concatenate([high, middle, rest - middle], axis=0).astype(BF16)


def fold_three(value):
    count = value.shape[1] // 3
    return value[:, :count] + value[:, count:2 * count] + value[:, 2 * count:]


def running_sum(rates):
    ones = lower_triangle(rates.shape[1]).astype(F32).astype(BF16)
    return fold_three(lax.dot_general(
        ones, split_three(rates), (((1,), (1,)), ((), ())), preferred_element_type=F32
    ))


def running_sum_rows(rates):
    ones = lower_triangle(rates.shape[1]).astype(F32).astype(BF16)
    count = rates.shape[0]
    value = lax.dot_general(
        split_three(rates), ones, (((1,), (1,)), ((), ())), preferred_element_type=F32
    )
    return value[:count] + value[count:2 * count] + value[2 * count:]


def in_hbm(*arrays):
    return [pltpu.with_memory_space_constraint(array, pltpu.HBM) for array in arrays]


def params(mib=KERNEL_MIB):
    return pltpu.CompilerParams(vmem_limit_bytes=mib * MIB)


def states_kernel(side_ref, rate_hbm, key_hbm, value_hbm, *refs):
    message_refs = refs[:CHAIN_PARTS]
    start_hbm, rate_ref, keys, values, starts, rate_sem, key_sem, value_sem, start_sem = refs[CHAIN_PARTS:]
    blocks, half = starts.shape[:2]
    width = keys.shape[1]
    size = keys.shape[0] // blocks
    per_part = half // CHAIN_PARTS
    columns = pl.ds(pl.multiple_of(side_ref[0] * width, width), width)
    rows = [slice(block * size, (block + 1) * size) for block in range(blocks)]
    loads = [
        (pltpu.make_async_copy(key_hbm.at[at, columns], keys.at[at], key_sem.at[block]),
         pltpu.make_async_copy(value_hbm.at[at, columns], values.at[at], value_sem.at[block]))
        for block, at in enumerate(rows)
    ]
    stores = [
        pltpu.make_async_copy(starts.at[block], start_hbm.at[block], start_sem.at[block])
        for block in range(blocks)
    ]
    rate_load = pltpu.make_async_copy(rate_hbm, rate_ref, rate_sem)
    rate_load.start()
    for load in [load for pair in loads[:2] for load in pair]:
        load.start()
    starts[0] = jnp.zeros_like(starts[0])
    stores[0].start()
    rate_load.wait()
    rates = jnp.where(side_ref[0] == 1, rate_ref[half:, :], rate_ref[:half, :])
    lead = jnp.zeros((1, half), F32)
    for block, at in enumerate(rows):
        running = running_sum(rates[:, at])
        total = running[-1:, :]
        fade = jnp.exp(total - running)
        block_decay = jnp.exp(total)
        lead = lead + total
        for load in loads[block]:
            load.wait()
        for load in loads[block + 2] if block + 2 < blocks else ():
            load.start()
        for head in range(half):
            of_head = head_columns(head)
            scaled = values[at, of_head].astype(F32) * fade[:, head:head + 1]
            gained = fold_pair(lax.dot_general(
                keys[at, of_head], split_pair(scaled), (((0,), (0,)), ((), ())),
                preferred_element_type=F32
            ))
            state = block_decay[:, head:head + 1] * starts[block, head] + gained
            if block + 1 < blocks:
                starts[block + 1, head] = state
            else:
                message_refs[head // per_part][head % per_part, :HEAD_DIM] = state
        if block + 1 < blocks:
            stores[block + 1].start()
    through = jnp.exp(lead)
    for head in range(half):
        message_refs[head // per_part][head % per_part, HEAD_DIM:] = jnp.broadcast_to(
            through[:, head:head + 1], (8, HEAD_DIM))
    for store in stores:
        store.wait()


def local_states(side, rates, key_vectors, value_vectors, block_len):
    tokens, features = key_vectors.shape
    half = features // HEAD_DIM // 2
    blocks = tokens // block_len
    message = jax.ShapeDtypeStruct((half // CHAIN_PARTS, HEAD_DIM + 8, HEAD_DIM), F32)
    starts = pltpu.HBM((blocks, half, HEAD_DIM, HEAD_DIM), F32)
    vmem, far = pl.BlockSpec(memory_space=pltpu.VMEM), pl.BlockSpec(memory_space=pl.ANY)
    *messages, starts = pl.pallas_call(
        states_kernel,
        in_specs=[pl.BlockSpec(memory_space=pltpu.SMEM), far, far, far],
        out_specs=[vmem] * CHAIN_PARTS + [far],
        out_shape=[message] * CHAIN_PARTS + [starts],
        scratch_shapes=[
            pltpu.VMEM(rates.shape, F32),
            pltpu.VMEM((tokens, features // 2), BF16),
            pltpu.VMEM((tokens, features // 2), BF16),
            pltpu.VMEM((blocks, half, HEAD_DIM, HEAD_DIM), F32),
            pltpu.SemaphoreType.DMA,
        ] + [pltpu.SemaphoreType.DMA((blocks,))] * 3,
        compiler_params=params(STREAM_MIB),
        cost_estimate=SHORT,
    )(side, *in_hbm(rates, key_vectors, value_vectors))
    return messages, starts


def inside_kernel(place_ref, rate_hbm, query_hbm, key_hbm, value_hbm, keep_hbm, send_hbm, after_ref,
                  *refs):
    del after_ref
    rate_ref, queries, keys, values, keeps, sends, parts, rate_sem, load_sem, store_sem = refs[-10:]
    outs = refs[:-10]
    heads, tokens = rate_ref.shape
    count, half = keeps.shape[:2]
    size = queries.shape[0] // count
    is_odd = place_ref[count] == 1
    rows = [slice(block * size, (block + 1) * size) for block in range(count)]
    loads = [[] for _ in rows]
    for block, at in enumerate(rows):
        place = place_ref[block]
        far = pl.ds(pl.multiple_of(place * size, size), size)
        pairs = [(query_hbm.at[far], queries.at[at]), (key_hbm.at[far], keys.at[at]),
                 (value_hbm.at[far], values.at[at]), (keep_hbm.at[place], keeps.at[block]),
                 (send_hbm.at[place], sends.at[block])]
        for i, (source, target) in enumerate(pairs):
            loads[block].append(pltpu.make_async_copy(source, target, load_sem.at[block, i]))
    rate_load = pltpu.make_async_copy(rate_hbm, rate_ref, rate_sem)
    for load in [rate_load] + loads[0]:
        load.start()
    rate_load.wait()
    stores = [
        pltpu.make_async_copy(parts.at[at], outs[2 * block], store_sem.at[block])
        for block, at in enumerate(rows)
    ]
    causal = lower_triangle(size)
    for block, at in enumerate(rows):
        begin = place_ref[block] * size
        rates = rate_ref[:, pl.ds(pl.multiple_of(begin, size), size)]
        ahead = (lax.broadcasted_iota(jnp.int32, (8, tokens), 1) < begin).astype(F32)
        lead = fold_three(lax.dot_general(
            ahead.astype(BF16), split_three(rate_ref[...]), (((1,), (1,)), ((), ())),
            preferred_element_type=F32,
        ))
        running = running_sum(rates)
        running_rows = running_sum_rows(rates)
        fade = jnp.exp(running)
        outs[2 * block + 1][...] = jnp.exp(running + lead[:1])
        for load in loads[block]:
            load.wait()
        for load in loads[block + 1] if block + 1 < count else ():
            load.start()
        for head in range(heads):
            of_head = head_columns(head)
            side, slot = head // half, head % half
            kept, sent = keeps[block, slot], sends[block, slot]
            start = jnp.where(is_odd, kept, sent) if side else jnp.where(is_odd, sent, kept)
            query = queries[at, of_head]
            scores = lax.dot_general(
                query, keys[at, of_head], (((1,), (1,)), ((), ())), preferred_element_type=F32
            )
            spread = running[:, head:head + 1] - running_rows[head:head + 1, :]
            decay = jnp.exp(jnp.where(causal, spread, -1e30))
            weights = (scores * decay).astype(BF16)
            inside = jnp.dot(weights, values[at, of_head], preferred_element_type=F32)
            carried = fold_pair(jnp.dot(query, split_pair(start), preferred_element_type=F32))
            parts[at, of_head] = inside + carried * fade[:, head:head + 1]
        stores[block].start()
    for store in stores:
        store.wait()


def inside_part(place, rates, queries, key_vectors, value_vectors, starts, block_len, after):
    count = place.shape[0] - 1
    features = queries.shape[1]
    heads = features // HEAD_DIM
    vmem, far = pl.BlockSpec(memory_space=pltpu.VMEM), pl.BlockSpec(memory_space=pl.ANY)
    rows = pltpu.VMEM((count * block_len, features), BF16)
    state = pltpu.VMEM((count, heads // 2, HEAD_DIM, HEAD_DIM), F32)
    return pl.pallas_call(
        inside_kernel,
        in_specs=[pl.BlockSpec(memory_space=pltpu.SMEM)] + [far] * 7,
        out_specs=[far, vmem] * count,
        out_shape=[
            pltpu.HBM((block_len, features), F32), pltpu.HBM((block_len, heads), F32),
        ] * count,
        scratch_shapes=[pltpu.VMEM(rates.shape, F32), rows, rows, rows, state, state,
                        pltpu.VMEM((count * block_len, features), F32), pltpu.SemaphoreType.DMA,
                        pltpu.SemaphoreType.DMA((count, 5)), pltpu.SemaphoreType.DMA((count,))],
        compiler_params=params(STREAM_MIB),
        cost_estimate=SHORT,
    )(place, *in_hbm(rates, queries, key_vectors, value_vectors, *starts), after)


def row_loads(first_row, block_len, place_ref, query_hbm, gate_hbm, parts_hbm, queries, gates, parts,
              leads, sem):
    rows = queries.shape[0] // 2
    loads = []
    for which, (part_hbm, lead_hbm) in enumerate(parts_hbm):
        whole = pl.ds(pl.multiple_of(place_ref[which] * block_len + first_row, rows), rows)
        group = slice(first_row, first_row + rows)
        at = slice(which * rows, (which + 1) * rows)
        pairs = [(query_hbm.at[whole], queries.at[at]), (part_hbm.at[group], parts.at[at]),
                 (gate_hbm.at[whole], gates.at[at]), (lead_hbm.at[group], leads.at[at])]
        loads += [pltpu.make_async_copy(source, target, sem.at[which, i])
                  for i, (source, target) in enumerate(pairs)]
    return loads


def bring_kernel(first_row, block_len, place_ref, query_hbm, gate_hbm, weight_hbm, part_0, lead_0,
                 part_1, lead_1, after_ref, queries, gates, parts, leads, weight, row_sem, weight_sem):
    del after_ref
    loads = row_loads(first_row, block_len, place_ref, query_hbm, gate_hbm,
                      ((part_0, lead_0), (part_1, lead_1)), queries, gates, parts, leads, row_sem)
    loads.append(pltpu.make_async_copy(weight_hbm.at[:, :weight.shape[1]], weight, weight_sem))
    for load in loads:
        load.start()
    for load in loads:
        load.wait()


def row_shapes(rows, features):
    return [((2 * rows, features), BF16), ((2 * rows, features), BF16), ((2 * rows, features), F32),
            ((2 * rows, features // HEAD_DIM), F32)]


def bring_rows(place, rows, first_row, block_len, queries, parts, gate_input, out_weight, after):
    features, width = out_weight.shape
    shapes = row_shapes(rows, features) + [((features, width // TILE // 2 * TILE), BF16)]
    return pl.pallas_call(
        functools.partial(bring_kernel, first_row, block_len),
        in_specs=[pl.BlockSpec(memory_space=pltpu.SMEM)] + [pl.BlockSpec(memory_space=pl.ANY)] * 8,
        out_specs=[pl.BlockSpec(memory_space=pltpu.VMEM)] * len(shapes),
        out_shape=[pltpu.VMEM(*shape) for shape in shapes],
        scratch_shapes=[pltpu.SemaphoreType.DMA((2, 4)), pltpu.SemaphoreType.DMA],
        compiler_params=params(),
        cost_estimate=SHORT,
    )(place, *in_hbm(queries, gate_input, out_weight, *parts[0], *parts[1]), after)


def project_kernel(first_row, block_len, pieces, brought, place_ref, *refs):
    states, refs = refs[:2 * CHAIN_PARTS], refs[2 * CHAIN_PARTS:]
    if brought:
        queries, gates, parts, leads, early, weight_hbm, after_ref, *refs = refs
    else:
        query_hbm, gate_hbm, weight_hbm, part_0, lead_0, part_1, lead_1, after_ref, *refs = refs
    del after_ref
    outs, refs = refs[:pieces + 1], refs[pieces + 1:]
    incoming, hidden, result, weight, state_sem, out_sem, weight_sem, *refs = refs
    rows, width = outs[-1].shape
    tiles = weight_sem.shape[0]
    tile = width // tiles
    is_odd = place_ref[2] == 1
    columns = [slice(at, at + tile) for at in range(0, width, tile)]
    loads = [pltpu.make_async_copy(ref, incoming.at[i], state_sem.at[i])
             for i, ref in enumerate(states)]
    skipped = early.shape[1] if brought else 0
    weights = [
        pltpu.make_async_copy(
            weight_hbm.at[:, at], weight.at[:, at.start - skipped:at.stop - skipped], weight_sem.at[i])
        for i, at in enumerate(columns) if at.start >= skipped
    ]
    if not brought:
        queries, gates, parts, leads, row_sem = refs
        loads += row_loads(first_row, block_len, place_ref, query_hbm, gate_hbm,
                           ((part_0, lead_0), (part_1, lead_1)), queries, gates, parts, leads, row_sem)
    heads = queries.shape[1] // HEAD_DIM
    half = heads // 2
    per_part = half // CHAIN_PARTS
    for load in loads + weights[:1]:
        load.start()
    for load in loads:
        load.wait()
    for load in weights[1:]:
        load.start()
    for head in range(heads):
        at = head_columns(head)
        side, place = head // half, head % half
        part, slot = place // per_part, place % per_part
        kept, got = incoming[part, slot], incoming[CHAIN_PARTS + part, slot]
        state = jnp.where(is_odd, kept, got) if side else jnp.where(is_odd, got, kept)
        carried = fold_pair(jnp.dot(queries[:, at], split_pair(state), preferred_element_type=F32))
        attended = parts[:, at] + carried * leads[:, head:head + 1]
        mean = jnp.mean(attended * attended, axis=1, keepdims=True)
        gate = gates[:, at].astype(F32)
        normed = attended * lax.rsqrt(mean + 1e-6)
        hidden[:, at] = (normed * (gate / (1.0 + jnp.exp(-gate)))).astype(BF16)
    stores = []
    for i, at in enumerate(columns):
        if at.start < skipped:
            tile_weight = early[:, at]
        else:
            weights[i - skipped // tile].wait()
            tile_weight = weight[:, at.start - skipped:at.stop - skipped]
        result[:, at] = jnp.dot(hidden[...], tile_weight, preferred_element_type=F32)
    begin = 0
    for j, out in enumerate(outs):
        size = out.shape[0]
        store = pltpu.make_async_copy(result.at[begin:begin + size], out, out_sem.at[j])
        store.start()
        stores.append(store)
        begin += size
    for store in stores:
        store.wait()


def project_rows(place, rows, first_row, block_len, queries, parts, gate_input, kept, got,
                 out_weight, after, pieces, brought=None):
    features = queries.shape[1]
    width = out_weight.shape[1]
    tiles = max(1, width // TILE)
    sizes = [rows // pieces] * pieces + [rows]
    far, vmem = pl.BlockSpec(memory_space=pl.ANY), pl.BlockSpec(memory_space=pltpu.VMEM)
    dma = pltpu.SemaphoreType.DMA
    scratch = [
        pltpu.VMEM((2 * CHAIN_PARTS, *kept[0].shape), F32),
        pltpu.VMEM((2 * rows, features), BF16),
        pltpu.VMEM((2 * rows, width), F32),
        pltpu.VMEM((features, width if brought is None else width - brought[-1].shape[1]), BF16),
        dma((2 * CHAIN_PARTS,)), dma((len(sizes),)), dma((tiles,)),
    ]
    if brought is not None:
        operands = [pltpu.with_memory_space_constraint(value, pltpu.VMEM) for value in brought]
        specs = [vmem] * len(operands) + [far]
        operands += in_hbm(out_weight)
    else:
        operands = in_hbm(queries, gate_input, out_weight, *parts[0], *parts[1])
        specs = [far] * len(operands)
        scratch += [pltpu.VMEM(*shape) for shape in row_shapes(rows, features)]
        scratch += [dma((2, 4))]
    return pl.pallas_call(
        functools.partial(project_kernel, first_row, block_len, pieces, brought is not None),
        in_specs=[pl.BlockSpec(memory_space=pltpu.SMEM)] + [far] * 2 * CHAIN_PARTS + specs + [far],
        out_specs=[far] * len(sizes),
        out_shape=[jax.ShapeDtypeStruct((size, width), F32) for size in sizes],
        scratch_shapes=scratch,
        compiler_params=params(),
        cost_estimate=SHORT,
    )(place, *kept, *got, *operands, after)


def add_kernel(own_ref, *refs):
    pieces, out_ref = refs[:-2], refs[-1]
    at = 0
    for ref in pieces:
        size = ref.shape[0]
        out_ref[at:at + size] = own_ref[at:at + size] + ref[...]
        at += size


def add_pieces(own, pieces, after):
    whole = pl.BlockSpec(own.shape, lambda: (0, 0))
    return pl.pallas_call(
        add_kernel,
        in_specs=[whole] + [pl.BlockSpec(piece.shape, lambda: (0, 0)) for piece in pieces]
        + [pl.BlockSpec(memory_space=pl.ANY)],
        out_specs=whole,
        out_shape=jax.ShapeDtypeStruct(own.shape, F32),
        compiler_params=params(),
        cost_estimate=SHORT,
    )(own, *pieces, after)


def finish_kernel(arrivals, own_ref, *refs):
    out_ref = refs[-1]
    arrived, pieces = refs[:arrivals], refs[arrivals:-2]
    at = 0
    for ref in pieces:
        size = ref.shape[0]
        total = own_ref[at:at + size] + ref[...]
        for other in arrived:
            total = total + other[at:at + size]
        out_ref[at:at + size] = total.astype(out_ref.dtype)
        at += size


def finish_rows(group, arrived, own, own_group, pieces, result, block_len):
    rows, width = arrived[0].shape
    whole = pl.BlockSpec((rows, width), lambda i: (0, 0))
    alias = {}
    if result is None:
        result = own
    else:
        alias = {1 + len(arrived) + len(pieces): 0}
    return pl.pallas_call(
        functools.partial(finish_kernel, len(arrived)),
        grid=(1,),
        in_specs=[pl.BlockSpec((rows, width), lambda i: (own_group, 0))] + [whole] * len(arrived)
        + [pl.BlockSpec(piece.shape, lambda i: (0, 0)) for piece in pieces]
        + [pl.BlockSpec(memory_space=pl.ANY)],
        out_specs=pl.BlockSpec((rows, width), lambda i: (group, 0)),
        out_shape=jax.ShapeDtypeStruct((block_len, width), BF16),
        input_output_aliases=alias,
        compiler_params=params(),
        cost_estimate=SHORT,
    )(own, *arrived, *pieces, result)


def hop_kernel(hops, odd_ref, *refs):
    landed, (kept_ref, got_ref, after_ref, value_ref) = refs[:hops], refs[hops:]
    del after_ref
    is_odd = odd_ref[0] == 1
    for slot in range(value_ref.shape[0]):
        kept, got = kept_ref[slot], got_ref[slot]
        early, late = jnp.where(is_odd, got, kept), jnp.where(is_odd, kept, got)
        late_decay = late[HEAD_DIM:HEAD_DIM + 1]
        value = early[:HEAD_DIM]
        if landed:
            before = landed[0][slot]
            for ref in landed[1:]:
                before = before + ref[slot]
            value = early[HEAD_DIM:HEAD_DIM + 1] * before + value
        value_ref[slot] = late_decay * value + late[:HEAD_DIM]


def hop_states(odd, landed, kept, got, after):
    vmem = pl.BlockSpec(memory_space=pltpu.VMEM)
    return pl.pallas_call(
        functools.partial(hop_kernel, len(landed)),
        in_specs=[pl.BlockSpec(memory_space=pltpu.SMEM)] + [vmem] * (len(landed) + 2)
        + [pl.BlockSpec(memory_space=pl.ANY)],
        out_specs=vmem,
        out_shape=jax.ShapeDtypeStruct((kept.shape[0], HEAD_DIM, HEAD_DIM), F32),
        compiler_params=params(),
        cost_estimate=SHORT,
    )(odd, *landed, kept, got, *in_hbm(after))


def entering_kernel(hops, odd_ref, *refs):
    landed, (kept_ref, got_ref, after_ref, keep_ref, back_ref) = refs[:hops], refs[hops:]
    del after_ref
    is_odd = odd_ref[0] == 1
    for slot in range(keep_ref.shape[0]):
        before = landed[0][slot]
        for ref in landed[1:]:
            before = before + ref[slot]
        first = jnp.where(is_odd, got_ref[slot], kept_ref[slot])
        after = first[HEAD_DIM:HEAD_DIM + 1] * before + first[:HEAD_DIM]
        keep_ref[slot] = jnp.where(is_odd, after, before)
        back_ref[slot] = jnp.where(is_odd, before, after)


def entering_states(odd, landed, kept, got, after):
    shape = jax.ShapeDtypeStruct(landed[0].shape, F32)
    vmem = pl.BlockSpec(memory_space=pltpu.VMEM)
    return pl.pallas_call(
        functools.partial(entering_kernel, len(landed)),
        in_specs=[pl.BlockSpec(memory_space=pltpu.SMEM)] + [vmem] * (len(landed) + 2)
        + [pl.BlockSpec(memory_space=pl.ANY)],
        out_specs=[vmem, vmem],
        out_shape=[shape, shape],
        compiler_params=params(),
        cost_estimate=SHORT,
    )(odd, *landed, kept, got, *in_hbm(after))


def incoming_states(odd, kept, got, after, meanwhile):
    count = lax.axis_size("seq")
    swap = [(i, i ^ 1) for i in range(count)]
    parts = range(CHAIN_PARTS)
    landed = [[] for _ in parts]
    for hop in range(count // 2 - 1):
        along = [(2 * hop, 2 * hop + 2), (2 * hop + 1, 2 * hop + 3)]
        for i in parts:
            value = hop_states(odd, landed[i], kept[i], got[i], after)
            landed[i].append(lax.ppermute(value, "seq", along))
        if hop == count // 2 - 3:
            for work in meanwhile:
                after = work(value)
    keep, back = [], []
    for i in parts:
        mine, other = entering_states(odd, landed[i], kept[i], got[i], after)
        keep.append(mine)
        back.append(lax.ppermute(other, "seq", swap))
    return keep, back


def per_device(queries, key_vectors, value_vectors, gate_input, log_decay, out_weight):
    tokens = queries.shape[0]
    count = lax.axis_size("head")
    chips = count // 2
    block_len = tokens // count
    sizes = [block_len // share for share in ROW_SHARES]
    firsts = [sum(sizes[:i]) for i in range(len(sizes))]
    index = lax.axis_index("head")
    chip, core = index // 2, index % 2
    place_in_seq = lax.axis_index("seq")
    odd = (place_in_seq % 2).reshape(1).astype(jnp.int32)
    rates = log_decay.T
    swap = [(i, i ^ 1) for i in range(lax.axis_size("seq"))]

    sent, sent_starts = local_states(1 - odd, rates, key_vectors, value_vectors, block_len)
    met = [lax.ppermute(piece, "seq", swap) for piece in sent]
    kept, kept_starts = local_states(odd, rates, key_vectors, value_vectors, block_len)

    def place_of(target):
        return jnp.stack([2 * target + 1 - core, 2 * target + core, odd[0]]).astype(jnp.int32)

    def parts_of(target, after):
        outs = inside_part(place_of(target), rates, queries, key_vectors, value_vectors,
                           (kept_starts, sent_starts), block_len, after)
        return outs[:2], outs[2:]

    def project(target, parts, group, after, pieces, brought=None):
        *theirs, mine = project_rows(
            place_of(target), sizes[group], firsts[group], block_len, queries, parts, gate_input, keep,
            got, out_weight, after, pieces, brought)
        return mine, [lax.ppermute(piece, "head", cores) for piece in theirs]

    cores = [(i, i ^ 1) for i in range(count)]
    targets = [(chip + step) % chips for step in range(1, chips)]
    parts = []

    def inside_of(target, after):
        parts.append(parts_of(target, after))
        return parts[-1][1][1]

    keep, got = incoming_states(
        odd, kept, met, kept_starts, [functools.partial(inside_of, target) for target in targets])
    last = keep[-1]
    brought = bring_rows(place_of(targets[0]), sizes[0], firsts[0], block_len, queries, parts[0],
                         gate_input, out_weight, last)
    landed, own, result = [last, last], [], None
    arrived = [[] for _ in sizes]
    for group in range(len(sizes)):
        for step, target in enumerate(targets):
            across = [(i, ((i // 2 + step + 1) % chips) * 2 + i % 2) for i in range(count)]
            mine, pieces = project(target, parts[step], group, last, CORE_PIECES, brought)
            brought = None
            last = add_pieces(mine, pieces, landed[-DEPTH])
            landed.append(lax.ppermute(last, "head", across))
            arrived[group].append(landed[-1])
    own_parts = parts_of(chip, last)
    groups = list(zip(firsts, sizes))
    own_rows, piece = block_len // OWN_GROUPS, block_len // 8
    sizes = [own_rows] * OWN_GROUPS
    firsts = [own_rows * i for i in range(OWN_GROUPS)]
    for group in range(len(sizes)):
        if group == len(sizes) - 1:
            last = landed[-2]
        own.append(project(chip, own_parts, group, last, own_rows // piece))
        last = own[-1][0]
    for group, (first, size) in enumerate(groups):
        mine, pieces = own[first // own_rows]
        at = first % own_rows
        result = finish_rows(first // size, arrived[group], mine, at // size,
                             pieces[at // piece:(at + size) // piece], result, block_len)
    return result


def solution(mesh):
    placed = (
        P("seq", "head"),
        P("seq", "head"),
        P("seq", "head"),
        P("seq", "head"),
        P("seq", "head"),
        P("head", None),
    )
    return jax.shard_map(
        per_device, mesh=mesh, in_specs=placed, out_specs=P(("seq", "head"), None), check_vma=False
    )
```

```python
import functools

import jax
import jax.numpy as jnp
from jax import lax
from jax.experimental import pallas as pl
from jax.experimental.pallas import tpu as pltpu
from jax.sharding import PartitionSpec as P

HEAD_DIM = 128
MIB = 1024 * 1024
ROW_SHARES = (4, 4, 4, 4)
OWN_GROUPS = 2
EARLY_GROUPS = 3
CHAIN_PARTS = 2
CORE_PIECES = 4
DEPTH = 2
TILE = 1024
STREAM_MIB = 32
KERNEL_MIB = 32
SHORT = pl.CostEstimate(flops=1, bytes_accessed=1, transcendentals=0)
F32 = jnp.float32
BF16 = jnp.bfloat16


def head_columns(head):
    return slice(head * HEAD_DIM, (head + 1) * HEAD_DIM)


def split_pair(value):
    high = value.astype(BF16)
    low = (value - high.astype(F32)).astype(BF16)
    return jnp.concatenate([high, low], axis=1)


def split_rows(value):
    high = value.astype(BF16)
    low = (value - high.astype(F32)).astype(BF16)
    return jnp.concatenate([high, low], axis=0)


def fold_pair(value):
    return value[:, :HEAD_DIM] + value[:, HEAD_DIM:]


def lower_triangle(size):
    rows = lax.broadcasted_iota(jnp.int32, (size, size), 0)
    columns = lax.broadcasted_iota(jnp.int32, (size, size), 1)
    return rows >= columns


def split_three(value):
    high = value.astype(BF16).astype(F32)
    rest = value - high
    middle = rest.astype(BF16).astype(F32)
    return jnp.concatenate([high, middle, rest - middle], axis=0).astype(BF16)


def running_sum(rates):
    ones = lower_triangle(rates.shape[1]).astype(F32).astype(BF16)
    count = rates.shape[0]
    value = lax.dot_general(
        split_three(rates), ones, (((1,), (1,)), ((), ())), preferred_element_type=F32
    )
    return value[:count] + value[count:2 * count] + value[2 * count:]


def in_hbm(*arrays):
    return [pltpu.with_memory_space_constraint(array, pltpu.HBM) for array in arrays]


def params(mib=KERNEL_MIB):
    return pltpu.CompilerParams(vmem_limit_bytes=mib * MIB)


def states_kernel(half_done, side_ref, rate_hbm, key_hbm, value_hbm, *refs):
    if half_done:
        other, *refs = refs
    message_refs, refs = refs[:CHAIN_PARTS], refs[CHAIN_PARTS:]
    if half_done:
        start_hbm, other_hbm, rate_ref, keys, values, rate_sem, key_sem, value_sem, starts, start_sem = refs
        stores = [pltpu.make_async_copy(starts, start_hbm, start_sem.at[0]),
                  pltpu.make_async_copy(other, other_hbm, start_sem.at[1])]
    else:
        starts, rate_ref, keys, values, rate_sem, key_sem, value_sem = refs
    blocks, half = starts.shape[:2]
    width = keys.shape[1]
    size = keys.shape[0] // blocks
    per_part = half // CHAIN_PARTS
    columns = pl.ds(pl.multiple_of(side_ref[0] * width, width), width)
    rows = [slice(block * size, (block + 1) * size) for block in range(blocks)]
    loads = [
        (pltpu.make_async_copy(key_hbm.at[at, columns], keys.at[at], key_sem.at[block]),
         pltpu.make_async_copy(value_hbm.at[at, columns], values.at[at], value_sem.at[block]))
        for block, at in enumerate(rows)
    ]
    rate_load = pltpu.make_async_copy(rate_hbm, rate_ref, rate_sem)
    rate_load.start()
    for load in [load for pair in loads[:2] for load in pair]:
        load.start()
    starts[0] = jnp.zeros_like(starts[0])
    rate_load.wait()
    rates = jnp.where(side_ref[0] == 1, rate_ref[half:, :], rate_ref[:half, :])
    lead = jnp.zeros((half, 1), F32)
    for block, at in enumerate(rows):
        running = running_sum(rates[:, at])
        total = running[:, -1:]
        fade = jnp.exp(total - running)
        block_decay = jnp.exp(total)
        lead = lead + total
        for load in loads[block]:
            load.wait()
        for load in loads[block + 2] if block + 2 < blocks else ():
            load.start()
        if half_done and block == 0:
            stores[1].start()
        for head in range(half):
            of_head = head_columns(head)
            scaled = keys[at, of_head].T.astype(F32) * fade[head:head + 1]
            gained = jnp.dot(split_rows(scaled), values[at, of_head], preferred_element_type=F32)
            gained = gained[:HEAD_DIM] + gained[HEAD_DIM:]
            state = block_decay[head:head + 1] * starts[block, head] + gained
            if block + 1 < blocks:
                starts[block + 1, head] = state
            else:
                message_refs[head // per_part][head % per_part, :HEAD_DIM] = state
    if half_done:
        stores[0].start()
    through = jnp.exp(lead)
    for head in range(half):
        message_refs[head // per_part][head % per_part, HEAD_DIM:] = jnp.broadcast_to(
            through[head:head + 1], (8, HEAD_DIM))
    if half_done:
        for store in stores:
            store.wait()


def local_states(side, rates, key_vectors, value_vectors, block_len, other=None):
    tokens, features = key_vectors.shape
    half = features // HEAD_DIM // 2
    blocks = tokens // block_len
    message = jax.ShapeDtypeStruct((half // CHAIN_PARTS, HEAD_DIM + 8, HEAD_DIM), F32)
    starts = ((blocks, half, HEAD_DIM, HEAD_DIM), F32)
    vmem, far = pl.BlockSpec(memory_space=pltpu.VMEM), pl.BlockSpec(memory_space=pl.ANY)
    dma = pltpu.SemaphoreType.DMA
    rows = pltpu.VMEM((tokens, features // 2), BF16)
    scratch = [pltpu.VMEM(rates.shape, F32), rows, rows, dma, dma((blocks,)), dma((blocks,))]
    if other is None:
        others, start_specs, start_shapes = [], [vmem], [jax.ShapeDtypeStruct(*starts)]
    else:
        others, start_specs, start_shapes = [other], [far] * 2, [pltpu.HBM(*starts)] * 2
        scratch += [pltpu.VMEM(*starts), dma((2,))]
    outs = pl.pallas_call(
        functools.partial(states_kernel, other is not None),
        in_specs=[pl.BlockSpec(memory_space=pltpu.SMEM), far, far, far] + [far] * len(others),
        out_specs=[vmem] * CHAIN_PARTS + start_specs,
        out_shape=[message] * CHAIN_PARTS + start_shapes,
        scratch_shapes=scratch,
        compiler_params=params(STREAM_MIB),
        cost_estimate=SHORT,
    )(side, *in_hbm(rates, key_vectors, value_vectors), *others)
    return outs[:CHAIN_PARTS], outs[CHAIN_PARTS:]


def inside_kernel(begin, end, place_ref, rate_hbm, query_hbm, key_hbm, value_hbm, keep_hbm, send_hbm,
                  after_ref, *refs):
    del after_ref
    rate_ref, queries, keys, values, keeps, sends, parts, rate_sem, load_sem, store_sem = refs[-10:]
    outs = refs[:-10]
    heads, tokens = rate_ref.shape
    count, half = keeps.shape[:2]
    size = tokens // keep_hbm.shape[0]
    is_odd = place_ref[count] == 1
    loads = []
    for block in range(count):
        place = place_ref[block]
        far = pl.ds(pl.multiple_of(place * size + begin, 16), end - begin)
        until = pl.ds(pl.multiple_of(place * size, size), end)
        pairs = [(query_hbm.at[far], queries), (key_hbm.at[until], keys), (value_hbm.at[until], values),
                 (keep_hbm.at[place], keeps), (send_hbm.at[place], sends)]
        loads.append([pltpu.make_async_copy(source, target.at[block], load_sem.at[block, i])
                      for i, (source, target) in enumerate(pairs)])
    rate_load = pltpu.make_async_copy(rate_hbm, rate_ref, rate_sem)
    for load in [rate_load] + loads[0]:
        load.start()
    rate_load.wait()
    stores = [
        pltpu.make_async_copy(parts.at[block], outs[2 * block], store_sem.at[block])
        for block in range(count)
    ]
    causal = lower_triangle(size)[begin:end, :end]
    for block in range(count):
        first = place_ref[block] * size
        rates = rate_ref[:, pl.ds(pl.multiple_of(first, size), size)]
        ahead = lax.broadcasted_iota(jnp.int32, (heads, tokens), 1) < first
        lead = jnp.sum(jnp.where(ahead, rate_ref[...], 0.0), axis=1, keepdims=True)
        running_rows = running_sum(rates)
        running = running_rows.T[begin:end]
        fade = jnp.exp(running)
        outs[2 * block + 1][...] = jnp.exp(running_rows + lead).T[begin:end]
        running_rows = running_rows[:, :end]
        for load in loads[block]:
            load.wait()
        for load in loads[block + 1] if block + 1 < count else ():
            load.start()
        for head in range(heads):
            of_head = head_columns(head)
            side, slot = head // half, head % half
            kept, sent = keeps[block, slot], sends[block, slot]
            start = jnp.where(is_odd, kept, sent) if side else jnp.where(is_odd, sent, kept)
            query = queries[block, :, of_head]
            scores = lax.dot_general(
                query, keys[block, :, of_head], (((1,), (1,)), ((), ())), preferred_element_type=F32
            )
            spread = running[:, head:head + 1] - running_rows[head:head + 1, :]
            decay = jnp.exp(jnp.where(causal, spread, -1e30))
            weights = (scores * decay).astype(BF16)
            inside = jnp.dot(weights, values[block, :, of_head], preferred_element_type=F32)
            carried = fold_pair(jnp.dot(query, split_pair(start), preferred_element_type=F32))
            parts[block, :, of_head] = inside + carried * fade[:, head:head + 1]
        stores[block].start()
    for store in stores:
        store.wait()


def inside_part(place, begin, end, rates, queries, key_vectors, value_vectors, starts, block_len, after):
    count = place.shape[0] - 1
    features = queries.shape[1]
    heads = features // HEAD_DIM
    rows = end - begin
    vmem, far = pl.BlockSpec(memory_space=pltpu.VMEM), pl.BlockSpec(memory_space=pl.ANY)
    keys = pltpu.VMEM((count, end, features), BF16)
    state = pltpu.VMEM((count, heads // 2, HEAD_DIM, HEAD_DIM), F32)
    return pl.pallas_call(
        functools.partial(inside_kernel, begin, end),
        in_specs=[pl.BlockSpec(memory_space=pltpu.SMEM)] + [far] * 7,
        out_specs=[far, vmem] * count,
        out_shape=[pltpu.HBM((rows, features), F32), pltpu.HBM((rows, heads), F32)] * count,
        scratch_shapes=[pltpu.VMEM(rates.shape, F32), pltpu.VMEM((count, rows, features), BF16), keys, keys,
                        state, state, pltpu.VMEM((count, rows, features), F32),
                        pltpu.SemaphoreType.DMA, pltpu.SemaphoreType.DMA((count, 5)),
                        pltpu.SemaphoreType.DMA((count,))],
        compiler_params=params(STREAM_MIB),
        cost_estimate=SHORT,
    )(place, *in_hbm(rates, queries, key_vectors, value_vectors, *starts), after)


def row_loads(first_row, part_row, block_len, place_ref, query_hbm, gate_hbm, parts_hbm, queries, gates, parts,
              leads, sem):
    rows = queries.shape[0] // 2
    loads = []
    for which, (part_hbm, lead_hbm) in enumerate(parts_hbm):
        whole = pl.ds(pl.multiple_of(place_ref[which] * block_len + first_row, rows), rows)
        group = slice(part_row, part_row + rows)
        at = slice(which * rows, (which + 1) * rows)
        pairs = [(query_hbm.at[whole], queries.at[at]), (part_hbm.at[group], parts.at[at]),
                 (gate_hbm.at[whole], gates.at[at]), (lead_hbm.at[group], leads.at[at])]
        loads += [pltpu.make_async_copy(source, target, sem.at[which, i])
                  for i, (source, target) in enumerate(pairs)]
    return loads


def bring_kernel(first_row, part_row, block_len, place_ref, query_hbm, gate_hbm, weight_hbm, part_0, lead_0,
                 part_1, lead_1, after_ref, queries, gates, parts, leads, weight, row_sem, weight_sem):
    del after_ref
    loads = row_loads(first_row, part_row, block_len, place_ref, query_hbm, gate_hbm,
                      ((part_0, lead_0), (part_1, lead_1)), queries, gates, parts, leads, row_sem)
    loads.append(pltpu.make_async_copy(weight_hbm.at[:, :weight.shape[1]], weight, weight_sem))
    for load in loads:
        load.start()
    for load in loads:
        load.wait()


def row_shapes(rows, features):
    return [((2 * rows, features), BF16), ((2 * rows, features), BF16), ((2 * rows, features), F32),
            ((2 * rows, features // HEAD_DIM), F32)]


def bring_rows(place, rows, first_row, part_row, block_len, queries, parts, gate_input, out_weight, after):
    features, width = out_weight.shape
    shapes = row_shapes(rows, features) + [((features, width // TILE // 2 * TILE), BF16)]
    return pl.pallas_call(
        functools.partial(bring_kernel, first_row, part_row, block_len),
        in_specs=[pl.BlockSpec(memory_space=pltpu.SMEM)] + [pl.BlockSpec(memory_space=pl.ANY)] * 8,
        out_specs=[pl.BlockSpec(memory_space=pltpu.VMEM)] * len(shapes),
        out_shape=[pltpu.VMEM(*shape) for shape in shapes],
        scratch_shapes=[pltpu.SemaphoreType.DMA((2, 4)), pltpu.SemaphoreType.DMA],
        compiler_params=params(),
        cost_estimate=SHORT,
    )(place, *in_hbm(queries, gate_input, out_weight, *parts[0], *parts[1]), after)


def project_kernel(first_row, part_row, block_len, pieces, brought, place_ref, *refs):
    states, refs = refs[:2 * CHAIN_PARTS], refs[2 * CHAIN_PARTS:]
    if brought:
        queries, gates, parts, leads, early, weight_hbm, after_ref, *refs = refs
    else:
        query_hbm, gate_hbm, weight_hbm, part_0, lead_0, part_1, lead_1, after_ref, *refs = refs
    del after_ref
    outs, refs = refs[:pieces + 1], refs[pieces + 1:]
    incoming, hidden, result, weight, state_sem, out_sem, weight_sem, *refs = refs
    rows, width = outs[-1].shape
    tiles = weight_sem.shape[0]
    tile = width // tiles
    is_odd = place_ref[2] == 1
    columns = [slice(at, at + tile) for at in range(0, width, tile)]
    loads = [pltpu.make_async_copy(ref, incoming.at[i], state_sem.at[i])
             for i, ref in enumerate(states)]
    skipped = early.shape[1] if brought else 0
    weights = [
        pltpu.make_async_copy(
            weight_hbm.at[:, at], weight.at[:, at.start - skipped:at.stop - skipped], weight_sem.at[i])
        for i, at in enumerate(columns) if at.start >= skipped
    ]
    if not brought:
        queries, gates, parts, leads, row_sem = refs
        loads += row_loads(first_row, part_row, block_len, place_ref, query_hbm, gate_hbm,
                           ((part_0, lead_0), (part_1, lead_1)), queries, gates, parts, leads, row_sem)
    heads = queries.shape[1] // HEAD_DIM
    half = heads // 2
    per_part = half // CHAIN_PARTS
    for load in loads + weights[:1]:
        load.start()
    for load in loads:
        load.wait()
    for load in weights[1:]:
        load.start()
    for head in range(heads):
        at = head_columns(head)
        side, place = head // half, head % half
        part, slot = place // per_part, place % per_part
        kept, got = incoming[part, slot], incoming[CHAIN_PARTS + part, slot]
        state = jnp.where(is_odd, kept, got) if side else jnp.where(is_odd, got, kept)
        carried = fold_pair(jnp.dot(queries[:, at], split_pair(state), preferred_element_type=F32))
        attended = parts[:, at] + carried * leads[:, head:head + 1]
        mean = jnp.mean(attended * attended, axis=1, keepdims=True)
        gate = gates[:, at].astype(F32)
        normed = attended * lax.rsqrt(mean + 1e-6)
        hidden[:, at] = (normed * (gate / (1.0 + jnp.exp(-gate)))).astype(BF16)
    stores = []
    for i, at in enumerate(columns):
        if at.start < skipped:
            tile_weight = early[:, at]
        else:
            weights[i - skipped // tile].wait()
            tile_weight = weight[:, at.start - skipped:at.stop - skipped]
        result[:, at] = jnp.dot(hidden[...], tile_weight, preferred_element_type=F32)
    begin = 0
    for j, out in enumerate(outs):
        size = out.shape[0]
        store = pltpu.make_async_copy(result.at[begin:begin + size], out, out_sem.at[j])
        store.start()
        stores.append(store)
        begin += size
    for store in stores:
        store.wait()


def project_rows(place, rows, first_row, part_row, block_len, queries, parts, gate_input, kept, got,
                 out_weight, after, pieces, brought=None):
    features = queries.shape[1]
    width = out_weight.shape[1]
    tiles = max(1, width // TILE)
    sizes = [rows // pieces] * pieces + [rows]
    far, vmem = pl.BlockSpec(memory_space=pl.ANY), pl.BlockSpec(memory_space=pltpu.VMEM)
    dma = pltpu.SemaphoreType.DMA
    scratch = [
        pltpu.VMEM((2 * CHAIN_PARTS, *kept[0].shape), F32),
        pltpu.VMEM((2 * rows, features), BF16),
        pltpu.VMEM((2 * rows, width), F32),
        pltpu.VMEM((features, width if brought is None else width - brought[-1].shape[1]), BF16),
        dma((2 * CHAIN_PARTS,)), dma((len(sizes),)), dma((tiles,)),
    ]
    if brought is not None:
        operands = [pltpu.with_memory_space_constraint(value, pltpu.VMEM) for value in brought]
        specs = [vmem] * len(operands) + [far]
        operands += in_hbm(out_weight)
    else:
        operands = in_hbm(queries, gate_input, out_weight, *parts[0], *parts[1])
        specs = [far] * len(operands)
        scratch += [pltpu.VMEM(*shape) for shape in row_shapes(rows, features)]
        scratch += [dma((2, 4))]
    return pl.pallas_call(
        functools.partial(project_kernel, first_row, part_row, block_len, pieces, brought is not None),
        in_specs=[pl.BlockSpec(memory_space=pltpu.SMEM)] + [far] * 2 * CHAIN_PARTS + specs + [far],
        out_specs=[far] * len(sizes),
        out_shape=[jax.ShapeDtypeStruct((size, width), F32) for size in sizes],
        scratch_shapes=scratch,
        compiler_params=params(),
        cost_estimate=SHORT,
    )(place, *kept, *got, *operands, after)


def add_kernel(own_ref, *refs):
    pieces, out_ref = refs[:-2], refs[-1]
    at = 0
    for ref in pieces:
        size = ref.shape[0]
        out_ref[at:at + size] = own_ref[at:at + size] + ref[...]
        at += size


def add_pieces(own, pieces, after):
    whole = pl.BlockSpec(own.shape, lambda: (0, 0))
    return pl.pallas_call(
        add_kernel,
        in_specs=[whole] + [pl.BlockSpec(piece.shape, lambda: (0, 0)) for piece in pieces]
        + [pl.BlockSpec(memory_space=pl.ANY)],
        out_specs=whole,
        out_shape=jax.ShapeDtypeStruct(own.shape, F32),
        compiler_params=params(),
        cost_estimate=SHORT,
    )(own, *pieces, after)


def finish_kernel(arrivals, own_ref, *refs):
    out_ref = refs[-1]
    arrived, pieces = refs[:arrivals], refs[arrivals:-2]
    at = 0
    for ref in pieces:
        size = ref.shape[0]
        total = own_ref[at:at + size] + ref[...]
        for other in arrived:
            total = total + other[at:at + size]
        out_ref[at:at + size] = total.astype(out_ref.dtype)
        at += size


def finish_rows(group, arrived, own, own_group, pieces, result, block_len):
    rows, width = arrived[0].shape
    whole = pl.BlockSpec((rows, width), lambda i: (0, 0))
    alias = {}
    if result is None:
        result = own
    else:
        alias = {1 + len(arrived) + len(pieces): 0}
    return pl.pallas_call(
        functools.partial(finish_kernel, len(arrived)),
        grid=(1,),
        in_specs=[pl.BlockSpec((rows, width), lambda i: (own_group, 0))] + [whole] * len(arrived)
        + [pl.BlockSpec(piece.shape, lambda i: (0, 0)) for piece in pieces]
        + [pl.BlockSpec(memory_space=pl.ANY)],
        out_specs=pl.BlockSpec((rows, width), lambda i: (group, 0)),
        out_shape=jax.ShapeDtypeStruct((block_len, width), BF16),
        input_output_aliases=alias,
        compiler_params=params(),
        cost_estimate=SHORT,
    )(own, *arrived, *pieces, result)


def hop_kernel(hops, odd_ref, *refs):
    landed, (kept_ref, got_ref, after_ref, value_ref) = refs[:hops], refs[hops:]
    del after_ref
    is_odd = odd_ref[0] == 1
    for slot in range(value_ref.shape[0]):
        kept, got = kept_ref[slot], got_ref[slot]
        early, late = jnp.where(is_odd, got, kept), jnp.where(is_odd, kept, got)
        late_decay = late[HEAD_DIM:HEAD_DIM + 1]
        value = early[:HEAD_DIM]
        if landed:
            before = landed[0][slot]
            for ref in landed[1:]:
                before = before + ref[slot]
            value = early[HEAD_DIM:HEAD_DIM + 1] * before + value
        value_ref[slot] = late_decay * value + late[:HEAD_DIM]


def hop_states(odd, landed, kept, got, after):
    vmem = pl.BlockSpec(memory_space=pltpu.VMEM)
    return pl.pallas_call(
        functools.partial(hop_kernel, len(landed)),
        in_specs=[pl.BlockSpec(memory_space=pltpu.SMEM)] + [vmem] * (len(landed) + 2)
        + [pl.BlockSpec(memory_space=pl.ANY)],
        out_specs=vmem,
        out_shape=jax.ShapeDtypeStruct((kept.shape[0], HEAD_DIM, HEAD_DIM), F32),
        compiler_params=params(),
        cost_estimate=SHORT,
    )(odd, *landed, kept, got, *in_hbm(after))


def entering_kernel(hops, odd_ref, *refs):
    landed, (kept_ref, got_ref, after_ref, keep_ref, back_ref) = refs[:hops], refs[hops:]
    del after_ref
    is_odd = odd_ref[0] == 1
    for slot in range(keep_ref.shape[0]):
        before = landed[0][slot]
        for ref in landed[1:]:
            before = before + ref[slot]
        first = jnp.where(is_odd, got_ref[slot], kept_ref[slot])
        after = first[HEAD_DIM:HEAD_DIM + 1] * before + first[:HEAD_DIM]
        keep_ref[slot] = jnp.where(is_odd, after, before)
        back_ref[slot] = jnp.where(is_odd, before, after)


def entering_states(odd, landed, kept, got, after):
    shape = jax.ShapeDtypeStruct(landed[0].shape, F32)
    vmem = pl.BlockSpec(memory_space=pltpu.VMEM)
    return pl.pallas_call(
        functools.partial(entering_kernel, len(landed)),
        in_specs=[pl.BlockSpec(memory_space=pltpu.SMEM)] + [vmem] * (len(landed) + 2)
        + [pl.BlockSpec(memory_space=pl.ANY)],
        out_specs=[vmem, vmem],
        out_shape=[shape, shape],
        compiler_params=params(),
        cost_estimate=SHORT,
    )(odd, *landed, kept, got, *in_hbm(after))


def incoming_states(odd, kept, got, after, meanwhile):
    count = lax.axis_size("seq")
    swap = [(i, i ^ 1) for i in range(count)]
    parts = range(CHAIN_PARTS)
    landed = [[] for _ in parts]
    for hop in range(count // 2 - 1):
        along = [(2 * hop, 2 * hop + 2), (2 * hop + 1, 2 * hop + 3)]
        for i in parts:
            value = hop_states(odd, landed[i], kept[i], got[i], after)
            landed[i].append(lax.ppermute(value, "seq", along))
        if hop == count // 2 - 3:
            for work in meanwhile:
                after = work(value)
    keep, back = [], []
    for i in parts:
        mine, other = entering_states(odd, landed[i], kept[i], got[i], after)
        keep.append(mine)
        back.append(lax.ppermute(other, "seq", swap))
    return keep, back


def per_device(queries, key_vectors, value_vectors, gate_input, log_decay, out_weight):
    tokens = queries.shape[0]
    count = lax.axis_size("head")
    chips = count // 2
    block_len = tokens // count
    sizes = [block_len // share for share in ROW_SHARES]
    firsts = [sum(sizes[:i]) for i in range(len(sizes))]
    index = lax.axis_index("head")
    chip, core = index // 2, index % 2
    place_in_seq = lax.axis_index("seq")
    odd = (place_in_seq % 2).reshape(1).astype(jnp.int32)
    rates = log_decay.T
    swap = [(i, i ^ 1) for i in range(lax.axis_size("seq"))]

    sent, (sent_starts,) = local_states(1 - odd, rates, key_vectors, value_vectors, block_len)
    met = [lax.ppermute(piece, "seq", swap) for piece in sent]
    kept, starts = local_states(odd, rates, key_vectors, value_vectors, block_len, sent_starts)

    def place_of(target):
        return jnp.stack([2 * target + 1 - core, 2 * target + core, odd[0]]).astype(jnp.int32)

    def parts_of(target, begin, end, after):
        outs = inside_part(place_of(target), begin, end, rates, queries, key_vectors, value_vectors,
                           starts, block_len, after)
        return outs[:2], outs[2:]

    def project(target, parts, part_begin, group, after, pieces, brought=None):
        first = firsts[group]
        *theirs, mine = project_rows(
            place_of(target), sizes[group], first, first - part_begin, block_len, queries, parts, gate_input, keep,
            got, out_weight, after, pieces, brought)
        return mine, [lax.ppermute(piece, "head", cores) for piece in theirs]

    cores = [(i, i ^ 1) for i in range(count)]
    targets = [(chip + step) % chips for step in range(1, chips)]
    parts = []

    def inside_of(target, after):
        parts.append(parts_of(target, 0, firsts[EARLY_GROUPS], after))
        return parts[-1][1][1]

    keep, got = incoming_states(
        odd, kept, met, starts[0], [functools.partial(inside_of, target) for target in targets])
    last = keep[-1]
    brought = bring_rows(place_of(targets[0]), sizes[0], 0, 0, block_len, queries, parts[0],
                         gate_input, out_weight, last)
    landed, own, result = [last, last], [], None
    arrived = [[] for _ in sizes]
    for group in range(len(sizes)):
        for step, target in enumerate(targets):
            across = [(i, ((i // 2 + step + 1) % chips) * 2 + i % 2) for i in range(count)]
            mine, pieces = project(
                target, parts[step], firsts[EARLY_GROUPS] if group >= EARLY_GROUPS else 0, group, last, CORE_PIECES, brought)
            brought = None
            last = add_pieces(mine, pieces, landed[-DEPTH])
            landed.append(lax.ppermute(last, "head", across))
            arrived[group].append(landed[-1])
        if group == EARLY_GROUPS - 1:
            parts = [parts_of(target, firsts[EARLY_GROUPS], block_len, last) for target in targets]
    own_parts = parts_of(chip, 0, block_len, last)
    groups = list(zip(firsts, sizes))
    own_rows, piece = block_len // OWN_GROUPS, block_len // 8
    sizes = [own_rows] * OWN_GROUPS
    firsts = [own_rows * i for i in range(OWN_GROUPS)]
    for group in range(len(sizes)):
        if group == len(sizes) - 1:
            last = landed[-2]
        own.append(project(chip, own_parts, 0, group, last, own_rows // piece))
        last = own[-1][0]
    for group, (first, size) in enumerate(groups):
        mine, pieces = own[first // own_rows]
        at = first % own_rows
        result = finish_rows(first // size, arrived[group], mine, at // size,
                             pieces[at // piece:(at + size) // piece], result, block_len)
    return result


def solution(mesh):
    placed = (
        P("seq", "head"),
        P("seq", "head"),
        P("seq", "head"),
        P("seq", "head"),
        P("seq", "head"),
        P("head", None),
    )
    return jax.shard_map(
        per_device, mesh=mesh, in_specs=placed, out_specs=P(("seq", "head"), None), check_vma=False
    )
```

```python
import functools

import jax
import jax.numpy as jnp
from jax import lax
from jax.experimental import pallas as pl
from jax.experimental.pallas import tpu as pltpu
from jax.sharding import PartitionSpec as P

HEAD_DIM = 128
MIB = 1024 * 1024
ROW_SHARES = (4, 4, 4, 4)
OWN_GROUPS = 2
EARLY_GROUPS = 3
CHAIN_PARTS = 2
CORE_PIECES = 4
DEPTH = 2
TILE = 1024
STREAM_MIB = 32
KERNEL_MIB = 32
SHORT = pl.CostEstimate(flops=1, bytes_accessed=1, transcendentals=0)
F32 = jnp.float32
BF16 = jnp.bfloat16


def head_columns(head):
    return slice(head * HEAD_DIM, (head + 1) * HEAD_DIM)


def split_pair(value):
    high = value.astype(BF16)
    low = (value - high.astype(F32)).astype(BF16)
    return jnp.concatenate([high, low], axis=1)


def split_rows(value):
    high = value.astype(BF16)
    low = (value - high.astype(F32)).astype(BF16)
    return jnp.concatenate([high, low], axis=0)


def fold_pair(value):
    return value[:, :HEAD_DIM] + value[:, HEAD_DIM:]


def lower_triangle(size):
    rows = lax.broadcasted_iota(jnp.int32, (size, size), 0)
    columns = lax.broadcasted_iota(jnp.int32, (size, size), 1)
    return rows >= columns


def split_three(value):
    high = value.astype(BF16).astype(F32)
    rest = value - high
    middle = rest.astype(BF16).astype(F32)
    return jnp.concatenate([high, middle, rest - middle], axis=0).astype(BF16)


def running_sum(rates):
    ones = lower_triangle(rates.shape[1]).astype(F32).astype(BF16)
    count = rates.shape[0]
    value = lax.dot_general(
        split_three(rates), ones, (((1,), (1,)), ((), ())), preferred_element_type=F32
    )
    return value[:count] + value[count:2 * count] + value[2 * count:]


def in_hbm(*arrays):
    return [pltpu.with_memory_space_constraint(array, pltpu.HBM) for array in arrays]


def params(mib=KERNEL_MIB):
    return pltpu.CompilerParams(vmem_limit_bytes=mib * MIB)


def states_kernel(half_done, side_ref, rate_hbm, key_hbm, value_hbm, *refs):
    if half_done:
        other, *refs = refs
    message_refs, refs = refs[:CHAIN_PARTS], refs[CHAIN_PARTS:]
    if half_done:
        start_hbm, other_hbm, rate_ref, keys, values, rate_sem, key_sem, value_sem, starts, start_sem = refs
        stores = [pltpu.make_async_copy(starts, start_hbm, start_sem.at[0]),
                  pltpu.make_async_copy(other, other_hbm, start_sem.at[1])]
    else:
        starts, rate_ref, keys, values, rate_sem, key_sem, value_sem = refs
    blocks, half = starts.shape[:2]
    width = keys.shape[1]
    size = keys.shape[0] // blocks
    per_part = half // CHAIN_PARTS
    columns = pl.ds(pl.multiple_of(side_ref[0] * width, width), width)
    rows = [slice(block * size, (block + 1) * size) for block in range(blocks)]
    loads = [
        (pltpu.make_async_copy(key_hbm.at[at, columns], keys.at[at], key_sem.at[block]),
         pltpu.make_async_copy(value_hbm.at[at, columns], values.at[at], value_sem.at[block]))
        for block, at in enumerate(rows)
    ]
    rate_load = pltpu.make_async_copy(rate_hbm, rate_ref, rate_sem)
    rate_load.start()
    for load in [load for pair in loads[:2] for load in pair]:
        load.start()
    starts[0] = jnp.zeros_like(starts[0])
    rate_load.wait()
    rates = jnp.where(side_ref[0] == 1, rate_ref[half:, :], rate_ref[:half, :])
    lead = jnp.zeros((half, 1), F32)
    for block, at in enumerate(rows):
        running = running_sum(rates[:, at])
        total = running[:, -1:]
        fade = jnp.exp(total - running)
        block_decay = jnp.exp(total)
        lead = lead + total
        for load in loads[block]:
            load.wait()
        for load in loads[block + 2] if block + 2 < blocks else ():
            load.start()
        if half_done and block == 0:
            stores[1].start()
        for head in range(half):
            of_head = head_columns(head)
            scaled = keys[at, of_head].T.astype(F32) * fade[head:head + 1]
            gained = jnp.dot(split_rows(scaled), values[at, of_head], preferred_element_type=F32)
            gained = gained[:HEAD_DIM] + gained[HEAD_DIM:]
            state = block_decay[head:head + 1] * starts[block, head] + gained
            if block + 1 < blocks:
                starts[block + 1, head] = state
            else:
                message_refs[head // per_part][head % per_part, :HEAD_DIM] = state
    if half_done:
        stores[0].start()
    through = jnp.exp(lead)
    for head in range(half):
        message_refs[head // per_part][head % per_part, HEAD_DIM:] = jnp.broadcast_to(
            through[head:head + 1], (8, HEAD_DIM))
    if half_done:
        for store in stores:
            store.wait()


def local_states(side, rates, key_vectors, value_vectors, block_len, other=None):
    tokens, features = key_vectors.shape
    half = features // HEAD_DIM // 2
    blocks = tokens // block_len
    message = jax.ShapeDtypeStruct((half // CHAIN_PARTS, HEAD_DIM + 8, HEAD_DIM), F32)
    starts = ((blocks, half, HEAD_DIM, HEAD_DIM), F32)
    vmem, far = pl.BlockSpec(memory_space=pltpu.VMEM), pl.BlockSpec(memory_space=pl.ANY)
    dma = pltpu.SemaphoreType.DMA
    rows = pltpu.VMEM((tokens, features // 2), BF16)
    scratch = [pltpu.VMEM(rates.shape, F32), rows, rows, dma, dma((blocks,)), dma((blocks,))]
    if other is None:
        others, start_specs, start_shapes = [], [vmem], [jax.ShapeDtypeStruct(*starts)]
    else:
        others, start_specs, start_shapes = [other], [far] * 2, [pltpu.HBM(*starts)] * 2
        scratch += [pltpu.VMEM(*starts), dma((2,))]
    outs = pl.pallas_call(
        functools.partial(states_kernel, other is not None),
        in_specs=[pl.BlockSpec(memory_space=pltpu.SMEM), far, far, far] + [far] * len(others),
        out_specs=[vmem] * CHAIN_PARTS + start_specs,
        out_shape=[message] * CHAIN_PARTS + start_shapes,
        scratch_shapes=scratch,
        compiler_params=params(STREAM_MIB),
        cost_estimate=SHORT,
    )(side, *in_hbm(rates, key_vectors, value_vectors), *others)
    return outs[:CHAIN_PARTS], outs[CHAIN_PARTS:]


def inside_kernel(begin, end, place_ref, rate_hbm, query_hbm, key_hbm, value_hbm, keep_hbm, send_hbm,
                  after_ref, *refs):
    del after_ref
    rate_ref, queries, keys, values, keeps, sends, parts, rate_sem, load_sem, store_sem = refs[-10:]
    outs = refs[:-10]
    heads, tokens = rate_ref.shape
    count, half = keeps.shape[:2]
    size = tokens // keep_hbm.shape[0]
    is_odd = place_ref[count] == 1
    loads = []
    for block in range(count):
        place = place_ref[block]
        far = pl.ds(pl.multiple_of(place * size + begin, 16), end - begin)
        until = pl.ds(pl.multiple_of(place * size, size), end)
        pairs = [(query_hbm.at[far], queries), (key_hbm.at[until], keys), (value_hbm.at[until], values),
                 (keep_hbm.at[place], keeps), (send_hbm.at[place], sends)]
        loads.append([pltpu.make_async_copy(source, target.at[block], load_sem.at[block, i])
                      for i, (source, target) in enumerate(pairs)])
    rate_load = pltpu.make_async_copy(rate_hbm, rate_ref, rate_sem)
    for load in [rate_load] + loads[0]:
        load.start()
    rate_load.wait()
    stores = [
        pltpu.make_async_copy(parts.at[block], outs[2 * block], store_sem.at[block])
        for block in range(count)
    ]
    causal = lower_triangle(size)[begin:end, :end]
    for block in range(count):
        first = place_ref[block] * size
        rates = rate_ref[:, pl.ds(pl.multiple_of(first, size), size)]
        ahead = lax.broadcasted_iota(jnp.int32, (heads, tokens), 1) < first
        lead = jnp.sum(jnp.where(ahead, rate_ref[...], 0.0), axis=1, keepdims=True)
        running_rows = running_sum(rates)
        running = running_rows.T[begin:end]
        fade = jnp.exp(running)
        outs[2 * block + 1][...] = jnp.exp(running_rows + lead).T[begin:end]
        running_rows = running_rows[:, :end]
        for load in loads[block]:
            load.wait()
        for load in loads[block + 1] if block + 1 < count else ():
            load.start()
        for head in range(heads):
            of_head = head_columns(head)
            side, slot = head // half, head % half
            kept, sent = keeps[block, slot], sends[block, slot]
            start = jnp.where(is_odd, kept, sent) if side else jnp.where(is_odd, sent, kept)
            query = queries[block, :, of_head]
            scores = lax.dot_general(
                query, keys[block, :, of_head], (((1,), (1,)), ((), ())), preferred_element_type=F32
            )
            spread = running[:, head:head + 1] - running_rows[head:head + 1, :]
            decay = jnp.exp(jnp.where(causal, spread, -1e30))
            weights = (scores * decay).astype(BF16)
            inside = jnp.dot(weights, values[block, :, of_head], preferred_element_type=F32)
            carried = fold_pair(jnp.dot(query, split_pair(start), preferred_element_type=F32))
            parts[block, :, of_head] = inside + carried * fade[:, head:head + 1]
        stores[block].start()
    for store in stores:
        store.wait()


def inside_part(place, begin, end, rates, queries, key_vectors, value_vectors, starts, block_len, after):
    count = place.shape[0] - 1
    features = queries.shape[1]
    heads = features // HEAD_DIM
    rows = end - begin
    vmem, far = pl.BlockSpec(memory_space=pltpu.VMEM), pl.BlockSpec(memory_space=pl.ANY)
    keys = pltpu.VMEM((count, end, features), BF16)
    state = pltpu.VMEM((count, heads // 2, HEAD_DIM, HEAD_DIM), F32)
    return pl.pallas_call(
        functools.partial(inside_kernel, begin, end),
        in_specs=[pl.BlockSpec(memory_space=pltpu.SMEM)] + [far] * 7,
        out_specs=[far, vmem] * count,
        out_shape=[pltpu.HBM((rows, features), F32), pltpu.HBM((rows, heads), F32)] * count,
        scratch_shapes=[pltpu.VMEM(rates.shape, F32), pltpu.VMEM((count, rows, features), BF16), keys, keys,
                        state, state, pltpu.VMEM((count, rows, features), F32),
                        pltpu.SemaphoreType.DMA, pltpu.SemaphoreType.DMA((count, 5)),
                        pltpu.SemaphoreType.DMA((count,))],
        compiler_params=params(STREAM_MIB),
        cost_estimate=SHORT,
    )(place, *in_hbm(rates, queries, key_vectors, value_vectors, *starts), after)


def row_loads(first_row, part_row, block_len, place_ref, query_hbm, gate_hbm, parts_hbm, queries, gates, parts,
              leads, sem):
    rows = queries.shape[0] // 2
    loads = []
    for which, (part_hbm, lead_hbm) in enumerate(parts_hbm):
        whole = pl.ds(pl.multiple_of(place_ref[which] * block_len + first_row, rows), rows)
        group = slice(part_row, part_row + rows)
        at = slice(which * rows, (which + 1) * rows)
        pairs = [(query_hbm.at[whole], queries.at[at]), (part_hbm.at[group], parts.at[at]),
                 (gate_hbm.at[whole], gates.at[at]), (lead_hbm.at[group], leads.at[at])]
        loads += [pltpu.make_async_copy(source, target, sem.at[which, i])
                  for i, (source, target) in enumerate(pairs)]
    return loads


def bring_kernel(first_row, part_row, block_len, place_ref, query_hbm, gate_hbm, weight_hbm, part_0, lead_0,
                 part_1, lead_1, after_ref, queries, gates, parts, leads, weight, row_sem, weight_sem):
    del after_ref
    loads = row_loads(first_row, part_row, block_len, place_ref, query_hbm, gate_hbm,
                      ((part_0, lead_0), (part_1, lead_1)), queries, gates, parts, leads, row_sem)
    loads.append(pltpu.make_async_copy(weight_hbm.at[:, :weight.shape[1]], weight, weight_sem))
    for load in loads:
        load.start()
    for load in loads:
        load.wait()


def row_shapes(rows, features):
    return [((2 * rows, features), BF16), ((2 * rows, features), BF16), ((2 * rows, features), F32),
            ((2 * rows, features // HEAD_DIM), F32)]


def bring_rows(place, rows, first_row, part_row, block_len, queries, parts, gate_input, out_weight, after):
    features, width = out_weight.shape
    shapes = row_shapes(rows, features) + [((features, width), BF16)]
    return pl.pallas_call(
        functools.partial(bring_kernel, first_row, part_row, block_len),
        in_specs=[pl.BlockSpec(memory_space=pltpu.SMEM)] + [pl.BlockSpec(memory_space=pl.ANY)] * 8,
        out_specs=[pl.BlockSpec(memory_space=pltpu.VMEM)] * len(shapes),
        out_shape=[pltpu.VMEM(*shape) for shape in shapes],
        scratch_shapes=[pltpu.SemaphoreType.DMA((2, 4)), pltpu.SemaphoreType.DMA],
        compiler_params=params(),
        cost_estimate=SHORT,
    )(place, *in_hbm(queries, gate_input, out_weight, *parts[0], *parts[1]), after)


def project_kernel(first_row, part_row, block_len, pieces, brought, place_ref, *refs):
    states, refs = refs[:2 * CHAIN_PARTS], refs[2 * CHAIN_PARTS:]
    if brought:
        queries, gates, parts, leads, early, weight_hbm, after_ref, *refs = refs
    else:
        query_hbm, gate_hbm, weight_hbm, part_0, lead_0, part_1, lead_1, after_ref, *refs = refs
    del after_ref
    outs, refs = refs[:pieces + 1], refs[pieces + 1:]
    incoming, hidden, result, weight, state_sem, out_sem, weight_sem, *refs = refs
    rows, width = outs[-1].shape
    tiles = weight_sem.shape[0]
    tile = width // tiles
    is_odd = place_ref[2] == 1
    columns = [slice(at, at + tile) for at in range(0, width, tile)]
    loads = [pltpu.make_async_copy(ref, incoming.at[i], state_sem.at[i])
             for i, ref in enumerate(states)]
    skipped = early.shape[1] if brought else 0
    weights = [
        pltpu.make_async_copy(
            weight_hbm.at[:, at], weight.at[:, at.start - skipped:at.stop - skipped], weight_sem.at[i])
        for i, at in enumerate(columns) if at.start >= skipped
    ]
    if not brought:
        queries, gates, parts, leads, row_sem = refs
        loads += row_loads(first_row, part_row, block_len, place_ref, query_hbm, gate_hbm,
                           ((part_0, lead_0), (part_1, lead_1)), queries, gates, parts, leads, row_sem)
    heads = queries.shape[1] // HEAD_DIM
    half = heads // 2
    per_part = half // CHAIN_PARTS
    for load in loads + weights[:1]:
        load.start()
    for load in loads:
        load.wait()
    for load in weights[1:]:
        load.start()
    for head in range(heads):
        at = head_columns(head)
        side, place = head // half, head % half
        part, slot = place // per_part, place % per_part
        kept, got = incoming[part, slot], incoming[CHAIN_PARTS + part, slot]
        state = jnp.where(is_odd, kept, got) if side else jnp.where(is_odd, got, kept)
        carried = fold_pair(jnp.dot(queries[:, at], split_pair(state), preferred_element_type=F32))
        attended = parts[:, at] + carried * leads[:, head:head + 1]
        mean = jnp.mean(attended * attended, axis=1, keepdims=True)
        gate = gates[:, at].astype(F32)
        normed = attended * lax.rsqrt(mean + 1e-6)
        hidden[:, at] = (normed * (gate / (1.0 + jnp.exp(-gate)))).astype(BF16)
    stores = []
    for i, at in enumerate(columns):
        if at.start < skipped:
            tile_weight = early[:, at]
        else:
            weights[i - skipped // tile].wait()
            tile_weight = weight[:, at.start - skipped:at.stop - skipped]
        result[:, at] = jnp.dot(hidden[...], tile_weight, preferred_element_type=F32)
    begin = 0
    for j, out in enumerate(outs):
        size = out.shape[0]
        store = pltpu.make_async_copy(result.at[begin:begin + size], out, out_sem.at[j])
        store.start()
        stores.append(store)
        begin += size
    for store in stores:
        store.wait()


def project_rows(place, rows, first_row, part_row, block_len, queries, parts, gate_input, kept, got,
                 out_weight, after, pieces, brought=None):
    features = queries.shape[1]
    width = out_weight.shape[1]
    tiles = max(1, width // TILE)
    sizes = [rows // pieces] * pieces + [rows]
    far, vmem = pl.BlockSpec(memory_space=pl.ANY), pl.BlockSpec(memory_space=pltpu.VMEM)
    dma = pltpu.SemaphoreType.DMA
    scratch = [
        pltpu.VMEM((2 * CHAIN_PARTS, *kept[0].shape), F32),
        pltpu.VMEM((2 * rows, features), BF16),
        pltpu.VMEM((2 * rows, width), F32),
        pltpu.VMEM((features, width if brought is None else width - brought[-1].shape[1]), BF16),
        dma((2 * CHAIN_PARTS,)), dma((len(sizes),)), dma((tiles,)),
    ]
    if brought is not None:
        operands = [pltpu.with_memory_space_constraint(value, pltpu.VMEM) for value in brought]
        specs = [vmem] * len(operands) + [far]
        operands += in_hbm(out_weight)
    else:
        operands = in_hbm(queries, gate_input, out_weight, *parts[0], *parts[1])
        specs = [far] * len(operands)
        scratch += [pltpu.VMEM(*shape) for shape in row_shapes(rows, features)]
        scratch += [dma((2, 4))]
    return pl.pallas_call(
        functools.partial(project_kernel, first_row, part_row, block_len, pieces, brought is not None),
        in_specs=[pl.BlockSpec(memory_space=pltpu.SMEM)] + [far] * 2 * CHAIN_PARTS + specs + [far],
        out_specs=[far] * len(sizes),
        out_shape=[jax.ShapeDtypeStruct((size, width), F32) for size in sizes],
        scratch_shapes=scratch,
        compiler_params=params(),
        cost_estimate=SHORT,
    )(place, *kept, *got, *operands, after)


def add_kernel(own_ref, *refs):
    pieces, out_ref = refs[:-2], refs[-1]
    at = 0
    for ref in pieces:
        size = ref.shape[0]
        out_ref[at:at + size] = own_ref[at:at + size] + ref[...]
        at += size


def add_pieces(own, pieces, after):
    whole = pl.BlockSpec(own.shape, lambda: (0, 0))
    return pl.pallas_call(
        add_kernel,
        in_specs=[whole] + [pl.BlockSpec(piece.shape, lambda: (0, 0)) for piece in pieces]
        + [pl.BlockSpec(memory_space=pl.ANY)],
        out_specs=whole,
        out_shape=jax.ShapeDtypeStruct(own.shape, F32),
        compiler_params=params(),
        cost_estimate=SHORT,
    )(own, *pieces, after)


def finish_kernel(arrivals, own_ref, *refs):
    out_ref = refs[-1]
    arrived, pieces = refs[:arrivals], refs[arrivals:-2]
    at = 0
    for ref in pieces:
        size = ref.shape[0]
        total = own_ref[at:at + size] + ref[...]
        for other in arrived:
            total = total + other[at:at + size]
        out_ref[at:at + size] = total.astype(out_ref.dtype)
        at += size


def finish_rows(group, arrived, own, own_group, pieces, result, block_len):
    rows, width = arrived[0].shape
    whole = pl.BlockSpec((rows, width), lambda i: (0, 0))
    alias = {}
    if result is None:
        result = own
    else:
        alias = {1 + len(arrived) + len(pieces): 0}
    return pl.pallas_call(
        functools.partial(finish_kernel, len(arrived)),
        grid=(1,),
        in_specs=[pl.BlockSpec((rows, width), lambda i: (own_group, 0))] + [whole] * len(arrived)
        + [pl.BlockSpec(piece.shape, lambda i: (0, 0)) for piece in pieces]
        + [pl.BlockSpec(memory_space=pl.ANY)],
        out_specs=pl.BlockSpec((rows, width), lambda i: (group, 0)),
        out_shape=jax.ShapeDtypeStruct((block_len, width), BF16),
        input_output_aliases=alias,
        compiler_params=params(),
        cost_estimate=SHORT,
    )(own, *arrived, *pieces, result)


def hop_kernel(hops, odd_ref, *refs):
    landed, (kept_ref, got_ref, after_ref, value_ref) = refs[:hops], refs[hops:]
    del after_ref
    is_odd = odd_ref[0] == 1
    for slot in range(value_ref.shape[0]):
        kept, got = kept_ref[slot], got_ref[slot]
        early, late = jnp.where(is_odd, got, kept), jnp.where(is_odd, kept, got)
        late_decay = late[HEAD_DIM:HEAD_DIM + 1]
        value = early[:HEAD_DIM]
        if landed:
            before = landed[0][slot]
            for ref in landed[1:]:
                before = before + ref[slot]
            value = early[HEAD_DIM:HEAD_DIM + 1] * before + value
        value_ref[slot] = late_decay * value + late[:HEAD_DIM]


def hop_states(odd, landed, kept, got, after):
    vmem = pl.BlockSpec(memory_space=pltpu.VMEM)
    return pl.pallas_call(
        functools.partial(hop_kernel, len(landed)),
        in_specs=[pl.BlockSpec(memory_space=pltpu.SMEM)] + [vmem] * (len(landed) + 2)
        + [pl.BlockSpec(memory_space=pl.ANY)],
        out_specs=vmem,
        out_shape=jax.ShapeDtypeStruct((kept.shape[0], HEAD_DIM, HEAD_DIM), F32),
        compiler_params=params(),
        cost_estimate=SHORT,
    )(odd, *landed, kept, got, *in_hbm(after))


def entering_kernel(hops, odd_ref, *refs):
    landed, (kept_ref, got_ref, after_ref, keep_ref, back_ref) = refs[:hops], refs[hops:]
    del after_ref
    is_odd = odd_ref[0] == 1
    for slot in range(keep_ref.shape[0]):
        before = landed[0][slot]
        for ref in landed[1:]:
            before = before + ref[slot]
        first = jnp.where(is_odd, got_ref[slot], kept_ref[slot])
        after = first[HEAD_DIM:HEAD_DIM + 1] * before + first[:HEAD_DIM]
        keep_ref[slot] = jnp.where(is_odd, after, before)
        back_ref[slot] = jnp.where(is_odd, before, after)


def entering_states(odd, landed, kept, got, after):
    shape = jax.ShapeDtypeStruct(landed[0].shape, F32)
    vmem = pl.BlockSpec(memory_space=pltpu.VMEM)
    return pl.pallas_call(
        functools.partial(entering_kernel, len(landed)),
        in_specs=[pl.BlockSpec(memory_space=pltpu.SMEM)] + [vmem] * (len(landed) + 2)
        + [pl.BlockSpec(memory_space=pl.ANY)],
        out_specs=[vmem, vmem],
        out_shape=[shape, shape],
        compiler_params=params(),
        cost_estimate=SHORT,
    )(odd, *landed, kept, got, *in_hbm(after))


def incoming_states(odd, kept, got, after, meanwhile):
    count = lax.axis_size("seq")
    swap = [(i, i ^ 1) for i in range(count)]
    parts = range(CHAIN_PARTS)
    landed = [[] for _ in parts]
    for hop in range(count // 2 - 1):
        along = [(2 * hop, 2 * hop + 2), (2 * hop + 1, 2 * hop + 3)]
        for i in parts:
            value = hop_states(odd, landed[i], kept[i], got[i], after)
            landed[i].append(lax.ppermute(value, "seq", along))
        if hop == count // 2 - 3:
            for work in meanwhile:
                after = work(value)
    keep, back = [], []
    for i in parts:
        mine, other = entering_states(odd, landed[i], kept[i], got[i], after)
        keep.append(mine)
        back.append(lax.ppermute(other, "seq", swap))
    return keep, back


def per_device(queries, key_vectors, value_vectors, gate_input, log_decay, out_weight):
    tokens = queries.shape[0]
    count = lax.axis_size("head")
    chips = count // 2
    block_len = tokens // count
    sizes = [block_len // share for share in ROW_SHARES]
    firsts = [sum(sizes[:i]) for i in range(len(sizes))]
    index = lax.axis_index("head")
    chip, core = index // 2, index % 2
    place_in_seq = lax.axis_index("seq")
    odd = (place_in_seq % 2).reshape(1).astype(jnp.int32)
    rates = log_decay.T
    swap = [(i, i ^ 1) for i in range(lax.axis_size("seq"))]

    sent, (sent_starts,) = local_states(1 - odd, rates, key_vectors, value_vectors, block_len)
    met = [lax.ppermute(piece, "seq", swap) for piece in sent]
    kept, starts = local_states(odd, rates, key_vectors, value_vectors, block_len, sent_starts)

    def place_of(target):
        return jnp.stack([2 * target + 1 - core, 2 * target + core, odd[0]]).astype(jnp.int32)

    def parts_of(target, begin, end, after):
        outs = inside_part(place_of(target), begin, end, rates, queries, key_vectors, value_vectors,
                           starts, block_len, after)
        return outs[:2], outs[2:]

    def project(target, parts, part_begin, group, after, pieces, brought=None):
        first = firsts[group]
        *theirs, mine = project_rows(
            place_of(target), sizes[group], first, first - part_begin, block_len, queries, parts, gate_input, keep,
            got, out_weight, after, pieces, brought)
        return mine, [lax.ppermute(piece, "head", cores) for piece in theirs]

    cores = [(i, i ^ 1) for i in range(count)]
    targets = [(chip + step) % chips for step in range(1, chips)]
    parts = []

    def inside_of(target, after):
        parts.append(parts_of(target, 0, firsts[EARLY_GROUPS], after))
        return parts[-1][1][1]

    keep, got = incoming_states(
        odd, kept, met, starts[0], [functools.partial(inside_of, target) for target in targets])
    last = keep[-1]
    brought = bring_rows(place_of(targets[0]), sizes[0], 0, 0, block_len, queries, parts[0],
                         gate_input, out_weight, last)
    landed, own, result = [last, last], [], None
    arrived = [[] for _ in sizes]
    for group in range(len(sizes)):
        for step, target in enumerate(targets):
            across = [(i, ((i // 2 + step + 1) % chips) * 2 + i % 2) for i in range(count)]
            mine, pieces = project(
                target, parts[step], firsts[EARLY_GROUPS] if group >= EARLY_GROUPS else 0, group, last, CORE_PIECES, brought)
            brought = None
            last = add_pieces(mine, pieces, landed[-DEPTH])
            landed.append(lax.ppermute(last, "head", across))
            arrived[group].append(landed[-1])
        if group == EARLY_GROUPS - 1:
            parts = [parts_of(target, firsts[EARLY_GROUPS], block_len, last) for target in targets]
    own_parts = parts_of(chip, 0, block_len, last)
    groups = list(zip(firsts, sizes))
    own_rows, piece = block_len // OWN_GROUPS, block_len // 8
    sizes = [own_rows] * OWN_GROUPS
    firsts = [own_rows * i for i in range(OWN_GROUPS)]
    for group in range(len(sizes)):
        if group == len(sizes) - 1:
            last = landed[-2]
        own.append(project(chip, own_parts, 0, group, last, own_rows // piece))
        last = own[-1][0]
    for group, (first, size) in enumerate(groups):
        mine, pieces = own[first // own_rows]
        at = first % own_rows
        result = finish_rows(first // size, arrived[group], mine, at // size,
                             pieces[at // piece:(at + size) // piece], result, block_len)
    return result


def solution(mesh):
    placed = (
        P("seq", "head"),
        P("seq", "head"),
        P("seq", "head"),
        P("seq", "head"),
        P("seq", "head"),
        P("head", None),
    )
    return jax.shard_map(
        per_device, mesh=mesh, in_specs=placed, out_specs=P(("seq", "head"), None), check_vma=False
    )
```

```python
import functools

import jax
import jax.numpy as jnp
from jax import lax
from jax.experimental import pallas as pl
from jax.experimental.pallas import tpu as pltpu
from jax.sharding import PartitionSpec as P

HEAD_DIM = 128
MIB = 1024 * 1024
ROW_SHARES = (4, 4, 4, 4)
OWN_GROUPS = 2
EARLY_GROUPS = 3
CHAIN_PARTS = 2
CORE_PIECES = 4
DEPTH = 2
TILE = 1024
STREAM_MIB = 32
KERNEL_MIB = 32
SHORT = pl.CostEstimate(flops=1, bytes_accessed=1, transcendentals=0)
F32 = jnp.float32
BF16 = jnp.bfloat16


def head_columns(head):
    return slice(head * HEAD_DIM, (head + 1) * HEAD_DIM)


def split_pair(value):
    high = value.astype(BF16)
    low = (value - high.astype(F32)).astype(BF16)
    return jnp.concatenate([high, low], axis=1)


def split_rows(value):
    high = value.astype(BF16)
    low = (value - high.astype(F32)).astype(BF16)
    return jnp.concatenate([high, low], axis=0)


def fold_pair(value):
    return value[:, :HEAD_DIM] + value[:, HEAD_DIM:]


def lower_triangle(size):
    rows = lax.broadcasted_iota(jnp.int32, (size, size), 0)
    columns = lax.broadcasted_iota(jnp.int32, (size, size), 1)
    return rows >= columns


def split_three(value):
    high = value.astype(BF16).astype(F32)
    rest = value - high
    middle = rest.astype(BF16).astype(F32)
    return jnp.concatenate([high, middle, rest - middle], axis=0).astype(BF16)


def running_sum(rates):
    ones = lower_triangle(rates.shape[1]).astype(F32).astype(BF16)
    count = rates.shape[0]
    value = lax.dot_general(
        split_three(rates), ones, (((1,), (1,)), ((), ())), preferred_element_type=F32
    )
    return value[:count] + value[count:2 * count] + value[2 * count:]


def in_hbm(*arrays):
    return [pltpu.with_memory_space_constraint(array, pltpu.HBM) for array in arrays]


def params(mib=KERNEL_MIB):
    return pltpu.CompilerParams(vmem_limit_bytes=mib * MIB)


def states_kernel(half_done, side_ref, rate_hbm, key_hbm, value_hbm, *refs):
    if half_done:
        other, *refs = refs
    message_refs, refs = refs[:CHAIN_PARTS], refs[CHAIN_PARTS:]
    if half_done:
        start_hbm, other_hbm, rate_ref, keys, values, rate_sem, key_sem, value_sem, starts, start_sem = refs
        stores = [pltpu.make_async_copy(starts, start_hbm, start_sem.at[0]),
                  pltpu.make_async_copy(other, other_hbm, start_sem.at[1])]
    else:
        starts, rate_ref, keys, values, rate_sem, key_sem, value_sem = refs
    blocks, half = starts.shape[:2]
    width = keys.shape[1]
    size = keys.shape[0] // blocks
    per_part = half // CHAIN_PARTS
    columns = pl.ds(pl.multiple_of(side_ref[0] * width, width), width)
    rows = [slice(block * size, (block + 1) * size) for block in range(blocks)]
    loads = [
        (pltpu.make_async_copy(key_hbm.at[at, columns], keys.at[at], key_sem.at[block]),
         pltpu.make_async_copy(value_hbm.at[at, columns], values.at[at], value_sem.at[block]))
        for block, at in enumerate(rows)
    ]
    rate_load = pltpu.make_async_copy(rate_hbm, rate_ref, rate_sem)
    rate_load.start()
    for load in [load for pair in loads[:2] for load in pair]:
        load.start()
    starts[0] = jnp.zeros_like(starts[0])
    rate_load.wait()
    rates = jnp.where(side_ref[0] == 1, rate_ref[half:, :], rate_ref[:half, :])
    lead = jnp.zeros((half, 1), F32)
    for block, at in enumerate(rows):
        running = running_sum(rates[:, at])
        total = running[:, -1:]
        fade = jnp.exp(total - running)
        block_decay = jnp.exp(total)
        lead = lead + total
        for load in loads[block]:
            load.wait()
        for load in loads[block + 2] if block + 2 < blocks else ():
            load.start()
        if half_done and block == 0:
            stores[1].start()
        for head in range(half):
            of_head = head_columns(head)
            scaled = keys[at, of_head].T.astype(F32) * fade[head:head + 1]
            gained = jnp.dot(split_rows(scaled), values[at, of_head], preferred_element_type=F32)
            gained = gained[:HEAD_DIM] + gained[HEAD_DIM:]
            state = block_decay[head:head + 1] * starts[block, head] + gained
            if block + 1 < blocks:
                starts[block + 1, head] = state
            else:
                message_refs[head // per_part][head % per_part, :HEAD_DIM] = state
    if half_done:
        stores[0].start()
    through = jnp.exp(lead)
    for head in range(half):
        message_refs[head // per_part][head % per_part, HEAD_DIM:] = jnp.broadcast_to(
            through[head:head + 1], (8, HEAD_DIM))
    if half_done:
        for store in stores:
            store.wait()


def local_states(side, rates, key_vectors, value_vectors, block_len, other=None):
    tokens, features = key_vectors.shape
    half = features // HEAD_DIM // 2
    blocks = tokens // block_len
    message = jax.ShapeDtypeStruct((half // CHAIN_PARTS, HEAD_DIM + 8, HEAD_DIM), F32)
    starts = ((blocks, half, HEAD_DIM, HEAD_DIM), F32)
    vmem, far = pl.BlockSpec(memory_space=pltpu.VMEM), pl.BlockSpec(memory_space=pl.ANY)
    dma = pltpu.SemaphoreType.DMA
    rows = pltpu.VMEM((tokens, features // 2), BF16)
    scratch = [pltpu.VMEM(rates.shape, F32), rows, rows, dma, dma((blocks,)), dma((blocks,))]
    if other is None:
        others, start_specs, start_shapes = [], [vmem], [jax.ShapeDtypeStruct(*starts)]
    else:
        others, start_specs, start_shapes = [other], [far] * 2, [pltpu.HBM(*starts)] * 2
        scratch += [pltpu.VMEM(*starts), dma((2,))]
    outs = pl.pallas_call(
        functools.partial(states_kernel, other is not None),
        in_specs=[pl.BlockSpec(memory_space=pltpu.SMEM), far, far, far] + [far] * len(others),
        out_specs=[vmem] * CHAIN_PARTS + start_specs,
        out_shape=[message] * CHAIN_PARTS + start_shapes,
        scratch_shapes=scratch,
        compiler_params=params(STREAM_MIB),
        cost_estimate=SHORT,
    )(side, *in_hbm(rates, key_vectors, value_vectors), *others)
    return outs[:CHAIN_PARTS], outs[CHAIN_PARTS:]


def inside_kernel(begin, end, place_ref, rate_hbm, query_hbm, key_hbm, value_hbm, keep_hbm, send_hbm,
                  after_ref, *refs):
    del after_ref
    rate_ref, queries, keys, values, keeps, sends, parts, rate_sem, load_sem, store_sem = refs[-10:]
    outs = refs[:-10]
    heads, tokens = rate_ref.shape
    count, half = keeps.shape[:2]
    size = tokens // keep_hbm.shape[0]
    is_odd = place_ref[count] == 1
    loads = []
    for block in range(count):
        place = place_ref[block]
        far = pl.ds(pl.multiple_of(place * size + begin, 16), end - begin)
        until = pl.ds(pl.multiple_of(place * size, size), end)
        pairs = [(query_hbm.at[far], queries), (key_hbm.at[until], keys), (value_hbm.at[until], values),
                 (keep_hbm.at[place], keeps), (send_hbm.at[place], sends)]
        loads.append([pltpu.make_async_copy(source, target.at[block], load_sem.at[block, i])
                      for i, (source, target) in enumerate(pairs)])
    rate_load = pltpu.make_async_copy(rate_hbm, rate_ref, rate_sem)
    for load in [rate_load] + loads[0]:
        load.start()
    rate_load.wait()
    stores = [
        pltpu.make_async_copy(parts.at[block], outs[2 * block], store_sem.at[block])
        for block in range(count)
    ]
    causal = lower_triangle(size)[begin:end, :end]
    for block in range(count):
        first = place_ref[block] * size
        rates = rate_ref[:, pl.ds(pl.multiple_of(first, size), size)]
        ahead = lax.broadcasted_iota(jnp.int32, (heads, tokens), 1) < first
        lead = jnp.sum(jnp.where(ahead, rate_ref[...], 0.0), axis=1, keepdims=True)
        running_rows = running_sum(rates)
        running = running_rows.T[begin:end]
        fade = jnp.exp(running)
        outs[2 * block + 1][...] = jnp.exp(running_rows + lead).T[begin:end]
        running_rows = running_rows[:, :end]
        for load in loads[block]:
            load.wait()
        for load in loads[block + 1] if block + 1 < count else ():
            load.start()
        for head in range(heads):
            of_head = head_columns(head)
            side, slot = head // half, head % half
            kept, sent = keeps[block, slot], sends[block, slot]
            start = jnp.where(is_odd, kept, sent) if side else jnp.where(is_odd, sent, kept)
            query = queries[block, :, of_head]
            scores = lax.dot_general(
                query, keys[block, :, of_head], (((1,), (1,)), ((), ())), preferred_element_type=F32
            )
            spread = running[:, head:head + 1] - running_rows[head:head + 1, :]
            decay = jnp.exp(jnp.where(causal, spread, -1e30))
            weights = (scores * decay).astype(BF16)
            inside = jnp.dot(weights, values[block, :, of_head], preferred_element_type=F32)
            carried = fold_pair(jnp.dot(query, split_pair(start), preferred_element_type=F32))
            parts[block, :, of_head] = inside + carried * fade[:, head:head + 1]
        stores[block].start()
    for store in stores:
        store.wait()


def inside_part(place, begin, end, rates, queries, key_vectors, value_vectors, starts, block_len, after):
    count = place.shape[0] - 1
    features = queries.shape[1]
    heads = features // HEAD_DIM
    rows = end - begin
    vmem, far = pl.BlockSpec(memory_space=pltpu.VMEM), pl.BlockSpec(memory_space=pl.ANY)
    keys = pltpu.VMEM((count, end, features), BF16)
    state = pltpu.VMEM((count, heads // 2, HEAD_DIM, HEAD_DIM), F32)
    return pl.pallas_call(
        functools.partial(inside_kernel, begin, end),
        in_specs=[pl.BlockSpec(memory_space=pltpu.SMEM)] + [far] * 7,
        out_specs=[far, vmem] * count,
        out_shape=[pltpu.HBM((rows, features), F32), pltpu.HBM((rows, heads), F32)] * count,
        scratch_shapes=[pltpu.VMEM(rates.shape, F32), pltpu.VMEM((count, rows, features), BF16), keys, keys,
                        state, state, pltpu.VMEM((count, rows, features), F32),
                        pltpu.SemaphoreType.DMA, pltpu.SemaphoreType.DMA((count, 5)),
                        pltpu.SemaphoreType.DMA((count,))],
        compiler_params=params(STREAM_MIB),
        cost_estimate=SHORT,
    )(place, *in_hbm(rates, queries, key_vectors, value_vectors, *starts), after)


def row_loads(first_row, part_row, block_len, place_ref, query_hbm, gate_hbm, parts_hbm, queries, gates, parts,
              leads, sem):
    rows = queries.shape[0] // 2
    loads = []
    for which, (part_hbm, lead_hbm) in enumerate(parts_hbm):
        whole = pl.ds(pl.multiple_of(place_ref[which] * block_len + first_row, rows), rows)
        group = slice(part_row, part_row + rows)
        at = slice(which * rows, (which + 1) * rows)
        pairs = [(query_hbm.at[whole], queries.at[at]), (part_hbm.at[group], parts.at[at]),
                 (gate_hbm.at[whole], gates.at[at]), (lead_hbm.at[group], leads.at[at])]
        loads += [pltpu.make_async_copy(source, target, sem.at[which, i])
                  for i, (source, target) in enumerate(pairs)]
    return loads


def bring_kernel(first_row, part_row, block_len, place_ref, query_hbm, gate_hbm, weight_hbm, part_0, lead_0,
                 part_1, lead_1, after_ref, queries, gates, parts, leads, weight, row_sem, weight_sem):
    del after_ref
    loads = row_loads(first_row, part_row, block_len, place_ref, query_hbm, gate_hbm,
                      ((part_0, lead_0), (part_1, lead_1)), queries, gates, parts, leads, row_sem)
    loads.append(pltpu.make_async_copy(weight_hbm.at[:, :weight.shape[1]], weight, weight_sem))
    for load in loads:
        load.start()
    for load in loads:
        load.wait()


def row_shapes(rows, features):
    return [((2 * rows, features), BF16), ((2 * rows, features), BF16), ((2 * rows, features), F32),
            ((2 * rows, features // HEAD_DIM), F32)]


def bring_rows(place, rows, first_row, part_row, block_len, queries, parts, gate_input, out_weight, after):
    features, width = out_weight.shape
    shapes = row_shapes(rows, features) + [((features, width), BF16)]
    return pl.pallas_call(
        functools.partial(bring_kernel, first_row, part_row, block_len),
        in_specs=[pl.BlockSpec(memory_space=pltpu.SMEM)] + [pl.BlockSpec(memory_space=pl.ANY)] * 8,
        out_specs=[pl.BlockSpec(memory_space=pltpu.VMEM)] * len(shapes),
        out_shape=[pltpu.VMEM(*shape) for shape in shapes],
        scratch_shapes=[pltpu.SemaphoreType.DMA((2, 4)), pltpu.SemaphoreType.DMA],
        compiler_params=params(),
        cost_estimate=SHORT,
    )(place, *in_hbm(queries, gate_input, out_weight, *parts[0], *parts[1]), after)


def project_kernel(first_row, part_row, block_len, pieces, brought, place_ref, *refs):
    states, refs = refs[:2 * CHAIN_PARTS], refs[2 * CHAIN_PARTS:]
    if brought:
        queries, gates, parts, leads, early, after_ref, *refs = refs
    else:
        query_hbm, gate_hbm, weight_hbm, part_0, lead_0, part_1, lead_1, after_ref, *refs = refs
    del after_ref
    outs, refs = refs[:pieces + 1], refs[pieces + 1:]
    incoming, hidden, result, weight, state_sem, out_sem, weight_sem, *refs = refs
    rows, width = outs[-1].shape
    tiles = weight_sem.shape[0]
    tile = width // tiles
    is_odd = place_ref[2] == 1
    columns = [slice(at, at + tile) for at in range(0, width, tile)]
    loads = [pltpu.make_async_copy(ref, incoming.at[i], state_sem.at[i])
             for i, ref in enumerate(states)]
    weights = [] if brought else [
        pltpu.make_async_copy(weight_hbm.at[:, at], weight.at[:, at], weight_sem.at[i])
        for i, at in enumerate(columns)
    ]
    weight = early if brought else weight
    if not brought:
        queries, gates, parts, leads, row_sem = refs
        loads += row_loads(first_row, part_row, block_len, place_ref, query_hbm, gate_hbm,
                           ((part_0, lead_0), (part_1, lead_1)), queries, gates, parts, leads, row_sem)
    heads = queries.shape[1] // HEAD_DIM
    half = heads // 2
    per_part = half // CHAIN_PARTS
    for load in loads + weights[:1]:
        load.start()
    for load in loads:
        load.wait()
    for load in weights[1:]:
        load.start()
    for head in range(heads):
        at = head_columns(head)
        side, place = head // half, head % half
        part, slot = place // per_part, place % per_part
        kept, got = incoming[part, slot], incoming[CHAIN_PARTS + part, slot]
        state = jnp.where(is_odd, kept, got) if side else jnp.where(is_odd, got, kept)
        carried = fold_pair(jnp.dot(queries[:, at], split_pair(state), preferred_element_type=F32))
        attended = parts[:, at] + carried * leads[:, head:head + 1]
        mean = jnp.mean(attended * attended, axis=1, keepdims=True)
        gate = gates[:, at].astype(F32)
        normed = attended * lax.rsqrt(mean + 1e-6)
        hidden[:, at] = (normed * (gate / (1.0 + jnp.exp(-gate)))).astype(BF16)
    stores = []
    for i, at in enumerate(columns):
        for load in weights[i:i + 1]:
            load.wait()
        result[:, at] = jnp.dot(hidden[...], weight[:, at], preferred_element_type=F32)
    begin = 0
    for j, out in enumerate(outs):
        size = out.shape[0]
        store = pltpu.make_async_copy(result.at[begin:begin + size], out, out_sem.at[j])
        store.start()
        stores.append(store)
        begin += size
    for store in stores:
        store.wait()


def project_rows(place, rows, first_row, part_row, block_len, queries, parts, gate_input, kept, got,
                 out_weight, after, pieces, brought=None):
    features = queries.shape[1]
    width = out_weight.shape[1]
    tiles = max(1, width // TILE)
    sizes = [rows // pieces] * pieces + [rows]
    far, vmem = pl.BlockSpec(memory_space=pl.ANY), pl.BlockSpec(memory_space=pltpu.VMEM)
    dma = pltpu.SemaphoreType.DMA
    scratch = [
        pltpu.VMEM((2 * CHAIN_PARTS, *kept[0].shape), F32),
        pltpu.VMEM((2 * rows, features), BF16),
        pltpu.VMEM((2 * rows, width), F32),
        pltpu.VMEM((features, HEAD_DIM if brought is not None else width), BF16),
        dma((2 * CHAIN_PARTS,)), dma((len(sizes),)), dma((tiles,)),
    ]
    if brought is not None:
        operands = [pltpu.with_memory_space_constraint(value, pltpu.VMEM) for value in brought]
        specs = [vmem] * len(operands)
    else:
        operands = in_hbm(queries, gate_input, out_weight, *parts[0], *parts[1])
        specs = [far] * len(operands)
        scratch += [pltpu.VMEM(*shape) for shape in row_shapes(rows, features)]
        scratch += [dma((2, 4))]
    return pl.pallas_call(
        functools.partial(project_kernel, first_row, part_row, block_len, pieces, brought is not None),
        in_specs=[pl.BlockSpec(memory_space=pltpu.SMEM)] + [far] * 2 * CHAIN_PARTS + specs + [far],
        out_specs=[far] * len(sizes),
        out_shape=[jax.ShapeDtypeStruct((size, width), F32) for size in sizes],
        scratch_shapes=scratch,
        compiler_params=params(),
        cost_estimate=SHORT,
    )(place, *kept, *got, *operands, after)


def add_kernel(own_ref, *refs):
    pieces, out_ref = refs[:-2], refs[-1]
    at = 0
    for ref in pieces:
        size = ref.shape[0]
        out_ref[at:at + size] = own_ref[at:at + size] + ref[...]
        at += size


def add_pieces(own, pieces, after):
    whole = pl.BlockSpec(own.shape, lambda: (0, 0))
    return pl.pallas_call(
        add_kernel,
        in_specs=[whole] + [pl.BlockSpec(piece.shape, lambda: (0, 0)) for piece in pieces]
        + [pl.BlockSpec(memory_space=pl.ANY)],
        out_specs=whole,
        out_shape=jax.ShapeDtypeStruct(own.shape, F32),
        compiler_params=params(),
        cost_estimate=SHORT,
    )(own, *pieces, after)


def finish_kernel(arrivals, own_ref, *refs):
    out_ref = refs[-1]
    arrived, pieces = refs[:arrivals], refs[arrivals:-2]
    at = 0
    for ref in pieces:
        size = ref.shape[0]
        total = own_ref[at:at + size] + ref[...]
        for other in arrived:
            total = total + other[at:at + size]
        out_ref[at:at + size] = total.astype(out_ref.dtype)
        at += size


def finish_rows(group, arrived, own, own_group, pieces, result, block_len):
    rows, width = arrived[0].shape
    whole = pl.BlockSpec((rows, width), lambda i: (0, 0))
    alias = {}
    if result is None:
        result = own
    else:
        alias = {1 + len(arrived) + len(pieces): 0}
    return pl.pallas_call(
        functools.partial(finish_kernel, len(arrived)),
        grid=(1,),
        in_specs=[pl.BlockSpec((rows, width), lambda i: (own_group, 0))] + [whole] * len(arrived)
        + [pl.BlockSpec(piece.shape, lambda i: (0, 0)) for piece in pieces]
        + [pl.BlockSpec(memory_space=pl.ANY)],
        out_specs=pl.BlockSpec((rows, width), lambda i: (group, 0)),
        out_shape=jax.ShapeDtypeStruct((block_len, width), BF16),
        input_output_aliases=alias,
        compiler_params=params(),
        cost_estimate=SHORT,
    )(own, *arrived, *pieces, result)


def hop_kernel(hops, odd_ref, *refs):
    landed, (kept_ref, got_ref, after_ref, value_ref) = refs[:hops], refs[hops:]
    del after_ref
    is_odd = odd_ref[0] == 1
    for slot in range(value_ref.shape[0]):
        kept, got = kept_ref[slot], got_ref[slot]
        early, late = jnp.where(is_odd, got, kept), jnp.where(is_odd, kept, got)
        late_decay = late[HEAD_DIM:HEAD_DIM + 1]
        value = early[:HEAD_DIM]
        if landed:
            before = landed[0][slot]
            for ref in landed[1:]:
                before = before + ref[slot]
            value = early[HEAD_DIM:HEAD_DIM + 1] * before + value
        value_ref[slot] = late_decay * value + late[:HEAD_DIM]


def hop_states(odd, landed, kept, got, after):
    vmem = pl.BlockSpec(memory_space=pltpu.VMEM)
    return pl.pallas_call(
        functools.partial(hop_kernel, len(landed)),
        in_specs=[pl.BlockSpec(memory_space=pltpu.SMEM)] + [vmem] * (len(landed) + 2)
        + [pl.BlockSpec(memory_space=pl.ANY)],
        out_specs=vmem,
        out_shape=jax.ShapeDtypeStruct((kept.shape[0], HEAD_DIM, HEAD_DIM), F32),
        compiler_params=params(),
        cost_estimate=SHORT,
    )(odd, *landed, kept, got, *in_hbm(after))


def entering_kernel(hops, odd_ref, *refs):
    landed, (kept_ref, got_ref, after_ref, keep_ref, back_ref) = refs[:hops], refs[hops:]
    del after_ref
    is_odd = odd_ref[0] == 1
    for slot in range(keep_ref.shape[0]):
        before = landed[0][slot]
        for ref in landed[1:]:
            before = before + ref[slot]
        first = jnp.where(is_odd, got_ref[slot], kept_ref[slot])
        after = first[HEAD_DIM:HEAD_DIM + 1] * before + first[:HEAD_DIM]
        keep_ref[slot] = jnp.where(is_odd, after, before)
        back_ref[slot] = jnp.where(is_odd, before, after)


def entering_states(odd, landed, kept, got, after):
    shape = jax.ShapeDtypeStruct(landed[0].shape, F32)
    vmem = pl.BlockSpec(memory_space=pltpu.VMEM)
    return pl.pallas_call(
        functools.partial(entering_kernel, len(landed)),
        in_specs=[pl.BlockSpec(memory_space=pltpu.SMEM)] + [vmem] * (len(landed) + 2)
        + [pl.BlockSpec(memory_space=pl.ANY)],
        out_specs=[vmem, vmem],
        out_shape=[shape, shape],
        compiler_params=params(),
        cost_estimate=SHORT,
    )(odd, *landed, kept, got, *in_hbm(after))


def incoming_states(odd, kept, got, after, meanwhile):
    count = lax.axis_size("seq")
    swap = [(i, i ^ 1) for i in range(count)]
    parts = range(CHAIN_PARTS)
    landed = [[] for _ in parts]
    for hop in range(count // 2 - 1):
        along = [(2 * hop, 2 * hop + 2), (2 * hop + 1, 2 * hop + 3)]
        for i in parts:
            value = hop_states(odd, landed[i], kept[i], got[i], after)
            landed[i].append(lax.ppermute(value, "seq", along))
        if hop == max(count // 2 - 3, 0):
            for work in meanwhile:
                after = work(value)
    keep, back = [], []
    for i in parts:
        mine, other = entering_states(odd, landed[i], kept[i], got[i], after)
        keep.append(mine)
        back.append(lax.ppermute(other, "seq", swap))
    return keep, back


def per_device(queries, key_vectors, value_vectors, gate_input, log_decay, out_weight):
    tokens = queries.shape[0]
    count = lax.axis_size("head")
    chips = count // 2
    block_len = tokens // count
    sizes = [block_len // share for share in ROW_SHARES]
    firsts = [sum(sizes[:i]) for i in range(len(sizes))]
    index = lax.axis_index("head")
    chip, core = index // 2, index % 2
    place_in_seq = lax.axis_index("seq")
    odd = (place_in_seq % 2).reshape(1).astype(jnp.int32)
    rates = log_decay.T
    swap = [(i, i ^ 1) for i in range(lax.axis_size("seq"))]

    sent, (sent_starts,) = local_states(1 - odd, rates, key_vectors, value_vectors, block_len)
    met = [lax.ppermute(piece, "seq", swap) for piece in sent]
    kept, starts = local_states(odd, rates, key_vectors, value_vectors, block_len, sent_starts)

    def place_of(target):
        return jnp.stack([2 * target + 1 - core, 2 * target + core, odd[0]]).astype(jnp.int32)

    def parts_of(target, begin, end, after):
        outs = inside_part(place_of(target), begin, end, rates, queries, key_vectors, value_vectors,
                           starts, block_len, after)
        return outs[:2], outs[2:]

    def project(target, parts, part_begin, group, after, pieces, brought=None):
        first = firsts[group]
        *theirs, mine = project_rows(
            place_of(target), sizes[group], first, first - part_begin, block_len, queries, parts, gate_input, keep,
            got, out_weight, after, pieces, brought)
        return mine, [lax.ppermute(piece, "head", cores) for piece in theirs]

    cores = [(i, i ^ 1) for i in range(count)]
    targets = [(chip + step) % chips for step in range(1, chips)]
    parts = []

    def inside_of(target, after):
        parts.append(parts_of(target, 0, firsts[EARLY_GROUPS], after))
        return parts[-1][1][1]

    keep, got = incoming_states(
        odd, kept, met, starts[0], [functools.partial(inside_of, target) for target in targets])
    last = keep[-1]
    brought = bring_rows(place_of(targets[0]), sizes[0], 0, 0, block_len, queries, parts[0],
                         gate_input, out_weight, last)
    landed, own, result = [last, last], [], None
    arrived = [[] for _ in sizes]
    for group in range(len(sizes)):
        for step, target in enumerate(targets):
            across = [(i, ((i // 2 + step + 1) % chips) * 2 + i % 2) for i in range(count)]
            mine, pieces = project(
                target, parts[step], firsts[EARLY_GROUPS] if group >= EARLY_GROUPS else 0, group, last, CORE_PIECES, brought)
            brought = None
            last = add_pieces(mine, pieces, landed[-DEPTH])
            landed.append(lax.ppermute(last, "head", across))
            arrived[group].append(landed[-1])
        if group == EARLY_GROUPS - 1:
            parts = [parts_of(target, firsts[EARLY_GROUPS], block_len, last) for target in targets]
    own_parts = parts_of(chip, 0, block_len, last)
    groups = list(zip(firsts, sizes))
    own_rows, piece = block_len // OWN_GROUPS, block_len // 8
    sizes = [own_rows] * OWN_GROUPS
    firsts = [own_rows * i for i in range(OWN_GROUPS)]
    for group in range(len(sizes)):
        if group == len(sizes) - 1:
            last = landed[-2]
        own.append(project(chip, own_parts, 0, group, last, own_rows // piece))
        last = own[-1][0]
    for group, (first, size) in enumerate(groups):
        mine, pieces = own[first // own_rows]
        at = first % own_rows
        result = finish_rows(first // size, arrived[group], mine, at // size,
                             pieces[at // piece:(at + size) // piece], result, block_len)
    return result


def solution(mesh):
    placed = (
        P("seq", "head"),
        P("seq", "head"),
        P("seq", "head"),
        P("seq", "head"),
        P("seq", "head"),
        P("head", None),
    )
    return jax.shard_map(
        per_device, mesh=mesh, in_specs=placed, out_specs=P(("seq", "head"), None), check_vma=False
    )
```

```python
import functools

import jax
import jax.numpy as jnp
from jax import lax
from jax.experimental import pallas as pl
from jax.experimental.pallas import tpu as pltpu
from jax.sharding import PartitionSpec as P

HEAD_DIM = 128
MIB = 1024 * 1024
ROW_SHARES = (4, 4, 4, 4)
OWN_GROUPS = 2
EARLY_GROUPS = 3
CHAIN_PARTS = 2
CORE_PIECES = 4
DEPTH = 2
TILE = 1024
STREAM_MIB = 32
KERNEL_MIB = 32
SHORT = pl.CostEstimate(flops=1, bytes_accessed=1, transcendentals=0)
F32 = jnp.float32
BF16 = jnp.bfloat16


def head_columns(head):
    return slice(head * HEAD_DIM, (head + 1) * HEAD_DIM)


def split_pair(value):
    high = value.astype(BF16)
    low = (value - high.astype(F32)).astype(BF16)
    return jnp.concatenate([high, low], axis=1)


def split_rows(value):
    high = value.astype(BF16)
    low = (value - high.astype(F32)).astype(BF16)
    return jnp.concatenate([high, low], axis=0)


def fold_pair(value):
    return value[:, :HEAD_DIM] + value[:, HEAD_DIM:]


def lower_triangle(size):
    rows = lax.broadcasted_iota(jnp.int32, (size, size), 0)
    columns = lax.broadcasted_iota(jnp.int32, (size, size), 1)
    return rows >= columns


def split_three(value):
    high = value.astype(BF16).astype(F32)
    rest = value - high
    middle = rest.astype(BF16).astype(F32)
    return jnp.concatenate([high, middle, rest - middle], axis=0).astype(BF16)


def running_sum(rates):
    ones = lower_triangle(rates.shape[1]).astype(F32).astype(BF16)
    count = rates.shape[0]
    value = lax.dot_general(
        split_three(rates), ones, (((1,), (1,)), ((), ())), preferred_element_type=F32
    )
    return value[:count] + value[count:2 * count] + value[2 * count:]


def in_hbm(*arrays):
    return [pltpu.with_memory_space_constraint(array, pltpu.HBM) for array in arrays]


def params(mib=KERNEL_MIB):
    return pltpu.CompilerParams(vmem_limit_bytes=mib * MIB)


def states_kernel(half_done, side_ref, rate_hbm, key_hbm, value_hbm, *refs):
    if half_done:
        other, *refs = refs
    message_refs, refs = refs[:CHAIN_PARTS], refs[CHAIN_PARTS:]
    if half_done:
        start_hbm, other_hbm, rate_ref, keys, values, rate_sem, key_sem, value_sem, starts, start_sem = refs
        stores = [pltpu.make_async_copy(starts, start_hbm, start_sem.at[0]),
                  pltpu.make_async_copy(other, other_hbm, start_sem.at[1])]
    else:
        starts, rate_ref, keys, values, rate_sem, key_sem, value_sem = refs
    blocks, half = starts.shape[:2]
    width = keys.shape[1]
    size = keys.shape[0] // blocks
    per_part = half // CHAIN_PARTS
    columns = pl.ds(pl.multiple_of(side_ref[0] * width, width), width)
    rows = [slice(block * size, (block + 1) * size) for block in range(blocks)]
    loads = [
        (pltpu.make_async_copy(key_hbm.at[at, columns], keys.at[at], key_sem.at[block]),
         pltpu.make_async_copy(value_hbm.at[at, columns], values.at[at], value_sem.at[block]))
        for block, at in enumerate(rows)
    ]
    rate_load = pltpu.make_async_copy(rate_hbm, rate_ref, rate_sem)
    rate_load.start()
    for load in [load for pair in loads[:2] for load in pair]:
        load.start()
    starts[0] = jnp.zeros_like(starts[0])
    rate_load.wait()
    rates = jnp.where(side_ref[0] == 1, rate_ref[half:, :], rate_ref[:half, :])
    lead = jnp.zeros((half, 1), F32)
    for block, at in enumerate(rows):
        running = running_sum(rates[:, at])
        total = running[:, -1:]
        fade = jnp.exp(total - running)
        block_decay = jnp.exp(total)
        lead = lead + total
        for load in loads[block]:
            load.wait()
        for load in loads[block + 2] if block + 2 < blocks else ():
            load.start()
        if half_done and block == 0:
            stores[1].start()
        for head in range(half):
            of_head = head_columns(head)
            scaled = keys[at, of_head].T.astype(F32) * fade[head:head + 1]
            gained = jnp.dot(split_rows(scaled), values[at, of_head], preferred_element_type=F32)
            gained = gained[:HEAD_DIM] + gained[HEAD_DIM:]
            state = block_decay[head:head + 1] * starts[block, head] + gained
            if block + 1 < blocks:
                starts[block + 1, head] = state
            else:
                message_refs[head // per_part][head % per_part, :HEAD_DIM] = state
    if half_done:
        stores[0].start()
    through = jnp.exp(lead)
    for head in range(half):
        message_refs[head // per_part][head % per_part, HEAD_DIM:] = jnp.broadcast_to(
            through[head:head + 1], (8, HEAD_DIM))
    if half_done:
        for store in stores:
            store.wait()


def local_states(side, rates, key_vectors, value_vectors, block_len, other=None):
    tokens, features = key_vectors.shape
    half = features // HEAD_DIM // 2
    blocks = tokens // block_len
    message = jax.ShapeDtypeStruct((half // CHAIN_PARTS, HEAD_DIM + 8, HEAD_DIM), F32)
    starts = ((blocks, half, HEAD_DIM, HEAD_DIM), F32)
    vmem, far = pl.BlockSpec(memory_space=pltpu.VMEM), pl.BlockSpec(memory_space=pl.ANY)
    dma = pltpu.SemaphoreType.DMA
    rows = pltpu.VMEM((tokens, features // 2), BF16)
    scratch = [pltpu.VMEM(rates.shape, F32), rows, rows, dma, dma((blocks,)), dma((blocks,))]
    if other is None:
        others, start_specs, start_shapes = [], [vmem], [jax.ShapeDtypeStruct(*starts)]
    else:
        others, start_specs, start_shapes = [other], [far] * 2, [pltpu.HBM(*starts)] * 2
        scratch += [pltpu.VMEM(*starts), dma((2,))]
    outs = pl.pallas_call(
        functools.partial(states_kernel, other is not None),
        in_specs=[pl.BlockSpec(memory_space=pltpu.SMEM), far, far, far] + [far] * len(others),
        out_specs=[vmem] * CHAIN_PARTS + start_specs,
        out_shape=[message] * CHAIN_PARTS + start_shapes,
        scratch_shapes=scratch,
        compiler_params=params(STREAM_MIB),
        cost_estimate=SHORT,
    )(side, *in_hbm(rates, key_vectors, value_vectors), *others)
    return outs[:CHAIN_PARTS], outs[CHAIN_PARTS:]


def inside_kernel(begin, end, place_ref, rate_hbm, query_hbm, key_hbm, value_hbm, keep_hbm, send_hbm,
                  after_ref, *refs):
    del after_ref
    rate_ref, queries, keys, values, keeps, sends, parts, rate_sem, load_sem, store_sem = refs[-10:]
    outs = refs[:-10]
    heads, tokens = rate_ref.shape
    count, half = keeps.shape[:2]
    size = tokens // keep_hbm.shape[0]
    is_odd = place_ref[count] == 1
    loads = []
    for block in range(count):
        place = place_ref[block]
        far = pl.ds(pl.multiple_of(place * size + begin, 16), end - begin)
        until = pl.ds(pl.multiple_of(place * size, size), end)
        pairs = [(query_hbm.at[far], queries), (key_hbm.at[until], keys), (value_hbm.at[until], values),
                 (keep_hbm.at[place], keeps), (send_hbm.at[place], sends)]
        loads.append([pltpu.make_async_copy(source, target.at[block], load_sem.at[block, i])
                      for i, (source, target) in enumerate(pairs)])
    rate_load = pltpu.make_async_copy(rate_hbm, rate_ref, rate_sem)
    for load in [rate_load] + loads[0]:
        load.start()
    rate_load.wait()
    stores = [
        pltpu.make_async_copy(parts.at[block], outs[2 * block], store_sem.at[block])
        for block in range(count)
    ]
    causal = lower_triangle(size)[begin:end, :end]
    for block in range(count):
        first = place_ref[block] * size
        rates = rate_ref[:, pl.ds(pl.multiple_of(first, size), size)]
        ahead = lax.broadcasted_iota(jnp.int32, (heads, tokens), 1) < first
        lead = jnp.sum(jnp.where(ahead, rate_ref[...], 0.0), axis=1, keepdims=True)
        running_rows = running_sum(rates)
        running = running_rows.T[begin:end]
        fade = jnp.exp(running)
        outs[2 * block + 1][...] = jnp.exp(running_rows + lead).T[begin:end]
        running_rows = running_rows[:, :end]
        for load in loads[block]:
            load.wait()
        for load in loads[block + 1] if block + 1 < count else ():
            load.start()
        for head in range(heads):
            of_head = head_columns(head)
            side, slot = head // half, head % half
            kept, sent = keeps[block, slot], sends[block, slot]
            start = jnp.where(is_odd, kept, sent) if side else jnp.where(is_odd, sent, kept)
            query = queries[block, :, of_head]
            scores = lax.dot_general(
                query, keys[block, :, of_head], (((1,), (1,)), ((), ())), preferred_element_type=F32
            )
            spread = running[:, head:head + 1] - running_rows[head:head + 1, :]
            decay = jnp.exp(jnp.where(causal, spread, -1e30))
            weights = (scores * decay).astype(BF16)
            inside = jnp.dot(weights, values[block, :, of_head], preferred_element_type=F32)
            carried = fold_pair(jnp.dot(query, split_pair(start), preferred_element_type=F32))
            parts[block, :, of_head] = inside + carried * fade[:, head:head + 1]
        stores[block].start()
    for store in stores:
        store.wait()


def inside_part(place, begin, end, rates, queries, key_vectors, value_vectors, starts, block_len, after):
    count = place.shape[0] - 1
    features = queries.shape[1]
    heads = features // HEAD_DIM
    rows = end - begin
    vmem, far = pl.BlockSpec(memory_space=pltpu.VMEM), pl.BlockSpec(memory_space=pl.ANY)
    keys = pltpu.VMEM((count, end, features), BF16)
    state = pltpu.VMEM((count, heads // 2, HEAD_DIM, HEAD_DIM), F32)
    return pl.pallas_call(
        functools.partial(inside_kernel, begin, end),
        in_specs=[pl.BlockSpec(memory_space=pltpu.SMEM)] + [far] * 7,
        out_specs=[far, vmem] * count,
        out_shape=[pltpu.HBM((rows, features), F32), pltpu.HBM((rows, heads), F32)] * count,
        scratch_shapes=[pltpu.VMEM(rates.shape, F32), pltpu.VMEM((count, rows, features), BF16), keys, keys,
                        state, state, pltpu.VMEM((count, rows, features), F32),
                        pltpu.SemaphoreType.DMA, pltpu.SemaphoreType.DMA((count, 5)),
                        pltpu.SemaphoreType.DMA((count,))],
        compiler_params=params(STREAM_MIB),
        cost_estimate=SHORT,
    )(place, *in_hbm(rates, queries, key_vectors, value_vectors, *starts), after)


def row_loads(first_row, part_row, block_len, place_ref, query_hbm, gate_hbm, parts_hbm, queries, gates, parts,
              leads, sem):
    rows = queries.shape[0] // 2
    loads = []
    for which, (part_hbm, lead_hbm) in enumerate(parts_hbm):
        whole = pl.ds(pl.multiple_of(place_ref[which] * block_len + first_row, rows), rows)
        group = slice(part_row, part_row + rows)
        at = slice(which * rows, (which + 1) * rows)
        pairs = [(query_hbm.at[whole], queries.at[at]), (part_hbm.at[group], parts.at[at]),
                 (gate_hbm.at[whole], gates.at[at]), (lead_hbm.at[group], leads.at[at])]
        loads += [pltpu.make_async_copy(source, target, sem.at[which, i])
                  for i, (source, target) in enumerate(pairs)]
    return loads


def bring_kernel(first_row, part_row, block_len, place_ref, query_hbm, gate_hbm, weight_hbm, part_0, lead_0,
                 part_1, lead_1, after_ref, queries, gates, parts, leads, weight, row_sem, weight_sem):
    del after_ref
    loads = row_loads(first_row, part_row, block_len, place_ref, query_hbm, gate_hbm,
                      ((part_0, lead_0), (part_1, lead_1)), queries, gates, parts, leads, row_sem)
    loads.append(pltpu.make_async_copy(weight_hbm.at[:, :weight.shape[1]], weight, weight_sem))
    for load in loads:
        load.start()
    for load in loads:
        load.wait()


def row_shapes(rows, features):
    return [((2 * rows, features), BF16), ((2 * rows, features), BF16), ((2 * rows, features), F32),
            ((2 * rows, features // HEAD_DIM), F32)]


def bring_rows(place, rows, first_row, part_row, block_len, queries, parts, gate_input, out_weight, after):
    features, width = out_weight.shape
    shapes = row_shapes(rows, features) + [((features, width), BF16)]
    return pl.pallas_call(
        functools.partial(bring_kernel, first_row, part_row, block_len),
        in_specs=[pl.BlockSpec(memory_space=pltpu.SMEM)] + [pl.BlockSpec(memory_space=pl.ANY)] * 8,
        out_specs=[pl.BlockSpec(memory_space=pltpu.VMEM)] * len(shapes),
        out_shape=[pltpu.VMEM(*shape) for shape in shapes],
        scratch_shapes=[pltpu.SemaphoreType.DMA((2, 4)), pltpu.SemaphoreType.DMA],
        compiler_params=params(),
        cost_estimate=SHORT,
    )(place, *in_hbm(queries, gate_input, out_weight, *parts[0], *parts[1]), after)


def project_kernel(first_row, part_row, block_len, pieces, brought, place_ref, *refs):
    states, refs = refs[:2 * CHAIN_PARTS], refs[2 * CHAIN_PARTS:]
    if brought:
        queries, gates, parts, leads, early, after_ref, *refs = refs
    else:
        query_hbm, gate_hbm, weight_hbm, part_0, lead_0, part_1, lead_1, after_ref, *refs = refs
    del after_ref
    outs, refs = refs[:pieces + 1], refs[pieces + 1:]
    incoming, hidden, result, weight, state_sem, out_sem, weight_sem, *refs = refs
    rows, width = outs[-1].shape
    tiles = weight_sem.shape[0]
    tile = width // tiles
    is_odd = place_ref[2] == 1
    columns = [slice(at, at + tile) for at in range(0, width, tile)]
    loads = [pltpu.make_async_copy(ref, incoming.at[i], state_sem.at[i])
             for i, ref in enumerate(states)]
    weights = [] if brought else [
        pltpu.make_async_copy(weight_hbm.at[:, at], weight.at[:, at], weight_sem.at[i])
        for i, at in enumerate(columns)
    ]
    weight = early if brought else weight
    if not brought:
        queries, gates, parts, leads, row_sem = refs
        loads += row_loads(first_row, part_row, block_len, place_ref, query_hbm, gate_hbm,
                           ((part_0, lead_0), (part_1, lead_1)), queries, gates, parts, leads, row_sem)
    heads = queries.shape[1] // HEAD_DIM
    half = heads // 2
    per_part = half // CHAIN_PARTS
    for load in loads + weights[:1]:
        load.start()
    for load in loads:
        load.wait()
    for load in weights[1:]:
        load.start()
    for head in range(heads):
        at = head_columns(head)
        side, place = head // half, head % half
        part, slot = place // per_part, place % per_part
        kept, got = incoming[part, slot], incoming[CHAIN_PARTS + part, slot]
        state = jnp.where(is_odd, kept, got) if side else jnp.where(is_odd, got, kept)
        carried = fold_pair(jnp.dot(queries[:, at], split_pair(state), preferred_element_type=F32))
        attended = parts[:, at] + carried * leads[:, head:head + 1]
        mean = jnp.mean(attended * attended, axis=1, keepdims=True)
        gate = gates[:, at].astype(F32)
        normed = attended * lax.rsqrt(mean + 1e-6)
        hidden[:, at] = (normed * (gate / (1.0 + jnp.exp(-gate)))).astype(BF16)
    stores = []
    for i, at in enumerate(columns):
        for load in weights[i:i + 1]:
            load.wait()
        result[:, at] = jnp.dot(hidden[...], weight[:, at], preferred_element_type=F32)
    begin = 0
    for j, out in enumerate(outs):
        size = out.shape[0]
        store = pltpu.make_async_copy(result.at[begin:begin + size], out, out_sem.at[j])
        store.start()
        stores.append(store)
        begin += size
    for store in stores:
        store.wait()


def project_rows(place, rows, first_row, part_row, block_len, queries, parts, gate_input, kept, got,
                 out_weight, after, pieces, brought=None):
    features = queries.shape[1]
    width = out_weight.shape[1]
    tiles = max(1, width // TILE)
    sizes = [rows // pieces] * pieces + [rows]
    far, vmem = pl.BlockSpec(memory_space=pl.ANY), pl.BlockSpec(memory_space=pltpu.VMEM)
    dma = pltpu.SemaphoreType.DMA
    scratch = [
        pltpu.VMEM((2 * CHAIN_PARTS, *kept[0].shape), F32),
        pltpu.VMEM((2 * rows, features), BF16),
        pltpu.VMEM((2 * rows, width), F32),
        pltpu.VMEM((features, HEAD_DIM if brought is not None else width), BF16),
        dma((2 * CHAIN_PARTS,)), dma((len(sizes),)), dma((tiles,)),
    ]
    if brought is not None:
        operands = [pltpu.with_memory_space_constraint(value, pltpu.VMEM) for value in brought]
        specs = [vmem] * len(operands)
    else:
        operands = in_hbm(queries, gate_input, out_weight, *parts[0], *parts[1])
        specs = [far] * len(operands)
        scratch += [pltpu.VMEM(*shape) for shape in row_shapes(rows, features)]
        scratch += [dma((2, 4))]
    return pl.pallas_call(
        functools.partial(project_kernel, first_row, part_row, block_len, pieces, brought is not None),
        in_specs=[pl.BlockSpec(memory_space=pltpu.SMEM)] + [far] * 2 * CHAIN_PARTS + specs + [far],
        out_specs=[far] * len(sizes),
        out_shape=[jax.ShapeDtypeStruct((size, width), F32) for size in sizes],
        scratch_shapes=scratch,
        compiler_params=params(),
        cost_estimate=SHORT,
    )(place, *kept, *got, *operands, after)


def add_kernel(own_ref, *refs):
    pieces, out_ref = refs[:-2], refs[-1]
    at = 0
    for ref in pieces:
        size = ref.shape[0]
        out_ref[at:at + size] = own_ref[at:at + size] + ref[...]
        at += size


def add_pieces(own, pieces, after):
    whole = pl.BlockSpec(own.shape, lambda: (0, 0))
    return pl.pallas_call(
        add_kernel,
        in_specs=[whole] + [pl.BlockSpec(piece.shape, lambda: (0, 0)) for piece in pieces]
        + [pl.BlockSpec(memory_space=pl.ANY)],
        out_specs=whole,
        out_shape=jax.ShapeDtypeStruct(own.shape, F32),
        compiler_params=params(),
        cost_estimate=SHORT,
    )(own, *pieces, after)


def finish_kernel(arrivals, own_ref, *refs):
    out_ref = refs[-1]
    arrived, pieces = refs[:arrivals], refs[arrivals:-2]
    at = 0
    for ref in pieces:
        size = ref.shape[0]
        total = own_ref[at:at + size] + ref[...]
        for other in arrived:
            total = total + other[at:at + size]
        out_ref[at:at + size] = total.astype(out_ref.dtype)
        at += size


def finish_rows(group, arrived, own, own_group, pieces, result, block_len):
    rows, width = arrived[0].shape
    whole = pl.BlockSpec((rows, width), lambda i: (0, 0))
    alias = {}
    if result is None:
        result = own
    else:
        alias = {1 + len(arrived) + len(pieces): 0}
    return pl.pallas_call(
        functools.partial(finish_kernel, len(arrived)),
        grid=(1,),
        in_specs=[pl.BlockSpec((rows, width), lambda i: (own_group, 0))] + [whole] * len(arrived)
        + [pl.BlockSpec(piece.shape, lambda i: (0, 0)) for piece in pieces]
        + [pl.BlockSpec(memory_space=pl.ANY)],
        out_specs=pl.BlockSpec((rows, width), lambda i: (group, 0)),
        out_shape=jax.ShapeDtypeStruct((block_len, width), BF16),
        input_output_aliases=alias,
        compiler_params=params(),
        cost_estimate=SHORT,
    )(own, *arrived, *pieces, result)


def hop_kernel(hops, odd_ref, *refs):
    landed, (kept_ref, got_ref, after_ref, value_ref) = refs[:hops], refs[hops:]
    del after_ref
    is_odd = odd_ref[0] == 1
    for slot in range(value_ref.shape[0]):
        kept, got = kept_ref[slot], got_ref[slot]
        early, late = jnp.where(is_odd, got, kept), jnp.where(is_odd, kept, got)
        late_decay = late[HEAD_DIM:HEAD_DIM + 1]
        value = early[:HEAD_DIM]
        if landed:
            before = landed[0][slot]
            for ref in landed[1:]:
                before = before + ref[slot]
            value = early[HEAD_DIM:HEAD_DIM + 1] * before + value
        value_ref[slot] = late_decay * value + late[:HEAD_DIM]


def hop_states(odd, landed, kept, got, after):
    vmem = pl.BlockSpec(memory_space=pltpu.VMEM)
    return pl.pallas_call(
        functools.partial(hop_kernel, len(landed)),
        in_specs=[pl.BlockSpec(memory_space=pltpu.SMEM)] + [vmem] * (len(landed) + 2)
        + [pl.BlockSpec(memory_space=pl.ANY)],
        out_specs=vmem,
        out_shape=jax.ShapeDtypeStruct((kept.shape[0], HEAD_DIM, HEAD_DIM), F32),
        compiler_params=params(),
        cost_estimate=SHORT,
    )(odd, *landed, kept, got, *in_hbm(after))


def entering_kernel(hops, odd_ref, *refs):
    landed, (kept_ref, got_ref, after_ref, keep_ref, back_ref) = refs[:hops], refs[hops:]
    del after_ref
    is_odd = odd_ref[0] == 1
    for slot in range(keep_ref.shape[0]):
        before = landed[0][slot]
        for ref in landed[1:]:
            before = before + ref[slot]
        first = jnp.where(is_odd, got_ref[slot], kept_ref[slot])
        after = first[HEAD_DIM:HEAD_DIM + 1] * before + first[:HEAD_DIM]
        keep_ref[slot] = jnp.where(is_odd, after, before)
        back_ref[slot] = jnp.where(is_odd, before, after)


def entering_states(odd, landed, kept, got, after):
    shape = jax.ShapeDtypeStruct(landed[0].shape, F32)
    vmem = pl.BlockSpec(memory_space=pltpu.VMEM)
    return pl.pallas_call(
        functools.partial(entering_kernel, len(landed)),
        in_specs=[pl.BlockSpec(memory_space=pltpu.SMEM)] + [vmem] * (len(landed) + 2)
        + [pl.BlockSpec(memory_space=pl.ANY)],
        out_specs=[vmem, vmem],
        out_shape=[shape, shape],
        compiler_params=params(),
        cost_estimate=SHORT,
    )(odd, *landed, kept, got, *in_hbm(after))


def incoming_states(odd, kept, got, after, meanwhile):
    count = lax.axis_size("seq")
    swap = [(i, i ^ 1) for i in range(count)]
    parts = range(CHAIN_PARTS)
    landed = [[] for _ in parts]
    for hop in range(count // 2 - 1):
        along = [(2 * hop, 2 * hop + 2), (2 * hop + 1, 2 * hop + 3)]
        for i in parts:
            value = hop_states(odd, landed[i], kept[i], got[i], after)
            landed[i].append(lax.ppermute(value, "seq", along))
        if hop == max(count // 2 - 3, 0):
            for work in meanwhile:
                after = work(value)
    keep, back = [], []
    for i in parts:
        mine, other = entering_states(odd, landed[i], kept[i], got[i], after)
        keep.append(mine)
        back.append(lax.ppermute(other, "seq", swap))
    return keep, back


def per_device(queries, key_vectors, value_vectors, gate_input, log_decay, out_weight):
    tokens = queries.shape[0]
    count = lax.axis_size("head")
    chips = count // 2
    block_len = tokens // count
    sizes = [block_len // share for share in ROW_SHARES]
    firsts = [sum(sizes[:i]) for i in range(len(sizes))]
    index = lax.axis_index("head")
    chip, core = index // 2, index % 2
    place_in_seq = lax.axis_index("seq")
    odd = (place_in_seq % 2).reshape(1).astype(jnp.int32)
    rates = log_decay.T
    swap = [(i, i ^ 1) for i in range(lax.axis_size("seq"))]

    sent, (sent_starts,) = local_states(1 - odd, rates, key_vectors, value_vectors, block_len)
    met = [lax.ppermute(piece, "seq", swap) for piece in sent]
    kept, starts = local_states(odd, rates, key_vectors, value_vectors, block_len, sent_starts)

    def place_of(target):
        return jnp.stack([2 * target + 1 - core, 2 * target + core, odd[0]]).astype(jnp.int32)

    def parts_of(target, begin, end, after):
        outs = inside_part(place_of(target), begin, end, rates, queries, key_vectors, value_vectors,
                           starts, block_len, after)
        return outs[:2], outs[2:]

    def project(target, parts, part_begin, group, after, pieces, brought=None):
        first = firsts[group]
        *theirs, mine = project_rows(
            place_of(target), sizes[group], first, first - part_begin, block_len, queries, parts, gate_input, keep,
            got, out_weight, after, pieces, brought)
        return mine, [lax.ppermute(piece, "head", cores) for piece in theirs]

    cores = [(i, i ^ 1) for i in range(count)]
    targets = [(chip + step) % chips for step in range(1, chips)]
    parts = []

    def inside_of(target, after):
        parts.append(parts_of(target, 0, firsts[EARLY_GROUPS], after))
        return parts[-1][1][1]

    keep, got = incoming_states(
        odd, kept, met, starts[0], [functools.partial(inside_of, target) for target in targets])
    last = keep[0]
    brought = bring_rows(place_of(targets[0]), sizes[0], 0, 0, block_len, queries, parts[0],
                         gate_input, out_weight, last)
    landed, own, result = [last, last], [], None
    arrived = [[] for _ in sizes]
    for group in range(len(sizes)):
        for step, target in enumerate(targets):
            across = [(i, ((i // 2 + step + 1) % chips) * 2 + i % 2) for i in range(count)]
            mine, pieces = project(
                target, parts[step], firsts[EARLY_GROUPS] if group >= EARLY_GROUPS else 0, group, last, CORE_PIECES, brought)
            brought = None
            last = add_pieces(mine, pieces, landed[-DEPTH])
            landed.append(lax.ppermute(last, "head", across))
            arrived[group].append(landed[-1])
        if group == EARLY_GROUPS - 1:
            parts = [parts_of(target, firsts[EARLY_GROUPS], block_len, last) for target in targets]
    own_parts = parts_of(chip, 0, block_len, last)
    groups = list(zip(firsts, sizes))
    own_rows, piece = block_len // OWN_GROUPS, block_len // 8
    sizes = [own_rows] * OWN_GROUPS
    firsts = [own_rows * i for i in range(OWN_GROUPS)]
    for group in range(len(sizes)):
        if group == len(sizes) - 1:
            last = landed[-2]
        own.append(project(chip, own_parts, 0, group, last, own_rows // piece))
        last = own[-1][0]
    for group, (first, size) in enumerate(groups):
        mine, pieces = own[first // own_rows]
        at = first % own_rows
        result = finish_rows(first // size, arrived[group], mine, at // size,
                             pieces[at // piece:(at + size) // piece], result, block_len)
    return result


def solution(mesh):
    placed = (
        P("seq", "head"),
        P("seq", "head"),
        P("seq", "head"),
        P("seq", "head"),
        P("seq", "head"),
        P("head", None),
    )
    return jax.shard_map(
        per_device, mesh=mesh, in_specs=placed, out_specs=P(("seq", "head"), None), check_vma=False
    )
```
